128 devices in a mesh: pool: 4 (over y), dev: 32 (over z, x, core).
Axes of the slice: x: 4, y: 4, z: 4, core: 2. Of those that a mesh axis runs over, the one named last changes fastest.
Arguments:
- hidden: bfloat16 [128, 32, 7168], P('dev', 'pool'), may hold values from -17.3 to 17.3
- query_latent_rows: bfloat16 [128, 32, 1536], P('dev', 'pool'), may hold values from -6 to 6
- store: bfloat16 [128, 32, 64, 576], P(('pool', 'dev')), may hold values from -41 to 41
- w_down: bfloat16 [7168, 576], replicated, may hold values from -0.0625 to 0.0625
- kv_gain: bfloat16 [512], replicated, may hold values from 0.5 to 1.5
- query_up_weight: bfloat16 [1536, 12288], P(None, 'pool'), may hold values from -0.15625 to 0.15625
- w_uk: bfloat16 [64, 128, 512], P('pool'), may hold values from -0.5 to 0.5
- w_uv: bfloat16 [64, 512, 128], P('pool'), may hold values from -0.25 to 0.25
- prefix_pages: int32 [128], replicated, may hold values from 2 to 64, as said below
- page_owner: int32 [128, 64], replicated, may hold values from 0 to 127, as said below
- page_slot: int32 [128, 64], replicated, may hold values from 0 to 31
- decode_order: int32 [128], replicated, may hold values from 0 to 127, as said below
Outputs:
- attended: bfloat16 [128, 32, 8192], P('dev', None, 'pool')
- handed: bfloat16 [128, 32, 576], P('dev', 'pool')
The draws below stay inside these ranges and needn't reach their ends.
Inputs may be any that keep to these rules, and one draw needn't show every extreme that they name: `prefix_pages`: every request has at least 2 prefix pages; some request has 64. `page_owner`: counting only used hits (page index below the request's prefix_pages), one owner holds at most 2 pages of the requests of one index of dev, and for every index of dev some owner holds exactly 2. Owners are flat indices pool * 32 + dev. `decode_order`: decode slots of one index of dev take the requests of that index, each once.
All inputs are finite; a program needn't handle non-finite values.
Results may differ from the reference program's by a relative error of at most 0.0095.
The reference program's roundings to bfloat16 on the way (of `new_latent`, `q_nope`, `q_rope`, `q_abs`, `keys`, `weights` and `mixed`) count: a program that leaves them out, or rounds other values in their place, can miss the bound.
Values may be sent and summed in bfloat16 or wider, within the bound.
A program may use at most 192 MiB of HBM per device.

```python
import jax
import jax.numpy as jnp
from jax import lax

D = 7168
LAT = 512
ROTARY_WIDTH = 64
QUERY_LATENT_DIM = 1536
HEAD_COUNT = 64
PLAIN_QUERY_DIM = 128
HV = 128
PAGE = 64
MAX_PAGES = 64
NEW_TOKEN_COUNT = 32
REQ_COL = 4
PAGES_DEV = 32
REQUEST_COUNT = 128
OWNERS = 128
KDIM = 576
CAP = 2


def pages_and_owners(key):
    column_count = REQUEST_COUNT // REQ_COL
    list_len = REQ_COL * MAX_PAGES
    capacity = CAP
    key_pages, key_forced, key_full, key_owner, key_order, key_pick = jax.random.split(key, 6)
    page_counts = jax.random.randint(key_pages, (column_count, REQ_COL), capacity, MAX_PAGES + 1)
    forced_req = jax.random.randint(key_forced, (column_count,), 0, REQ_COL)
    full_column = jax.random.randint(key_full, (), 0, column_count)
    is_forced = jnp.arange(REQ_COL)[None, :] == forced_req[:, None]
    full_mark = jnp.logical_and(is_forced, (jnp.arange(column_count) == full_column)[:, None])
    page_counts = jnp.where(full_mark, MAX_PAGES, page_counts)
    heavy_owner = jax.random.randint(key_owner, (column_count,), 0, OWNERS)
    order_keys = jax.random.split(key_order, column_count)
    pick_keys = jax.random.split(key_pick, column_count)
    forced_pages = jnp.sum(jnp.where(is_forced, page_counts, 0), axis=1)

    def one_column(forced_one, forced_count, owner, order_key, pick_key):
        entry_owner = jnp.arange(list_len, dtype=jnp.int32) // capacity
        rank_keys = jax.random.permutation(order_key, list_len)
        sort_key = rank_keys + list_len * (entry_owner == owner).astype(jnp.int32)
        others = entry_owner[jnp.argsort(sort_key, stable=True)][:list_len - capacity]
        page_rank = jax.random.permutation(pick_key, MAX_PAGES)
        page_key = page_rank + MAX_PAGES * (jnp.arange(MAX_PAGES) >= forced_count).astype(jnp.int32)
        chosen_pages = jnp.argsort(page_key, stable=True)[:capacity]
        marked = jnp.zeros((list_len,), jnp.int32).at[forced_one * MAX_PAGES + chosen_pages].set(1)
        fill_index = jnp.cumsum(1 - marked) - 1
        return jnp.where(marked == 1, owner, others[jnp.clip(fill_index, 0, list_len - capacity - 1)]).astype(jnp.int32)
    owners = jax.vmap(one_column)(forced_req, forced_pages, heavy_owner, order_keys, pick_keys)
    return (page_counts.reshape(REQUEST_COUNT).astype(jnp.int32), owners.reshape(REQUEST_COUNT, MAX_PAGES))


def draw_prefix_pages(key, part):
    page_counts, owners = pages_and_owners(key)
    return page_counts


def draw_page_owner(key, part):
    page_counts, owners = pages_and_owners(key)
    return owners


def draw_decode_order(key, part):
    key = jax.random.fold_in(key, 7)
    column_count = REQUEST_COUNT // REQ_COL
    key_list = jax.random.split(key, column_count)
    inner_perm = jax.vmap(lambda one_key: jax.random.permutation(one_key, REQ_COL))(key_list)
    return (inner_perm + (jnp.arange(column_count) * REQ_COL)[:, None]).reshape(REQUEST_COUNT).astype(jnp.int32)


def draw_store(key, part):
    key = jax.random.fold_in(key, 11)
    key_value = jax.random.fold_in(key, 0)
    array_shape = (OWNERS, PAGES_DEV, PAGE, KDIM)
    sample = jnp.clip(jax.random.normal(key_value, array_shape, jnp.float32), -5.0, 5.0)
    return sample.astype(jnp.bfloat16)


def draw_hidden(key, part):
    key = jax.random.fold_in(key, 13)
    key_value = jax.random.fold_in(key, 0)
    array_shape = (REQUEST_COUNT, NEW_TOKEN_COUNT, D)
    sample = jnp.clip(jax.random.normal(key_value, array_shape, jnp.float32), -5.0, 5.0)
    return sample.astype(jnp.bfloat16)


def place_ends(result, rng, low, largest):
    longest = result.shape.index(max(result.shape))
    spots = []
    for shift in (0, 1):
        where = [jax.random.randint(jax.random.fold_in(rng, axis), (), 0, length) for axis, length in enumerate(result.shape)]
        where[longest] = (where[longest] + shift) % result.shape[longest]
        spots.append(tuple(where))
    return result.at[spots[0]].set(low).at[spots[1]].set(largest)


def shard_levels(key, dims, pieces, least, largest):
    factor_of, own = 1.0, jax.random.fold_in(key, 6)
    for axis_at, parts in pieces:
        heights = jnp.exp(jax.random.uniform(jax.random.fold_in(own, axis_at), (parts,), jnp.float32, least / len(pieces), largest / len(pieces)))
        factor_of = factor_of * jnp.repeat(heights, dims[axis_at] // parts).reshape([-1 if axis == axis_at else 1 for axis in range(len(dims))])
    return factor_of


def noise(key, dims, deviation, bound, shards=(), kind=jnp.bfloat16):
    values = jax.random.normal(key, dims, jnp.float32) * deviation
    if len(shards) > 0:
        values = shard_levels(key, dims, shards, -0.22, 0.18) * values
    return jnp.clip(values, min=-bound, max=bound).astype(kind)


def setup_inputs(seed: int = 0) -> dict:
    keys = jax.random.split(jax.random.key(seed), 13)
    hidden = draw_hidden(jax.random.fold_in(keys[12], 71), 0)
    query_latent_rows = noise(keys[1], (REQUEST_COUNT, NEW_TOKEN_COUNT, QUERY_LATENT_DIM), 1.0, 6.0, ((0, 32), (1, 4)))
    store = draw_store(jax.random.fold_in(keys[12], 71), 0)
    w_down = noise(keys[3], (D, KDIM), D ** -0.5, 0.0625)
    kv_gain = jnp.clip(1.0 + 0.1 * jax.random.normal(keys[4], (LAT,), jnp.float32), 0.5, 1.5).astype(jnp.bfloat16)
    query_up_weight = noise(keys[5], (QUERY_LATENT_DIM, HEAD_COUNT * (PLAIN_QUERY_DIM + ROTARY_WIDTH)), QUERY_LATENT_DIM ** -0.5, 0.15625, ((1, 4),))
    w_uk = noise(keys[6], (HEAD_COUNT, PLAIN_QUERY_DIM, LAT), PLAIN_QUERY_DIM ** -0.5, 0.5, ((0, 4),))
    w_uv = noise(keys[7], (HEAD_COUNT, LAT, HV), LAT ** -0.5, 0.25, ((0, 4),))
    prefix_pages = draw_prefix_pages(jax.random.fold_in(keys[12], 71), 0)
    page_owner = draw_page_owner(jax.random.fold_in(keys[12], 71), 0)
    page_slot = place_ends(jax.random.randint(keys[10], (REQUEST_COUNT, MAX_PAGES), 0, PAGES_DEV), jax.random.fold_in(keys[10], 1), 0, PAGES_DEV - 1).astype(jnp.int32)
    decode_order = draw_decode_order(jax.random.fold_in(keys[12], 71), 0)
    return dict(hidden=hidden, query_latent_rows=query_latent_rows, store=store, w_down=w_down, kv_gain=kv_gain, query_up_weight=query_up_weight, w_uk=w_uk, w_uv=w_uv, prefix_pages=prefix_pages, page_owner=page_owner, page_slot=page_slot, decode_order=decode_order)


def rotate(sample, positions):
    half_dim = sample.shape[-1] // 2
    frequency = jnp.exp(jnp.arange(half_dim, dtype=jnp.float32) * (-2.0 * jnp.log(50000.0) / sample.shape[-1]))
    angles = positions.astype(jnp.float32)[:, None] * frequency[None, :]
    angles = angles.reshape(angles.shape[:1] + (1,) * (sample.ndim - 2) + angles.shape[1:])
    cosine = jnp.cos(angles)
    sine_part = jnp.sin(angles)
    first_half = sample[..., :half_dim]
    second_half = sample[..., half_dim:]
    return jnp.concatenate([first_half * cosine - second_half * sine_part, first_half * sine_part + second_half * cosine], axis=-1)

def reference(hidden, query_latent_rows, store, w_down, kv_gain, query_up_weight, w_uk, w_uv, prefix_pages, page_owner, page_slot, decode_order):
    score_scale = (PLAIN_QUERY_DIM + ROTARY_WIDTH) ** (-0.5)
    prefix_keys = MAX_PAGES * PAGE
    gain = kv_gain.astype(jnp.float32)

    def one_request(item):
        hidden_rows, query_latent, prefix_len, owners, slots = item
        positions = prefix_len * PAGE + jnp.arange(NEW_TOKEN_COUNT, dtype=jnp.int32)
        projected = jnp.dot(hidden_rows, w_down, preferred_element_type=jnp.float32)
        latent = projected[:, :LAT]
        latent = latent * lax.rsqrt(lax.optimization_barrier(jnp.mean(latent * latent, axis=-1, keepdims=True)) + 1e-06) * gain
        new_rows = jnp.concatenate([latent, rotate(projected[:, LAT:], positions)], axis=-1).astype(jnp.bfloat16)
        query_raw = jnp.dot(query_latent, query_up_weight, preferred_element_type=jnp.float32).reshape(NEW_TOKEN_COUNT, HEAD_COUNT, PLAIN_QUERY_DIM + ROTARY_WIDTH)
        q_nope = query_raw[..., :PLAIN_QUERY_DIM].astype(jnp.bfloat16)
        q_rope = rotate(query_raw[..., PLAIN_QUERY_DIM:], positions).astype(jnp.bfloat16)
        q_abs = jnp.einsum('thn,hnl->thl', q_nope.astype(jnp.float32), w_uk.astype(jnp.float32)).astype(jnp.bfloat16)
        query = jnp.concatenate([q_abs, q_rope], axis=-1)
        prefix = store[owners, slots].reshape(prefix_keys, KDIM)
        key_rows = jnp.concatenate([prefix, new_rows], axis=0)
        key_index = jnp.arange(prefix_keys + NEW_TOKEN_COUNT, dtype=jnp.int32)[None, :]
        query_index = jnp.arange(NEW_TOKEN_COUNT, dtype=jnp.int32)[:, None]
        in_range = jnp.where(key_index < prefix_keys, key_index < prefix_len * PAGE, key_index - prefix_keys <= query_index)
        scores = jnp.einsum('thk,sk->ths', query.astype(jnp.float32), key_rows.astype(jnp.float32)) * score_scale
        scores = jnp.where(in_range[:, None, :], scores, -jnp.inf)
        row_max = lax.optimization_barrier(jnp.max(scores, axis=-1, keepdims=True))
        exp_scores = jnp.exp(scores - row_max)
        denominator = lax.optimization_barrier(jnp.sum(exp_scores, axis=-1))
        weights = exp_scores.astype(jnp.bfloat16)
        mixed = jnp.einsum('ths,sl->thl', weights.astype(jnp.float32), key_rows[:, :LAT].astype(jnp.float32)) / denominator[..., None]
        mixed = mixed.astype(jnp.bfloat16)
        attended_rows = jnp.einsum('thl,hlv->thv', mixed.astype(jnp.float32), w_uv.astype(jnp.float32))
        return (attended_rows.reshape(NEW_TOKEN_COUNT, HEAD_COUNT * HV).astype(jnp.bfloat16), new_rows)
    attended, new_latent = lax.map(one_request, (hidden, query_latent_rows, prefix_pages, page_owner, page_slot))
    return (attended, new_latent[decode_order])
```

```python
import functools
import math

import jax
import jax.numpy as jnp
from jax import lax
from jax.experimental import pallas as pl
from jax.experimental.pallas import tpu as pltpu
from jax.sharding import PartitionSpec as P

TILE = 4
LOW = -1e30


def rotate(sample, positions):
    half_dim = sample.shape[-1] // 2
    frequency = jnp.exp(
        jnp.arange(half_dim, dtype=jnp.float32) * (-2.0 * jnp.log(50000.0) / sample.shape[-1])
    )
    angles = positions.astype(jnp.float32)[:, None] * frequency[None, :]
    angles = angles.reshape(angles.shape[:1] + (1,) * (sample.ndim - 2) + angles.shape[1:])
    cosine = jnp.cos(angles)
    sine_part = jnp.sin(angles)
    first_half = sample[..., :half_dim]
    second_half = sample[..., half_dim:]
    return jnp.concatenate(
        [
            first_half * cosine - second_half * sine_part,
            first_half * sine_part + second_half * cosine,
        ],
        axis=-1,
    )


def attention_step(
    order_ref, start_ref, *refs, call, n_blocks, first, last, scale, lat, page, own_rows, new_len
):
    blocks = refs[:n_blocks]
    refs = refs[n_blocks:]
    q_refs, refs = refs[:2], refs[2:]
    if first:
        new_ref, new_pos_ref = refs[:2]
        refs = refs[2:]
    else:
        acc_in, stat_in = refs[:2]
        refs = refs[2:]
    acc_out, stat_out = refs[:2]
    refs = refs[2:]
    pages, sem = refs[:2]
    acc = refs[2] if last else acc_out.at[0]
    request = pl.program_id(0)
    count = blocks[0].shape[0]

    @pl.when(request == 0)
    def _():
        copies = [
            pltpu.make_async_copy(block, pages.at[pl.ds(i * count, count)], sem.at[i])
            for i, block in enumerate(blocks)
        ]
        for copy in copies:
            copy.start()
        for copy in copies:
            copy.wait()

    factor = scale * math.log2(math.e)

    def scores_of(keys, half):
        return jnp.dot(keys, q_refs[half][0], preferred_element_type=jnp.float32) * factor

    def weigh(keys, weights):
        return lax.dot_general(
            keys[:, :lat],
            weights.astype(jnp.bfloat16),
            (((0,), (0,)), ((), ())),
            preferred_element_type=jnp.float32,
        )

    if first:
        new_keys = new_ref[0]
        key_pos = new_pos_ref[...]
        for half in range(2):
            cols = pl.ds(half * own_rows, own_rows)
            score = scores_of(new_keys, half)
            token = lax.broadcasted_iota(jnp.int32, score.shape, 1) % new_len
            live = key_pos[:, :1] <= token
            score = jnp.where(live, score, LOW)
            top = jnp.max(score, axis=0, keepdims=True)
            weights = jnp.where(live, jnp.exp2(score - top), 0.0)
            stat_out[0, 0:1, cols] = top
            stat_out[0, 1:2, cols] = jnp.sum(weights, axis=0, keepdims=True)
            acc[:, cols] = weigh(new_keys, weights)
    else:
        stat_out[...] = stat_in[...]
        acc[...] = acc_in[0]

    begin = start_ref[call * 8 + request]
    end = start_ref[call * 8 + request + 1]
    n_slots = end - begin

    def step(tile, masked):
        at = begin + tile * TILE
        parts = []
        for g in range(TILE):
            spot = jnp.minimum(at + g, end - 1)
            parts.append(pages[order_ref[call * 64 + spot]])
        keys = jnp.concatenate(parts, axis=0)
        for half in range(2):
            cols = pl.ds(half * own_rows, own_rows)
            score = scores_of(keys, half)
            if masked:
                row = lax.broadcasted_iota(jnp.int32, score.shape, 0)
                score = jnp.where(row < (n_slots - tile * TILE) * page, score, LOW)
            old = stat_out[0, 0:1, cols]
            top = jnp.maximum(old, jnp.max(score, axis=0, keepdims=True))
            shrink = jnp.exp2(old - top)
            weights = jnp.exp2(score - top)
            stat_out[0, 0:1, cols] = top
            stat_out[0, 1:2, cols] = stat_out[0, 1:2, cols] * shrink + jnp.sum(
                weights, axis=0, keepdims=True
            )
            acc[:, cols] = acc[:, cols] * shrink + weigh(keys, weights)

    full = n_slots // TILE

    @pl.loop(0, full)
    def _(tile):
        step(tile, False)

    @pl.when(n_slots > full * TILE)
    def _():
        step(full, True)

    if last:
        total = stat_out[0, 1:2, :]
        inverse = jnp.where(total > 0, 1.0 / total, 0.0)
        acc_out[0] = (acc[...] * inverse).astype(jnp.bfloat16)


def attend(call, order, start, blocks, queries, state, new, first, last, scale, lat, new_len):
    req, key_dim, own_rows = queries[0].shape
    page = blocks[0].shape[1]
    rows = 2 * own_rows
    count = blocks[0].shape[0] * len(blocks)
    kernel = functools.partial(
        attention_step,
        call=call,
        n_blocks=len(blocks),
        first=first,
        last=last,
        scale=scale,
        lat=lat,
        page=page,
        own_rows=own_rows,
        new_len=new_len,
    )
    in_specs = [pl.BlockSpec(memory_space=pl.ANY)] * len(blocks)
    in_specs += [pl.BlockSpec((1, key_dim, own_rows), lambda r, *_: (r, 0, 0))] * 2
    operands = list(blocks) + list(queries)
    if first:
        in_specs += [
            pl.BlockSpec((1,) + new[0].shape[1:], lambda r, *_: (r, 0, 0)),
            pl.BlockSpec(new[1].shape, lambda r, *_: (0, 0)),
        ]
        operands += list(new)
    else:
        in_specs += [
            pl.BlockSpec((1, lat, rows), lambda r, *_: (r, 0, 0)),
            pl.BlockSpec((1, 2, rows), lambda r, *_: (r, 0, 0)),
        ]
        operands += list(state)
    scratch = [
        pltpu.VMEM((count, page, key_dim), jnp.bfloat16),
        pltpu.SemaphoreType.DMA((len(blocks),)),
    ]
    if last:
        scratch.append(pltpu.VMEM((lat, rows), jnp.float32))
    return pl.pallas_call(
        kernel,
        grid_spec=pltpu.PrefetchScalarGridSpec(
            num_scalar_prefetch=2,
            grid=(req,),
            in_specs=in_specs,
            out_specs=[
                pl.BlockSpec((1, lat, rows), lambda r, *_: (r, 0, 0)),
                pl.BlockSpec((1, 2, rows), lambda r, *_: (r, 0, 0)),
            ],
            scratch_shapes=scratch,
        ),
        out_shape=[
            jax.ShapeDtypeStruct((req, lat, rows), jnp.bfloat16 if last else jnp.float32),
            jax.ShapeDtypeStruct((req, 2, rows), jnp.float32),
        ],
        compiler_params=pltpu.CompilerParams(
            dimension_semantics=("arbitrary",), vmem_limit_bytes=48 * 2**20
        ),
        cost_estimate=pl.CostEstimate(
            flops=2 * rows * count * page * (key_dim + lat),
            bytes_accessed=4 * req * lat * rows * 2 + count * page * key_dim * 2,
            transcendentals=rows * count * page,
        ),
        name=f"attend_{call}",
    )(order, start, *operands)


def partner_lists(pool_count, dev_count):
    head_pairs, key_pairs = [], []
    for pool in range(pool_count):
        near, far = pool ^ 1, pool_count - 1 - pool
        for dev in range(dev_count):
            head, key = (near, far) if dev % 2 == 0 else (far, near)
            head_pairs.append((pool * dev_count + dev, head * dev_count + dev))
            key_pairs.append((pool * dev_count + dev, key * dev_count + dev))
    return head_pairs, key_pairs


def on_device(
    hidden,
    query_latent_rows,
    store,
    w_down,
    kv_gain,
    query_up_weight,
    w_uk,
    w_uv,
    prefix_pages,
    page_owner,
    page_slot,
    decode_order,
):
    pool_count = lax.axis_size("pool")
    dev_count = lax.axis_size("dev")
    pool_index = lax.axis_index("pool")
    column = lax.axis_index("dev")
    req_col, quarter, model_width = hidden.shape
    new_len = quarter * pool_count
    lat_dim = kv_gain.shape[0]
    key_dim = w_down.shape[1]
    heads_local, nope_dim, _ = w_uk.shape
    head_v = w_uv.shape[2]
    rope_dim = key_dim - lat_dim
    page_len = store.shape[2]
    n_slots = store.shape[1]
    max_pages = page_owner.shape[1]
    list_len = req_col * max_pages
    first_row = column * req_col
    score_scale = (nope_dim + rope_dim) ** (-0.5)
    axes = ("pool", "dev")
    head_pairs, key_pairs = partner_lists(pool_count, dev_count)
    odd = column % 2
    near, far = pool_index ^ 1, pool_count - 1 - pool_index
    key_partner = jnp.where(odd == 0, far, near)

    entry = jnp.arange(list_len, dtype=jnp.int32)
    page_of = jnp.arange(max_pages, dtype=jnp.int32)
    used = page_of[None, :] < prefix_pages[:, None]
    me_flat = pool_index * dev_count + column
    mine = jnp.logical_and(page_owner == me_flat, used).reshape(dev_count, list_len)
    code = entry[None, :] * n_slots + page_slot.reshape(dev_count, list_len)
    low = jnp.min(jnp.where(mine, code, list_len * n_slots), axis=1) % n_slots
    high = jnp.max(jnp.where(mine, code, 0), axis=1) % n_slots
    outgoing = [store[0][low], store[0][high]]
    arrived = [lax.all_to_all(o, "dev", split_axis=0, concat_axis=0, tiled=True) for o in outgoing]
    passed = [lax.ppermute(a, axes, key_pairs) for a in arrived]

    own_lists = lax.dynamic_slice_in_dim(page_owner, first_row, req_col).reshape(list_len)
    prefix_mine = lax.dynamic_slice_in_dim(prefix_pages, first_row, req_col)
    own_used = (page_of[None, :] < prefix_mine[:, None]).reshape(list_len)
    source = jnp.stack([pool_index, key_partner])[:, None] * dev_count + jnp.arange(
        dev_count, dtype=jnp.int32
    )
    hit = jnp.logical_and(own_lists == source[..., None], own_used)
    head_entry = jnp.min(jnp.where(hit, entry, list_len), axis=-1)
    tail_entry = jnp.max(jnp.where(hit, entry, -1), axis=-1)
    req_low = head_entry // max_pages
    req_high = jnp.where(tail_entry > head_entry, tail_entry // max_pages, req_col)
    nobody = jnp.full((dev_count,), req_col, jnp.int32)
    lists = jnp.stack(
        [
            jnp.concatenate([req_low[0], nobody]),
            jnp.concatenate([req_low[1], req_high[0]]),
            jnp.concatenate([req_high[1], nobody]),
        ]
    )
    width = 2 * dev_count
    spot = jnp.arange(width, dtype=jnp.int32)
    rank_key = lists * width + spot
    rank = jnp.sum((rank_key[:, None, :] < rank_key[:, :, None]).astype(jnp.int32), axis=-1)
    order = jnp.sum(
        jnp.where(rank[:, None, :] == spot[None, :, None], spot[None, None, :], 0), axis=-1
    ).reshape(-1)
    start = jnp.sum(
        (lists[:, None, :] < jnp.arange(8, dtype=jnp.int32)[None, :, None]).astype(jnp.int32),
        axis=-1,
    ).reshape(-1)

    local_pos = (
        prefix_mine[:, None] * page_len
        + pool_index * quarter
        + jnp.arange(quarter, dtype=jnp.int32)[None, :]
    )
    projected = jnp.dot(
        hidden.reshape(req_col * quarter, model_width), w_down, preferred_element_type=jnp.float32
    )
    latent = projected[:, :lat_dim]
    latent = (
        latent
        * lax.rsqrt(jnp.mean(latent * latent, axis=-1, keepdims=True) + 1e-06)
        * kv_gain.astype(jnp.float32)
    )
    new_local = jnp.concatenate(
        [latent, rotate(projected[:, lat_dim:], local_pos.reshape(-1))], axis=-1
    )
    new_local = new_local.astype(jnp.bfloat16).reshape(req_col, quarter, key_dim)
    handed_index = lax.dynamic_slice_in_dim(decode_order, first_row, req_col) - first_row
    handed = new_local[handed_index]
    new_other = lax.ppermute(new_local, axes, key_pairs)
    new_keys = jnp.concatenate([new_local, new_other], axis=1)
    new_pos = jnp.concatenate(
        [
            pool_index * quarter + jnp.arange(quarter, dtype=jnp.int32),
            key_partner * quarter + jnp.arange(quarter, dtype=jnp.int32),
        ]
    )
    new_pos = jnp.broadcast_to(new_pos[:, None], (2 * quarter, 128))

    w_uv_other = lax.ppermute(w_uv, axes, head_pairs)
    q_full = lax.all_gather(query_latent_rows, "pool", axis=1, tiled=True)
    positions = prefix_mine[:, None] * page_len + jnp.arange(new_len, dtype=jnp.int32)[None, :]
    query_raw = jnp.dot(
        q_full.reshape(req_col * new_len, -1), query_up_weight, preferred_element_type=jnp.float32
    )
    query_raw = query_raw.reshape(req_col * new_len, heads_local, nope_dim + rope_dim)
    q_nope = query_raw[..., :nope_dim].astype(jnp.bfloat16)
    q_rope = rotate(query_raw[..., nope_dim:], positions.reshape(-1)).astype(jnp.bfloat16)
    q_abs = jnp.einsum("thn,hnl->lht", q_nope, w_uk, preferred_element_type=jnp.float32).astype(
        jnp.bfloat16
    )
    q_rows = jnp.concatenate([q_abs, q_rope.transpose(2, 1, 0)], axis=0)
    query = (
        q_rows.reshape(key_dim, heads_local, req_col, new_len)
        .transpose(2, 0, 1, 3)
        .reshape(req_col, key_dim, heads_local * new_len)
    )
    query_other = lax.ppermute(query, axes, head_pairs)
    queries = (query, query_other)

    common = dict(scale=score_scale, lat=lat_dim, new_len=new_len)
    state = attend(
        0, order, start, [arrived[0]], queries, None, (new_keys, new_pos), True, False, **common
    )
    state = attend(
        1, order, start, [passed[0], arrived[1]], queries, state, None, False, False, **common
    )
    mixed, stat = attend(2, order, start, [passed[1]], queries, state, None, False, True, **common)

    mixed = mixed.reshape(req_col, lat_dim, 2, heads_local, new_len)
    stat = stat.reshape(req_col, 2, 2, heads_local, new_len)
    part_own = jnp.einsum(
        "rlht,hlv->rthv", mixed[:, :, 0], w_uv, preferred_element_type=jnp.float32
    )
    part_send = jnp.einsum(
        "rlht,hlv->rthv", mixed[:, :, 1], w_uv_other, preferred_element_type=jnp.float32
    )
    part_got = lax.ppermute(part_send, axes, head_pairs)
    stat_got = lax.ppermute(stat[:, :, 1], axes, head_pairs)
    top = jnp.maximum(stat[:, 0, 0], stat_got[:, 0])
    mass_own = stat[:, 1, 0] * jnp.exp2(stat[:, 0, 0] - top)
    mass_got = stat_got[:, 1] * jnp.exp2(stat_got[:, 0] - top)
    share = (mass_own / (mass_own + mass_got)).transpose(0, 2, 1)[..., None]
    attended = part_own * share + part_got * (1.0 - share)
    attended = attended.astype(jnp.bfloat16).reshape(req_col, new_len, heads_local * head_v)
    return (attended, handed)


def solution(mesh):
    in_specs = (
        P("dev", "pool", None),
        P("dev", "pool", None),
        P(("pool", "dev"), None, None, None),
        P(),
        P(),
        P(None, "pool"),
        P("pool", None, None),
        P("pool", None, None),
        P(),
        P(),
        P(),
        P(),
    )
    out_specs = (P("dev", None, "pool"), P("dev", "pool", None))
    return jax.shard_map(
        on_device, mesh=mesh, in_specs=in_specs, out_specs=out_specs, check_vma=False
    )
```

```python
import functools
import math

import jax
import jax.numpy as jnp
from jax import lax
from jax.experimental import pallas as pl
from jax.experimental.pallas import tpu as pltpu
from jax.sharding import PartitionSpec as P

TILE = 4
LOW = -1e30
FORWARDED = 16
MESH = pl.DeviceIdType.MESH
STEPS = [
    (0, 1), (1, 0), (0, 3), (3, 0), (1, 1), (3, 3), (1, 3), (3, 1),
    (0, 2), (2, 0), (1, 2), (2, 1), (3, 2), (2, 3), (2, 2),
]
OFFSETS = [(0, 0, 0), (0, 0, 1)] + [(z, x, c) for z, x in STEPS for c in (0, 1)]


def shifted(dev, offset, sign):
    core, x, z = dev % 2, (dev // 2) % 4, dev // 8
    dz, dx, dc = offset
    return ((z + sign * dz + 4) % 4 * 4 + (x + sign * dx + 4) % 4) * 2 + (core + dc) % 2


def partners(pool, dev):
    near = pool + 1 - 2 * (pool % 2)
    far = 3 - pool
    odd = dev % 2
    return near + odd * (far - near), far + odd * (near - far)


def exchange_kernel(
    ql_ref, hidden_ref, outgoing, wd_ref, qup_ref, wuk_ref, gain_ref, cos_ref, sin_ref, lcos_ref, lsin_ref,
    arr_a, arr_b, pass_a, q_own, q_other, new_own, new_other,
    ql_in, wd_v, qup_v, wuk_v, q_s, new_s, q_full,
    load_sem, ql_send, ql_recv, page_send, page_recv, pass_send, pass_recv, pair_send, pair_recv,
):
    pool, dev = lax.axis_index("pool"), lax.axis_index("dev")
    head_partner, key_partner = partners(pool, dev)
    req, key_dim, own_rows = q_s.shape
    lat = wuk_v.shape[2]
    heads, nope, _ = wuk_v.shape
    rope = key_dim - lat
    half_rope = rope // 2
    quarter = ql_in.shape[1] // req
    new_len = 4 * quarter
    n_send = len(OFFSETS)

    loads = [
        pltpu.make_async_copy(wd_ref, wd_v, load_sem.at[0]),
        pltpu.make_async_copy(qup_ref, qup_v, load_sem.at[1]),
        pltpu.make_async_copy(wuk_ref, wuk_v, load_sem.at[2]),
    ]
    own_pages = pltpu.make_async_copy(outgoing.at[dev], arr_a.at[0], load_sem.at[3])
    for copy in loads + [own_pages]:
        copy.start()

    barrier = pltpu.get_barrier_semaphore()
    for offset in OFFSETS[1:]:
        pl.semaphore_signal(
            barrier, inc=1, device_id=(pool, shifted(dev, offset, 1)), device_id_type=MESH
        )
    for step in range(1, 4):
        pl.semaphore_signal(
            barrier, inc=1, device_id=((pool + step) % 4, dev), device_id_type=MESH
        )
    pl.semaphore_wait(barrier, n_send - 1 + 3)

    def remote(src, dst, send, recv, target):
        return pltpu.make_async_remote_copy(
            src_ref=src, dst_ref=dst, send_sem=send, recv_sem=recv, device_id=target, device_id_type=MESH
        )

    ql_sends = [
        remote(ql_ref, ql_in.at[pool], ql_send.at[s - 1], ql_recv.at[s - 1], ((pool + s) % 4, dev))
        for s in range(1, 4)
    ]
    ql_gets = [
        remote(
            ql_ref, ql_in.at[(pool + 4 - s) % 4], ql_send.at[s - 1], ql_recv.at[s - 1], (head_partner, dev)
        )
        for s in range(1, 4)
    ]
    for copy in ql_sends:
        copy.start()
    n_a = arr_a.shape[0]

    def landing(j):
        return arr_a.at[j] if j < n_a else arr_b.at[j - n_a]

    sends = [None]
    for j in range(1, n_send):
        target = shifted(dev, OFFSETS[j], 1)
        copy = remote(
            outgoing.at[target], landing(j), page_send.at[j], page_recv.at[j], (pool, target)
        )
        copy.start()
        sends.append(copy)
    passes = [
        remote(
            outgoing.at[dev] if j == 0 else arr_a.at[j],
            pass_a.at[j],
            pass_send.at[j],
            pass_recv.at[j],
            (key_partner, dev),
        )
        for j in range(n_a)
    ]
    passes[0].start()

    loads[0].wait()
    projected = lax.dot_general(
        wd_v[...], hidden_ref[...], (((1,), (1,)), ((), ())), preferred_element_type=jnp.float32
    )
    latent = projected[:lat]
    latent = (
        latent
        * lax.rsqrt(jnp.mean(latent * latent, axis=0, keepdims=True) + 1e-06)
        * gain_ref[...].astype(jnp.float32)
    )
    first, second = projected[lat : lat + half_rope], projected[lat + half_rope :]
    lcos, lsin = lcos_ref[...], lsin_ref[...]
    new_rows = jnp.concatenate(
        [latent, first * lcos - second * lsin, first * lsin + second * lcos], axis=0
    )
    new_s[...] = new_rows.T.astype(jnp.bfloat16)
    new_send = remote(new_s, new_other, pair_send.at[0], pair_recv.at[0], (key_partner, dev))
    new_send.start()
    new_keep = pltpu.make_async_copy(new_s, new_own, load_sem.at[4])
    new_keep.start()

    ql_in[pool] = ql_ref[...]
    for copy in ql_gets:
        copy.wait_recv()
    for y in range(4):
        rows = ql_in[y].astype(jnp.float32)
        for r in range(req):
            q_full[pl.ds(r * new_len + y * quarter, quarter), :] = rows[
                r * quarter : (r + 1) * quarter
            ]
    for copy in loads[1:]:
        copy.wait()
    cos, sin = cos_ref[...], sin_ref[...]
    group = 128 // new_len
    width = nope + rope

    @pl.loop(0, heads // group)
    def _(g):
        lanes = pl.ds(pl.multiple_of(g * (group * width), 128), group * width)
        raw = jnp.dot(
            q_full[...].astype(jnp.bfloat16), qup_v[:, lanes], preferred_element_type=jnp.float32
        ).T
        built = []
        for j in range(group):
            at = j * width
            q_nope = raw[at : at + nope].astype(jnp.bfloat16)
            q_abs = lax.dot_general(
                wuk_v[g * group + j],
                q_nope,
                (((0,), (0,)), ((), ())),
                preferred_element_type=jnp.float32,
            )
            x = raw[at + nope : at + nope + half_rope]
            y = raw[at + nope + half_rope : at + width]
            built.append(
                jnp.concatenate([q_abs, x * cos - y * sin, x * sin + y * cos], axis=0).astype(
                    jnp.bfloat16
                )
            )
        cols = pl.ds(pl.multiple_of(g * 128, 128), 128)
        for r in range(req):
            q_s[r, :, cols] = jnp.concatenate(
                [b[:, r * new_len : (r + 1) * new_len] for b in built], axis=1
            )

    q_send = remote(q_s, q_other, pair_send.at[1], pair_recv.at[1], (head_partner, dev))
    q_send.start()
    q_keep = pltpu.make_async_copy(q_s, q_own, load_sem.at[5])
    q_keep.start()

    for j in range(1, n_send):
        sends[j].wait_recv()
        if j < n_a:
            passes[j].start()
    for copy in ql_sends:
        copy.wait_send()
    for copy in sends[1:]:
        copy.wait_send()
    own_pages.wait()
    new_keep.wait()
    q_keep.wait()
    new_send.wait()
    q_send.wait()
    for copy in passes:
        copy.wait()


def exchange(ql, hidden, outgoing, wd, qup, wuk, gain, cos, sin, lcos, lsin, req):
    n_cols, per, page, key_dim = outgoing.shape
    heads, nope, lat = wuk.shape
    tokens = ql.shape[0]
    new_len = 4 * tokens // req
    bf16 = jnp.bfloat16
    any_spec = pl.BlockSpec(memory_space=pl.ANY)
    vmem = pl.BlockSpec(memory_space=pltpu.VMEM)
    own_rows = heads * new_len
    query = jax.ShapeDtypeStruct((req, key_dim, own_rows), bf16)
    new = jax.ShapeDtypeStruct((tokens, key_dim), bf16)
    near = jax.ShapeDtypeStruct((FORWARDED, per, page, key_dim), bf16)
    far = jax.ShapeDtypeStruct((n_cols - FORWARDED, per, page, key_dim), bf16)
    dma = pltpu.SemaphoreType.DMA
    return pl.pallas_call(
        exchange_kernel,
        in_specs=[vmem, vmem, any_spec, any_spec, any_spec, any_spec] + [vmem] * 5,
        out_specs=[any_spec] * 7,
        out_shape=[near, far, near, query, query, new, new],
        scratch_shapes=[
            pltpu.VMEM((4,) + ql.shape, bf16),
            pltpu.VMEM(wd.shape, bf16),
            pltpu.VMEM(qup.shape, bf16),
            pltpu.VMEM(wuk.shape, bf16),
            pltpu.VMEM(query.shape, bf16),
            pltpu.VMEM(new.shape, bf16),
            pltpu.VMEM((req * new_len, ql.shape[1]), jnp.float32),
            dma((6,)),
            dma((3,)),
            dma((3,)),
            dma((n_cols,)),
            dma((n_cols,)),
            dma((FORWARDED,)),
            dma((FORWARDED,)),
            dma((2,)),
            dma((2,)),
        ],
        compiler_params=pltpu.CompilerParams(
            collective_id=1, has_side_effects=True, vmem_limit_bytes=48 * 2**20
        ),
        cost_estimate=pl.CostEstimate(flops=10**10, bytes_accessed=10**8, transcendentals=0),
        name="exchange",
    )(ql, hidden, outgoing, wd, qup, wuk, gain, cos, sin, lcos, lsin)


def attention_step(
    order_ref, start_ref, *refs, call, sizes, first, last, scale, lat, page, own_rows, new_len
):
    n_blocks = len(sizes)
    blocks, refs = refs[:n_blocks], refs[n_blocks:]
    q_refs, refs = refs[:2], refs[2:]
    if first:
        new_ref, new_pos_ref = refs[:2]
    else:
        acc_in, stat_in = refs[:2]
    refs = refs[2:]
    if last:
        mix_out, acc_out, stat_own, stat_part = refs[:4]
        refs = refs[4:]
    else:
        acc_out, stat_out = refs[:2]
        refs = refs[2:]
    pages, sem, first_scores, second_scores = refs[:4]
    acc = refs[4] if last else acc_out.at[0]
    sheets = (first_scores, second_scores)
    request = pl.program_id(0)

    @pl.when(request == 0)
    def _():
        copies, at = [], 0
        for i, block in enumerate(blocks):
            copies.append(
                pltpu.make_async_copy(block, pages.at[pl.ds(at, sizes[i])], sem.at[i])
            )
            at += sizes[i]
        for copy in copies:
            copy.start()
        for copy in copies:
            copy.wait()

    factor = scale * math.log2(math.e)
    half_cols = [pl.ds(half * own_rows, own_rows) for half in range(2)]
    pad = q_refs[0].shape[1] % 128
    bias_rows = jnp.where(
        lax.broadcasted_iota(jnp.int32, (pad, own_rows), 0) == 0, 1.0, 0.0
    ).astype(jnp.bfloat16)
    key_lane = lax.broadcasted_iota(jnp.int32, (page, pad), 1)

    def scores_of(keys, half):
        query = jnp.concatenate([q_refs[half][0], bias_rows], axis=0)
        return jnp.dot(keys, query, preferred_element_type=jnp.float32)

    def weigh(keys, weights):
        return lax.dot_general(
            keys[:, :lat], weights, (((0,), (0,)), ((), ())), preferred_element_type=jnp.float32
        )

    state = []
    for half in range(2):
        if first:
            new_keys = new_ref[0]
            score = jnp.dot(new_keys, q_refs[half][0], preferred_element_type=jnp.float32)
            token = lax.broadcasted_iota(jnp.int32, score.shape, 1) % new_len
            live = new_pos_ref[:, :1] <= token
            score = jnp.where(live, score, LOW)
            top = jnp.max(score, axis=0, keepdims=True)
            weights = jnp.where(live, jnp.exp2((score - top) * factor), 0.0)
            state += [top, jnp.sum(weights, axis=0, keepdims=True)]
            acc[:, half_cols[half]] = weigh(new_keys, weights.astype(jnp.bfloat16))
        else:
            state += [stat_in[0, 0:1, half_cols[half]], stat_in[0, 1:2, half_cols[half]]]
            acc[:, half_cols[half]] = acc_in[0, :, half_cols[half]]

    begin = start_ref[call * 8 + request]
    end = start_ref[call * 8 + request + 1]
    tiles = (end - begin + TILE - 1) // TILE

    def keys_of(tile):
        parts = []
        for g in range(TILE):
            spot = begin + tile * TILE + g
            rows = pages[order_ref[call * 128 + jnp.maximum(jnp.minimum(spot, end - 1), 0)]]
            bias = jnp.where((key_lane == 0) & (spot >= end), LOW, 0.0).astype(jnp.bfloat16)
            parts.append(jnp.concatenate([rows, bias], axis=1))
        return jnp.concatenate(parts, axis=0)

    def soften(half, top, total):
        score = sheets[half][...]
        new_top = jnp.maximum(top, jnp.max(score, axis=0, keepdims=True))
        shrink = jnp.exp2((top - new_top) * factor)
        weights = jnp.exp2((score - new_top) * factor)
        total = total * shrink + jnp.sum(weights, axis=0, keepdims=True)
        return new_top, total, shrink, weights.astype(jnp.bfloat16)

    def add(half, keys, weights, shrink):
        cols = half_cols[half]
        acc[:, cols] = acc[:, cols] * shrink + weigh(keys, weights)

    @pl.when(tiles > 0)
    def _():
        sheets[0][...] = scores_of(keys_of(0), 0)

    def body(tile, carry):
        top0, total0, top1, total1 = carry
        keys = keys_of(tile)
        sheets[1][...] = scores_of(keys, 1)
        top0, total0, shrink, weights = soften(0, top0, total0)
        add(0, keys, weights, shrink)
        sheets[0][...] = scores_of(keys_of(jnp.minimum(tile + 1, tiles - 1)), 0)
        top1, total1, shrink, weights = soften(1, top1, total1)
        add(1, keys, weights, shrink)
        return top0, total0, top1, total1

    state = lax.fori_loop(0, tiles, body, tuple(state))

    if last:
        stat_own[request, 0:1, :] = state[0]
        stat_own[request, 1:2, :] = state[1]
        stat_part[request, 0:1, :] = state[2]
        stat_part[request, 1:2, :] = state[3]
        inverse = jnp.where(state[3] > 0, 1.0 / state[3], 0.0)
        for g in range(own_rows // 128):
            acc_out[g, 0] = acc[:, g * 128 : (g + 1) * 128]
            at = own_rows + g * 128
            mix_out[g, 0] = (
                acc[:, at : at + 128] * inverse[:, g * 128 : (g + 1) * 128]
            ).astype(jnp.bfloat16)
    else:
        for half in range(2):
            stat_out[0, 0:1, half_cols[half]] = state[2 * half]
            stat_out[0, 1:2, half_cols[half]] = state[2 * half + 1]


def attend(call, order, start, blocks, queries, state, new, scale, lat, new_len):
    first, last = call == 0, call == 1
    req, key_dim, own_rows = queries[0].shape
    page = blocks[0].shape[1]
    rows = 2 * own_rows
    sizes = [b.shape[0] for b in blocks]
    count = sum(sizes)
    kernel = functools.partial(
        attention_step,
        call=call,
        sizes=sizes,
        first=first,
        last=last,
        scale=scale,
        lat=lat,
        page=page,
        own_rows=own_rows,
        new_len=new_len,
    )
    in_specs = [pl.BlockSpec(memory_space=pl.ANY)] * len(blocks)
    in_specs += [pl.BlockSpec((1, key_dim, own_rows), lambda r, *_: (r, 0, 0))] * 2
    operands = list(blocks) + list(queries)
    acc_spec = pl.BlockSpec((1, lat, rows), lambda r, *_: (r, 0, 0))
    stat_spec = pl.BlockSpec((1, 2, rows), lambda r, *_: (r, 0, 0))
    if first:
        in_specs += [
            pl.BlockSpec((1,) + new[0].shape[1:], lambda r, *_: (r, 0, 0)),
            pl.BlockSpec(new[1].shape, lambda r, *_: (0, 0)),
        ]
        operands += list(new)
    else:
        in_specs += [acc_spec, stat_spec]
        operands += list(state)
    scratch = [
        pltpu.VMEM((count, page, key_dim), jnp.bfloat16),
        pltpu.SemaphoreType.DMA((len(blocks),)),
        pltpu.VMEM((TILE * page, own_rows), jnp.float32),
        pltpu.VMEM((TILE * page, own_rows), jnp.float32),
    ]
    if last:
        scratch.append(pltpu.VMEM((lat, rows), jnp.float32))
        groups = own_rows // 128
        group_spec = pl.BlockSpec((groups, 1, lat, 128), lambda r, *_: (0, r, 0, 0))
        small_spec = pl.BlockSpec((req, 2, own_rows), lambda r, *_: (0, 0, 0))
        out_specs = [group_spec, group_spec, small_spec, small_spec]
        out_shape = [
            jax.ShapeDtypeStruct((groups, req, lat, 128), jnp.bfloat16),
            jax.ShapeDtypeStruct((groups, req, lat, 128), jnp.float32),
            jax.ShapeDtypeStruct((req, 2, own_rows), jnp.float32),
            jax.ShapeDtypeStruct((req, 2, own_rows), jnp.float32),
        ]
    else:
        out_specs = [acc_spec, stat_spec]
        out_shape = [
            jax.ShapeDtypeStruct((req, lat, rows), jnp.float32),
            jax.ShapeDtypeStruct((req, 2, rows), jnp.float32),
        ]
    return pl.pallas_call(
        kernel,
        grid_spec=pltpu.PrefetchScalarGridSpec(
            num_scalar_prefetch=2,
            grid=(req,),
            in_specs=in_specs,
            out_specs=out_specs,
            scratch_shapes=scratch,
        ),
        out_shape=out_shape,
        compiler_params=pltpu.CompilerParams(
            dimension_semantics=("arbitrary",), vmem_limit_bytes=48 * 2**20
        ),
        cost_estimate=pl.CostEstimate(
            flops=2 * rows * count * page * (key_dim + lat),
            bytes_accessed=4 * req * lat * rows * 2 + count * page * key_dim * 2,
            transcendentals=rows * count * page,
        ),
        name=f"attend_{call}",
    )(order, start, *operands)


def merge_kernel(
    mix_ref, acc_ref, wuv_ref, stat_own, stat_part, out_ref,
    mix_in, stat_in, acc_v, wuv_v, load_sem, send_sem, recv_sem, *, factor,
):
    pool, dev = lax.axis_index("pool"), lax.axis_index("dev")
    head_partner, _ = partners(pool, dev)
    groups, req, lat, _ = mix_in.shape
    heads, _, head_v = wuv_v.shape
    group = heads // groups
    new_len = 128 // group
    loads = [pltpu.make_async_copy(wuv_ref, wuv_v, load_sem.at[groups])]
    loads += [
        pltpu.make_async_copy(acc_ref.at[g], acc_v.at[g], load_sem.at[g]) for g in range(groups)
    ]
    barrier = pltpu.get_barrier_semaphore()
    pl.semaphore_signal(barrier, inc=1, device_id=(head_partner, dev), device_id_type=MESH)
    pl.semaphore_wait(barrier, 1)

    def remote(src, dst, i):
        return pltpu.make_async_remote_copy(
            src_ref=src,
            dst_ref=dst,
            send_sem=send_sem.at[i],
            recv_sem=recv_sem.at[i],
            device_id=(head_partner, dev),
            device_id_type=MESH,
        )

    sends = [remote(stat_part, stat_in, groups)]
    sends += [remote(mix_ref.at[g], mix_in.at[g], g) for g in range(groups)]
    for copy in sends:
        copy.start()
    for copy in loads:
        copy.start()
    sends[0].wait_recv()
    own_share, got_share = [], []
    for r in range(req):
        top_own, top_got = stat_own[r, 0:1, :], stat_in[r, 0:1, :]
        top = jnp.maximum(top_own, top_got)
        scale_own = jnp.exp2((top_own - top) * factor)
        mass_got = stat_in[r, 1:2, :] * jnp.exp2((top_got - top) * factor)
        inverse = 1.0 / (stat_own[r, 1:2, :] * scale_own + mass_got)
        own_share.append(scale_own * inverse)
        got_share.append(mass_got * inverse)
    loads[0].wait()
    for g in range(groups):
        loads[1 + g].wait()
        sends[1 + g].wait_recv()
        lanes = slice(g * 128, (g + 1) * 128)
        mixed = [
            (
                acc_v[g, r] * own_share[r][:, lanes]
                + mix_in[g, r].astype(jnp.float32) * got_share[r][:, lanes]
            ).astype(jnp.bfloat16)
            for r in range(req)
        ]
        for j in range(group):
            part = jnp.concatenate(
                [m[:, j * new_len : (j + 1) * new_len] for m in mixed], axis=1
            )
            head = g * group + j
            result = lax.dot_general(
                part, wuv_v[head], (((0,), (0,)), ((), ())), preferred_element_type=jnp.float32
            ).astype(jnp.bfloat16)
            for r in range(req):
                out_ref[r, :, head * head_v : (head + 1) * head_v] = result[
                    r * new_len : (r + 1) * new_len
                ]
    for copy in sends:
        copy.wait_send()


def merge(mix, acc, w_uv, stat_own, stat_part, scale):
    groups, req, lat, _ = mix.shape
    heads, _, head_v = w_uv.shape
    new_len = groups * 128 // heads
    any_spec = pl.BlockSpec(memory_space=pl.ANY)
    vmem = pl.BlockSpec(memory_space=pltpu.VMEM)
    return pl.pallas_call(
        functools.partial(merge_kernel, factor=scale * math.log2(math.e)),
        in_specs=[any_spec, any_spec, any_spec, vmem, vmem],
        out_specs=vmem,
        out_shape=jax.ShapeDtypeStruct((req, new_len, heads * head_v), jnp.bfloat16),
        scratch_shapes=[
            pltpu.VMEM(mix.shape, jnp.bfloat16),
            pltpu.VMEM(stat_part.shape, jnp.float32),
            pltpu.VMEM(acc.shape, jnp.float32),
            pltpu.VMEM(w_uv.shape, jnp.bfloat16),
            pltpu.SemaphoreType.DMA((groups + 1,)),
            pltpu.SemaphoreType.DMA((groups + 1,)),
            pltpu.SemaphoreType.DMA((groups + 1,)),
        ],
        compiler_params=pltpu.CompilerParams(
            collective_id=2, has_side_effects=True, vmem_limit_bytes=32 * 2**20
        ),
        name="merge",
    )(mix, acc, w_uv, stat_own, stat_part)


def on_device(
    hidden,
    query_latent_rows,
    store,
    w_down,
    kv_gain,
    query_up_weight,
    w_uk,
    w_uv,
    prefix_pages,
    page_owner,
    page_slot,
    decode_order,
):
    pool_count = lax.axis_size("pool")
    dev_count = lax.axis_size("dev")
    pool_index = lax.axis_index("pool")
    column = lax.axis_index("dev")
    req_col, quarter, model_width = hidden.shape
    new_len = quarter * pool_count
    lat_dim = kv_gain.shape[0]
    key_dim = w_down.shape[1]
    heads_local, nope_dim, _ = w_uk.shape
    rope_dim = key_dim - lat_dim
    page_len = store.shape[2]
    n_slots = store.shape[1]
    max_pages = page_owner.shape[1]
    list_len = req_col * max_pages
    first_row = column * req_col
    score_scale = (nope_dim + rope_dim) ** (-0.5)
    head_partner, key_partner = partners(pool_index, column)

    owner_t, slot_t = page_owner.T, page_slot.T
    page_of = jnp.arange(max_pages, dtype=jnp.int32)
    within = jnp.arange(prefix_pages.shape[0], dtype=jnp.int32) % req_col
    entry = within[None, :] * max_pages + page_of[:, None]
    used = page_of[:, None] < prefix_pages[None, :]
    mine = jnp.logical_and(owner_t == pool_index * dev_count + column, used)
    code = entry * n_slots + slot_t
    low = jnp.min(jnp.where(mine, code, list_len * n_slots), axis=0)
    high = jnp.max(jnp.where(mine, code, 0), axis=0)
    low = jnp.min(low.reshape(dev_count, req_col), axis=1)
    high = jnp.max(high.reshape(dev_count, req_col), axis=1)
    outgoing = store[0][jnp.stack([low, high], axis=1) % n_slots]

    prefix_mine = lax.dynamic_slice_in_dim(prefix_pages, first_row, req_col)
    frequency = jnp.exp(
        jnp.arange(rope_dim // 2, dtype=jnp.float32) * (-2.0 * jnp.log(50000.0) / rope_dim)
    )
    positions = prefix_mine[:, None] * page_len + jnp.arange(new_len, dtype=jnp.int32)[None, :]
    local_pos = (
        prefix_mine[:, None] * page_len
        + pool_index * quarter
        + jnp.arange(quarter, dtype=jnp.int32)[None, :]
    )
    angles = frequency[:, None] * positions.reshape(-1).astype(jnp.float32)[None, :]
    local_angles = frequency[:, None] * local_pos.reshape(-1).astype(jnp.float32)[None, :]

    near, far, passed, query, query_other, new_local, new_other = exchange(
        query_latent_rows.reshape(req_col * quarter, -1),
        hidden.reshape(req_col * quarter, model_width),
        outgoing,
        w_down.T,
        query_up_weight,
        w_uk,
        kv_gain[:, None],
        jnp.cos(angles),
        jnp.sin(angles),
        jnp.cos(local_angles),
        jnp.sin(local_angles),
        req_col,
    )
    pairs = []
    for pool in range(pool_count):
        for dev in range(dev_count):
            pairs.append((pool * dev_count + dev, partners(pool, dev)[1] * dev_count + dev))
    passed_far = lax.ppermute(far, ("pool", "dev"), pairs)

    own_t = lax.dynamic_slice_in_dim(owner_t, first_row, req_col, 1)
    own_used = page_of[:, None] < prefix_mine[None, :]
    own_entry = jnp.arange(req_col, dtype=jnp.int32)[None, :] * max_pages + page_of[:, None]
    senders = jnp.stack([shifted(column, offset, -1) for offset in OFFSETS])
    source = (
        jnp.stack([pool_index, key_partner])[:, None] * dev_count + senders[None, :]
    ).reshape(-1)
    hit = jnp.logical_and(own_t[None] == source[:, None, None], own_used[None])
    head_entry = jnp.min(jnp.where(hit, own_entry[None], list_len), axis=(1, 2))
    tail_entry = jnp.max(jnp.where(hit, own_entry[None], -1), axis=(1, 2))
    req_low = head_entry // max_pages
    req_high = jnp.where(tail_entry > head_entry, tail_entry // max_pages, req_col)
    slots = jnp.stack([req_low, req_high], axis=1).reshape(2, 2 * dev_count)
    cut = 2 * FORWARDED
    width = 4 * dev_count
    listed = [
        jnp.concatenate([slots[0, :cut], slots[1, :cut], slots[0, cut:]]),
        slots[1, cut:],
    ]
    lists = jnp.stack(
        [jnp.concatenate([x, jnp.full((width - x.shape[0],), req_col, jnp.int32)]) for x in listed]
    )
    spot = jnp.arange(width, dtype=jnp.int32)
    rank_key = lists * width + spot
    rank = jnp.sum((rank_key[:, None, :] < rank_key[:, :, None]).astype(jnp.int32), axis=-1)
    order = jnp.sum(
        jnp.where(rank[:, None, :] == spot[None, :, None], spot[None, None, :], 0), axis=-1
    ).reshape(-1)
    start = jnp.sum(
        (lists[:, None, :] < jnp.arange(8, dtype=jnp.int32)[None, :, None]).astype(jnp.int32),
        axis=-1,
    ).reshape(-1)

    new_local = new_local.reshape(req_col, quarter, key_dim)
    new_other = new_other.reshape(req_col, quarter, key_dim)
    handed = new_local[lax.dynamic_slice_in_dim(decode_order, first_row, req_col) - first_row]
    new_keys = jnp.concatenate([new_local, new_other], axis=1)
    turn = jnp.arange(quarter, dtype=jnp.int32)
    new_pos = jnp.concatenate([pool_index * quarter + turn, key_partner * quarter + turn])
    new_pos = jnp.broadcast_to(new_pos[:, None], (2 * quarter, 128))

    def flat_pages(block):
        return block.reshape((-1,) + block.shape[2:])

    queries = (query, query_other)
    common = dict(scale=score_scale, lat=lat_dim, new_len=new_len)
    state = attend(
        0,
        order,
        start,
        [flat_pages(near), flat_pages(passed), flat_pages(far)],
        queries,
        None,
        (new_keys, new_pos),
        **common,
    )
    mix, acc, stat_own, stat_part = attend(
        1, order, start, [flat_pages(passed_far)], queries, state, None, **common
    )
    attended = merge(mix, acc, w_uv, stat_own, stat_part, score_scale)
    return (attended, handed)


def solution(mesh):
    in_specs = (
        P("dev", "pool", None),
        P("dev", "pool", None),
        P(("pool", "dev"), None, None, None),
        P(),
        P(),
        P(None, "pool"),
        P("pool", None, None),
        P("pool", None, None),
        P(),
        P(),
        P(),
        P(),
    )
    out_specs = (P("dev", None, "pool"), P("dev", "pool", None))
    return jax.shard_map(
        on_device, mesh=mesh, in_specs=in_specs, out_specs=out_specs, check_vma=False
    )
```

```python
import functools
import math

import jax
import jax.numpy as jnp
from jax import lax
from jax.experimental import pallas as pl
from jax.experimental.pallas import tpu as pltpu
from jax.sharding import PartitionSpec as P

TILE = 4
LOW = -1e30
FORWARDED = 24
VMEM_BYTES = 60 * 2**20
MESH = pl.DeviceIdType.MESH
STEPS = [
    (0, 1), (1, 0), (0, 3), (3, 0), (1, 1), (3, 3), (1, 3), (3, 1),
    (0, 2), (2, 0), (1, 2), (2, 1), (3, 2), (2, 3), (2, 2),
]
OFFSETS = [(0, 0, 0), (0, 0, 1)] + [(z, x, c) for z, x in STEPS for c in (0, 1)]


def shifted(dev, offset, sign):
    core, x, z = dev % 2, (dev // 2) % 4, dev // 8
    dz, dx, dc = offset
    return ((z + sign * dz + 4) % 4 * 4 + (x + sign * dx + 4) % 4) * 2 + (core + dc) % 2


def partners(pool, dev):
    near = pool + 1 - 2 * (pool % 2)
    far = 3 - pool
    odd = dev % 2
    return near + odd * (far - near), far + odd * (near - far)


def exchange_kernel(
    slot_ref, ql_ref, hidden_ref, gain_ref, cos_ref, sin_ref, lcos_ref, lsin_ref, store_ref, wd_ref, qup_ref, wuk_ref,
    arr_a, arr_b, pass_a, q_own, q_other, new_own, new_other,
    store_v, packed, ql_in, wd_v, qup_v, wuk_v, q_s, new_s, q_full,
    load_sem, ql_send, ql_recv, page_send, page_recv, pass_send, pass_recv, pair_send, pair_recv,
):
    pool, dev = lax.axis_index("pool"), lax.axis_index("dev")
    head_partner, key_partner = partners(pool, dev)
    req, key_dim, own_rows = q_s.shape
    heads, nope, lat = wuk_v.shape
    rope = key_dim - lat
    half_rope = rope // 2
    quarter = ql_in.shape[1] // req
    new_len = 4 * quarter
    page = store_v.shape[1]
    n_send = len(OFFSETS)
    n_a = arr_a.shape[0]

    load_store = pltpu.make_async_copy(store_ref, store_v, load_sem.at[6])
    load_store.start()
    loads = [
        pltpu.make_async_copy(wd_ref, wd_v, load_sem.at[0]),
        pltpu.make_async_copy(qup_ref, qup_v, load_sem.at[1]),
        pltpu.make_async_copy(wuk_ref, wuk_v, load_sem.at[2]),
    ]
    for copy in loads:
        copy.start()

    barrier = pltpu.get_barrier_semaphore()
    for offset in OFFSETS[1:]:
        pl.semaphore_signal(
            barrier, inc=1, device_id=(pool, shifted(dev, offset, 1)), device_id_type=MESH
        )
    for step in range(1, 4):
        pl.semaphore_signal(
            barrier, inc=1, device_id=((pool + step) % 4, dev), device_id_type=MESH
        )

    def pack(j):
        target = shifted(dev, OFFSETS[j], 1)
        pages = [store_v[slot_ref[2 * target + k]] for k in range(2)]
        for k in range(2):
            packed[j, k * page : (k + 1) * page, :] = pages[k][:, :lat]
        keys = jnp.concatenate([p[:, lat:] for p in pages], axis=1)
        step = page * 2 * rope // lat
        packed[j, 2 * page :, :] = jnp.concatenate(
            [keys[i * step : (i + 1) * step] for i in range(page // step)], axis=1
        )

    load_store.wait()
    pack(0)
    pack(1)
    pl.semaphore_wait(barrier, n_send - 1 + 3)

    def remote(src, dst, send, recv, target):
        return pltpu.make_async_remote_copy(
            src_ref=src, dst_ref=dst, send_sem=send, recv_sem=recv, device_id=target, device_id_type=MESH
        )

    ql_sends = [
        remote(ql_ref, ql_in.at[pool], ql_send.at[s - 1], ql_recv.at[s - 1], ((pool + s) % 4, dev))
        for s in range(1, 4)
    ]
    ql_gets = [
        remote(
            ql_ref, ql_in.at[(pool + 4 - s) % 4], ql_send.at[s - 1], ql_recv.at[s - 1], (head_partner, dev)
        )
        for s in range(1, 4)
    ]
    for copy in ql_sends:
        copy.start()

    def landing(j):
        return arr_a.at[j] if j < n_a else arr_b.at[j - n_a]

    passes = [
        remote(
            packed.at[0] if j == 0 else arr_a.at[j],
            pass_a.at[j],
            pass_send.at[j],
            pass_recv.at[j],
            (key_partner, dev),
        )
        for j in range(n_a)
    ]
    sends = [None]
    for j in range(1, n_send):
        if j > 1:
            pack(j)
        copy = remote(
            packed.at[j],
            landing(j),
            page_send.at[j],
            page_recv.at[j],
            (pool, shifted(dev, OFFSETS[j], 1)),
        )
        copy.start()
        sends.append(copy)
        if j == 1:
            passes[0].start()
    own_pages = pltpu.make_async_copy(packed.at[0], arr_a.at[0], load_sem.at[3])
    own_pages.start()

    def pass_on(first, last):
        for j in range(first, last):
            sends[j].wait_recv()
            if j < n_a:
                passes[j].start()

    loads[0].wait()
    projected = lax.dot_general(
        wd_v[...], hidden_ref[...], (((1,), (1,)), ((), ())), preferred_element_type=jnp.float32
    )
    latent = projected[:lat]
    latent = latent * lax.rsqrt(jnp.mean(latent * latent, axis=0, keepdims=True) + 1e-06)
    first, second = projected[lat : lat + half_rope], projected[lat + half_rope :]
    lcos, lsin = lcos_ref[...], lsin_ref[...]
    rotated = jnp.concatenate([first * lcos - second * lsin, first * lsin + second * lcos], axis=0)
    new_s[...] = jnp.concatenate(
        [latent.T * gain_ref[...].astype(jnp.float32), rotated.T], axis=1
    ).astype(jnp.bfloat16)
    new_send = remote(new_s, new_other, pair_send.at[0], pair_recv.at[0], (key_partner, dev))
    new_send.start()
    new_keep = pltpu.make_async_copy(new_s, new_own, load_sem.at[4])
    new_keep.start()
    pass_on(1, 3)

    ql_in[pool] = ql_ref[...]
    for copy in ql_gets:
        copy.wait_recv()
    for y in range(4):
        rows = ql_in[y].astype(jnp.float32)
        for r in range(req):
            q_full[pl.ds(r * new_len + y * quarter, quarter), :] = rows[
                r * quarter : (r + 1) * quarter
            ]
    for copy in loads[1:]:
        copy.wait()
    group = 128 // new_len
    width = nope + rope

    def project(g):
        raw = jnp.dot(
            q_full[...].astype(jnp.bfloat16),
            qup_v[:, g * group * width : (g + 1) * group * width],
            preferred_element_type=jnp.float32,
        ).T
        cos, sin = cos_ref[...], sin_ref[...]
        built = []
        for j in range(group):
            at = j * width
            q_nope = raw[at : at + nope].astype(jnp.bfloat16)
            q_abs = lax.dot_general(
                wuk_v[g * group + j],
                q_nope,
                (((0,), (0,)), ((), ())),
                preferred_element_type=jnp.float32,
            )
            x = raw[at + nope : at + nope + half_rope]
            y = raw[at + nope + half_rope : at + width]
            built.append(
                jnp.concatenate([q_abs, x * cos - y * sin, x * sin + y * cos], axis=0).astype(
                    jnp.bfloat16
                )
            )
        for r in range(req):
            q_s[r, :, g * 128 : (g + 1) * 128] = jnp.concatenate(
                [b[:, r * new_len : (r + 1) * new_len] for b in built], axis=1
            )

    done = 3
    for g in range(heads // group):
        project(g)
        if g < heads // group - 1:
            pass_on(done, done + 2)
            done += 2

    q_send = remote(q_s, q_other, pair_send.at[1], pair_recv.at[1], (head_partner, dev))
    q_send.start()
    q_keep = pltpu.make_async_copy(q_s, q_own, load_sem.at[5])
    q_keep.start()

    pass_on(done, n_send)
    for copy in ql_sends:
        copy.wait_send()
    for copy in sends[1:]:
        copy.wait_send()
    own_pages.wait()
    new_keep.wait()
    q_keep.wait()
    new_send.wait()
    q_send.wait()
    for copy in passes:
        copy.wait()


def exchange(slots, ql, hidden, gain, angles, store, wd, qup, wuk, req):
    n_cols = slots.shape[0] // 2
    n_slots, page, key_dim = store.shape
    heads, nope, lat = wuk.shape
    tokens = ql.shape[0]
    new_len = 4 * tokens // req
    bf16 = jnp.bfloat16
    any_spec = pl.BlockSpec(memory_space=pl.ANY)
    vmem = pl.BlockSpec(memory_space=pltpu.VMEM)
    own_rows = heads * new_len
    pair = (2 * page * key_dim // lat, lat)
    query = jax.ShapeDtypeStruct((req, key_dim, own_rows), bf16)
    new = jax.ShapeDtypeStruct((tokens, key_dim), bf16)
    near = jax.ShapeDtypeStruct((FORWARDED,) + pair, bf16)
    far = jax.ShapeDtypeStruct((n_cols - FORWARDED,) + pair, bf16)
    dma = pltpu.SemaphoreType.DMA
    return pl.pallas_call(
        exchange_kernel,
        in_specs=[pl.BlockSpec(memory_space=pltpu.SMEM)] + [vmem] * 7 + [any_spec] * 4,
        out_specs=[any_spec] * 7,
        out_shape=[near, far, near, query, query, new, new],
        scratch_shapes=[
            pltpu.VMEM(store.shape, bf16),
            pltpu.VMEM((n_cols,) + pair, bf16),
            pltpu.VMEM((4,) + ql.shape, bf16),
            pltpu.VMEM(wd.shape, bf16),
            pltpu.VMEM(qup.shape, bf16),
            pltpu.VMEM(wuk.shape, bf16),
            pltpu.VMEM(query.shape, bf16),
            pltpu.VMEM(new.shape, bf16),
            pltpu.VMEM((req * new_len, ql.shape[1]), jnp.float32),
            dma((7,)),
            dma((3,)),
            dma((3,)),
            dma((n_cols,)),
            dma((n_cols,)),
            dma((FORWARDED,)),
            dma((FORWARDED,)),
            dma((2,)),
            dma((2,)),
        ],
        compiler_params=pltpu.CompilerParams(
            collective_id=1, has_side_effects=True, vmem_limit_bytes=VMEM_BYTES
        ),
        cost_estimate=pl.CostEstimate(flops=10**10, bytes_accessed=10**8, transcendentals=0),
        name="exchange",
    )(slots, ql, hidden, gain, *angles, store, wd, qup, wuk)


def attention_step(
    order_ref, start_ref, *refs, call, sizes, first, kind, scale, page, new_len
):
    n_blocks = len(sizes)
    blocks, refs = refs[:n_blocks], refs[n_blocks:]
    q_ref, refs = refs[0], refs[1:]
    inputs, refs = refs[:2], refs[2:]
    result, mass, refs = refs[0], refs[1], refs[2:]
    pairs, sem, even, odd = refs[:4]
    acc = result.at[0] if kind == "state" else refs[4]
    lat, rows = acc.shape
    request = pl.program_id(0)

    @pl.when(request == 0)
    def _():
        copies, at = [], 0
        for i, block in enumerate(blocks):
            copies.append(pltpu.make_async_copy(block, pairs.at[pl.ds(at, sizes[i])], sem.at[i]))
            at += sizes[i]
        for copy in copies:
            copy.start()
        for copy in copies:
            copy.wait()

    factor = scale * math.log2(math.e)
    rope = q_ref.shape[1] - lat
    pad = 128 - rope
    bias_rows = jnp.where(
        lax.broadcasted_iota(jnp.int32, (pad, rows), 0) == 0, 1.0, 0.0
    ).astype(jnp.bfloat16)
    key_lane = lax.broadcasted_iota(jnp.int32, (page, pad), 1)

    def weigh(keys, weights):
        return lax.dot_general(
            keys[:, :lat], weights, (((0,), (0,)), ((), ())), preferred_element_type=jnp.float32
        )

    if first:
        new_ref, new_pos_ref = inputs
        new_keys = new_ref[0]
        score = jnp.dot(new_keys, q_ref[0], preferred_element_type=jnp.float32)
        token = lax.broadcasted_iota(jnp.int32, score.shape, 1) % new_len
        live = new_pos_ref[:, :1] <= token
        score = jnp.where(live, score, LOW)
        top = jnp.max(score, axis=0, keepdims=True)
        weights = jnp.where(live, jnp.exp2((score - top) * factor), 0.0)
        total = jnp.sum(weights, axis=0, keepdims=True)
        acc[...] = weigh(new_keys, weights.astype(jnp.bfloat16))
    else:
        acc_in, mass_in = inputs
        top, total = mass_in[0, 0:1, :], mass_in[0, 1:2, :]
        acc[...] = acc_in[0]

    begin = start_ref[call * 8 + request]
    end = start_ref[call * 8 + request + 1]
    tiles = (end - begin + TILE - 1) // TILE

    def keys_of(tile):
        parts = []
        for g in range(TILE):
            spot = begin + tile * TILE + g
            index = order_ref[call * 128 + jnp.maximum(jnp.minimum(spot, end - 1), 0)]
            pair, turn = index // 2, index % 2
            latent = pairs[pair, pl.ds(pl.multiple_of(turn * page, page), page), :]
            both = pairs[pair, pl.ds(2 * page, 2 * page * rope // lat), :]
            both = jnp.concatenate([both[:, i * 128 : (i + 1) * 128] for i in range(lat // 128)], axis=0)
            rotary = jnp.where(turn == 0, both[:, :rope], both[:, rope:])
            bias = jnp.where((key_lane == 0) & (spot >= end), LOW, 0.0).astype(jnp.bfloat16)
            parts.append(jnp.concatenate([latent, rotary, bias], axis=1))
        return jnp.concatenate(parts, axis=0)

    def scores_of(keys):
        query = jnp.concatenate([q_ref[0], bias_rows], axis=0)
        return jnp.dot(keys, query, preferred_element_type=jnp.float32)

    def take(sheet, keys, top, total):
        score = sheet[...]
        new_top = jnp.maximum(top, jnp.max(score, axis=0, keepdims=True))
        shrink = jnp.exp2((top - new_top) * factor)
        weights = jnp.exp2((score - new_top) * factor)
        total = total * shrink + jnp.sum(weights, axis=0, keepdims=True)
        acc[...] = acc[...] * shrink + weigh(keys, weights.astype(jnp.bfloat16))
        return new_top, total

    @pl.when(tiles > 0)
    def _():
        even[...] = scores_of(keys_of(0))

    def body(step, carry):
        tile = 2 * step
        later = keys_of(tile + 1)
        odd[...] = scores_of(later)
        carry = take(even, keys_of(tile), *carry)
        even[...] = scores_of(keys_of(jnp.minimum(tile + 2, tiles - 1)))
        return take(odd, later, *carry)

    carry = lax.fori_loop(0, tiles // 2, body, (top, total))
    top, total = lax.cond(
        tiles % 2 == 1,
        lambda c: take(even, keys_of(tiles - 1), *c),
        lambda c: c,
        carry,
    )

    if kind == "state":
        mass[0, 0:1, :] = top
        mass[0, 1:2, :] = total
        return
    live = total > 0
    inverse = jnp.where(live, 1.0 / total, 0.0)
    log_mass = jnp.where(live, top * factor + jnp.log(total) * math.log2(math.e), LOW)
    mass[request] = log_mass
    groups = rows // 128
    for g in range(groups):
        lanes = slice(g * 128, (g + 1) * 128)
        mixed = acc[:, lanes] * inverse[:, lanes]
        if kind == "own":
            result[g, 0] = mixed
        else:
            result[g, 0, :lat, :] = mixed.astype(jnp.bfloat16)
            high = log_mass[:, lanes].astype(jnp.bfloat16)
            rest = log_mass[:, lanes] - high.astype(jnp.float32)
            middle = rest.astype(jnp.bfloat16)
            low = (rest - middle.astype(jnp.float32)).astype(jnp.bfloat16)
            row = lax.broadcasted_iota(jnp.int32, (16, 128), 0)
            terms = [t.astype(jnp.float32) for t in (high, middle, low)]
            result[g, 0, lat:, :] = jnp.where(
                row == 0, terms[0], jnp.where(row == 1, terms[1], jnp.where(row == 2, terms[2], 0.0))
            ).astype(jnp.bfloat16)


def attend(call, order, start, blocks, query, inputs, kind, scale, lat, new_len):
    first = inputs[0].dtype == jnp.bfloat16
    req, key_dim, rows = query.shape
    sizes = [b.shape[0] for b in blocks]
    count = sum(sizes)
    page = blocks[0].shape[1] * lat // key_dim // 2
    groups = rows // 128
    kernel = functools.partial(
        attention_step, call=call, sizes=sizes, first=first, kind=kind, scale=scale, page=page, new_len=new_len
    )
    acc_spec = pl.BlockSpec((1, lat, rows), lambda r, *_: (r, 0, 0))
    mass_spec = pl.BlockSpec((1, 2, rows), lambda r, *_: (r, 0, 0))
    in_specs = [pl.BlockSpec(memory_space=pl.ANY)] * len(blocks)
    in_specs += [pl.BlockSpec((1, key_dim, rows), lambda r, *_: (r, 0, 0))]
    if first:
        in_specs += [
            pl.BlockSpec((1,) + inputs[0].shape[1:], lambda r, *_: (r, 0, 0)),
            pl.BlockSpec(inputs[1].shape, lambda r, *_: (0, 0)),
        ]
    else:
        in_specs += [acc_spec, mass_spec]
    scratch = [
        pltpu.VMEM((count,) + blocks[0].shape[1:], jnp.bfloat16),
        pltpu.SemaphoreType.DMA((len(blocks),)),
        pltpu.VMEM((TILE * page, rows), jnp.float32),
        pltpu.VMEM((TILE * page, rows), jnp.float32),
    ]
    if kind == "state":
        out_specs = [acc_spec, mass_spec]
        out_shape = [
            jax.ShapeDtypeStruct((req, lat, rows), jnp.float32),
            jax.ShapeDtypeStruct((req, 2, rows), jnp.float32),
        ]
    else:
        scratch.append(pltpu.VMEM((lat, rows), jnp.float32))
        deep = lat + 16 if kind == "partner" else lat
        out_specs = [
            pl.BlockSpec((groups, 1, deep, 128), lambda r, *_: (0, r, 0, 0)),
            pl.BlockSpec((req, 1, rows), lambda r, *_: (0, 0, 0)),
        ]
        out_shape = [
            jax.ShapeDtypeStruct(
                (groups, req, deep, 128), jnp.bfloat16 if kind == "partner" else jnp.float32
            ),
            jax.ShapeDtypeStruct((req, 1, rows), jnp.float32),
        ]
    return pl.pallas_call(
        kernel,
        grid_spec=pltpu.PrefetchScalarGridSpec(
            num_scalar_prefetch=2,
            grid=(req,),
            in_specs=in_specs,
            out_specs=out_specs,
            scratch_shapes=scratch,
        ),
        out_shape=out_shape,
        compiler_params=pltpu.CompilerParams(
            dimension_semantics=("arbitrary",), vmem_limit_bytes=VMEM_BYTES
        ),
        cost_estimate=pl.CostEstimate(
            flops=8 * rows * count * page * (key_dim + lat),
            bytes_accessed=4 * req * lat * rows * 2 + count * page * key_dim * 2,
            transcendentals=2 * rows * count * page,
        ),
        name=f"attend_{call}_{kind}",
    )(order, start, *blocks, query, *inputs)


def merge_step(got_ref, own_ref, mass_ref, wuv_ref, out_ref):
    _, req, deep, _ = got_ref.shape
    group, lat, head_v = wuv_ref.shape
    new_len = 128 // group
    high, low = [], []
    for r in range(req):
        tail = got_ref[0, r, lat:, :].astype(jnp.float32)
        got_mass = tail[0:1] + tail[1:2] + tail[2:3]
        share = 1.0 / (1.0 + jnp.exp2(mass_ref[r] - got_mass))
        mixed = own_ref[0, r] * (1.0 - share) + got_ref[0, r, :lat, :].astype(jnp.float32) * share
        high.append(mixed.astype(jnp.bfloat16))
        low.append((mixed - high[-1].astype(jnp.float32)).astype(jnp.bfloat16))
    for j in range(group):
        total = None
        for part in (high, low):
            columns = jnp.concatenate([m[:, j * new_len : (j + 1) * new_len] for m in part], axis=1)
            term = lax.dot_general(
                columns, wuv_ref[j], (((0,), (0,)), ((), ())), preferred_element_type=jnp.float32
            )
            total = term if total is None else total + term
        total = total.astype(jnp.bfloat16)
        for r in range(req):
            out_ref[r, :, j * head_v : (j + 1) * head_v] = total[r * new_len : (r + 1) * new_len]


def merge(got, own, mass, w_uv):
    groups, req, deep, _ = got.shape
    heads, lat, head_v = w_uv.shape
    group = heads // groups
    new_len = 128 // group
    return pl.pallas_call(
        merge_step,
        grid=(groups,),
        in_specs=[
            pl.BlockSpec((1, req, deep, 128), lambda g: (g, 0, 0, 0)),
            pl.BlockSpec((1, req, lat, 128), lambda g: (g, 0, 0, 0)),
            pl.BlockSpec((req, 1, 128), lambda g: (0, 0, g)),
            pl.BlockSpec((group, lat, head_v), lambda g: (g, 0, 0)),
        ],
        out_specs=pl.BlockSpec((req, new_len, group * head_v), lambda g: (0, 0, g)),
        out_shape=jax.ShapeDtypeStruct((req, new_len, heads * head_v), jnp.bfloat16),
        compiler_params=pltpu.CompilerParams(
            dimension_semantics=("arbitrary",), vmem_limit_bytes=VMEM_BYTES
        ),
        name="merge",
    )(got, own, mass, w_uv)


def partner_pairs(pool_count, dev_count, which):
    return [
        (pool * dev_count + dev, partners(pool, dev)[which] * dev_count + dev)
        for pool in range(pool_count)
        for dev in range(dev_count)
    ]


def on_device(
    hidden,
    query_latent_rows,
    store,
    w_down,
    kv_gain,
    query_up_weight,
    w_uk,
    w_uv,
    prefix_pages,
    page_owner,
    page_slot,
    decode_order,
):
    pool_count = lax.axis_size("pool")
    dev_count = lax.axis_size("dev")
    pool_index = lax.axis_index("pool")
    column = lax.axis_index("dev")
    req_col, quarter, model_width = hidden.shape
    new_len = quarter * pool_count
    lat_dim = kv_gain.shape[0]
    key_dim = w_down.shape[1]
    heads_local, nope_dim, _ = w_uk.shape
    rope_dim = key_dim - lat_dim
    page_len = store.shape[2]
    n_slots = store.shape[1]
    max_pages = page_owner.shape[1]
    list_len = req_col * max_pages
    first_row = column * req_col
    score_scale = (nope_dim + rope_dim) ** (-0.5)
    head_partner, key_partner = partners(pool_index, column)

    owner_t, slot_t = page_owner.T, page_slot.T
    page_of = jnp.arange(max_pages, dtype=jnp.int32)
    within = jnp.arange(prefix_pages.shape[0], dtype=jnp.int32) % req_col
    entry = within[None, :] * max_pages + page_of[:, None]
    used = page_of[:, None] < prefix_pages[None, :]
    mine = jnp.logical_and(owner_t == pool_index * dev_count + column, used)
    code = entry * n_slots + slot_t
    low = jnp.min(jnp.where(mine, code, list_len * n_slots), axis=0)
    high = jnp.max(jnp.where(mine, code, 0), axis=0)
    low = jnp.min(low.reshape(dev_count, req_col), axis=1)
    high = jnp.max(high.reshape(dev_count, req_col), axis=1)
    send_slots = (jnp.stack([low, high], axis=1) % n_slots).reshape(-1)

    prefix_mine = lax.dynamic_slice_in_dim(prefix_pages, first_row, req_col)
    frequency = jnp.exp(
        jnp.arange(rope_dim // 2, dtype=jnp.float32) * (-2.0 * jnp.log(50000.0) / rope_dim)
    )
    positions = prefix_mine[:, None] * page_len + jnp.arange(new_len, dtype=jnp.int32)[None, :]
    local_pos = (
        prefix_mine[:, None] * page_len
        + pool_index * quarter
        + jnp.arange(quarter, dtype=jnp.int32)[None, :]
    )
    angles = frequency[:, None] * positions.reshape(-1).astype(jnp.float32)[None, :]
    local_angles = frequency[:, None] * local_pos.reshape(-1).astype(jnp.float32)[None, :]

    near, far, passed, query, query_other, new_local, new_other = exchange(
        send_slots,
        query_latent_rows.reshape(req_col * quarter, -1),
        hidden.reshape(req_col * quarter, model_width),
        kv_gain[None, :],
        (jnp.cos(angles), jnp.sin(angles), jnp.cos(local_angles), jnp.sin(local_angles)),
        store[0],
        w_down.T,
        query_up_weight,
        w_uk,
        req_col,
    )
    axes = ("pool", "dev")
    passed_far = lax.ppermute(far, axes, partner_pairs(pool_count, dev_count, 1))

    own_t = lax.dynamic_slice_in_dim(owner_t, first_row, req_col, 1)
    own_used = page_of[:, None] < prefix_mine[None, :]
    own_entry = jnp.arange(req_col, dtype=jnp.int32)[None, :] * max_pages + page_of[:, None]
    senders = jnp.stack([shifted(column, offset, -1) for offset in OFFSETS])
    source = (
        jnp.stack([pool_index, key_partner])[:, None] * dev_count + senders[None, :]
    ).reshape(-1)
    hit = jnp.logical_and(own_t[None] == source[:, None, None], own_used[None])
    head_entry = jnp.min(jnp.where(hit, own_entry[None], list_len), axis=(1, 2))
    tail_entry = jnp.max(jnp.where(hit, own_entry[None], -1), axis=(1, 2))
    req_low = head_entry // max_pages
    req_high = jnp.where(tail_entry > head_entry, tail_entry // max_pages, req_col)
    slots = jnp.stack([req_low, req_high], axis=1).reshape(2, 2 * dev_count)
    cut = 2 * FORWARDED
    width = 4 * dev_count
    early = jnp.concatenate([slots[0, :cut], slots[1, :cut], slots[0, cut:]])
    listed = [early, slots[1, cut:], jnp.concatenate([early, slots[1, cut:]])]
    lists = jnp.stack(
        [jnp.concatenate([x, jnp.full((width - x.shape[0],), req_col, jnp.int32)]) for x in listed]
    )
    spot = jnp.arange(width, dtype=jnp.int32)
    rank_key = lists * width + spot
    rank = jnp.sum((rank_key[:, None, :] < rank_key[:, :, None]).astype(jnp.int32), axis=-1)
    order = jnp.sum(
        jnp.where(rank[:, None, :] == spot[None, :, None], spot[None, None, :], 0), axis=-1
    ).reshape(-1)
    start = jnp.sum(
        (lists[:, None, :] < jnp.arange(8, dtype=jnp.int32)[None, :, None]).astype(jnp.int32),
        axis=-1,
    ).reshape(-1)

    new_local = new_local.reshape(req_col, quarter, key_dim)
    new_other = new_other.reshape(req_col, quarter, key_dim)
    handed = new_local[lax.dynamic_slice_in_dim(decode_order, first_row, req_col) - first_row]
    new_keys = jnp.concatenate([new_local, new_other], axis=1)
    turn = jnp.arange(quarter, dtype=jnp.int32)
    new_pos = jnp.concatenate([pool_index * quarter + turn, key_partner * quarter + turn])
    new_pos = jnp.broadcast_to(new_pos[:, None], (2 * quarter, 128))

    common = dict(scale=score_scale, lat=lat_dim, new_len=new_len)
    early_blocks, new = [near, passed, far], (new_keys, new_pos)
    state = attend(0, order, start, early_blocks, query_other, new, "state", **common)
    part, part_mass = attend(
        1, order, start, [passed_far], query_other, state, "partner", **common
    )
    got = lax.ppermute(part, axes, partner_pairs(pool_count, dev_count, 0))
    order, part_mass = lax.optimization_barrier((order, part_mass))
    own, own_mass = attend(
        2, order, start, early_blocks + [passed_far], query, new, "own", **common
    )
    attended = merge(got, own, own_mass, w_uv)
    return (attended, handed)


def solution(mesh):
    in_specs = (
        P("dev", "pool", None),
        P("dev", "pool", None),
        P(("pool", "dev"), None, None, None),
        P(),
        P(),
        P(None, "pool"),
        P("pool", None, None),
        P("pool", None, None),
        P(),
        P(),
        P(),
        P(),
    )
    out_specs = (P("dev", None, "pool"), P("dev", "pool", None))
    return jax.shard_map(
        on_device, mesh=mesh, in_specs=in_specs, out_specs=out_specs, check_vma=False
    )
```

```python
import functools
import math

import jax
import jax.numpy as jnp
from jax import lax
from jax.experimental import pallas as pl
from jax.experimental.pallas import tpu as pltpu
from jax.sharding import PartitionSpec as P

TILE = 4
LOW = -1e30
FORWARDED = 21
VMEM_BYTES = 60 * 2**20
MESH = pl.DeviceIdType.MESH
STEPS = [
    (0, 1), (1, 0), (0, 3), (3, 0), (1, 1), (3, 3), (1, 3), (3, 1),
    (0, 2), (2, 0), (1, 2), (2, 1), (3, 2), (2, 3), (2, 2),
]
OFFSETS = [(0, 0, 0)] + [(z, x, 0) for z, x in STEPS] + [(0, 0, 1)] + [(z, x, 1) for z, x in STEPS]


def shifted(dev, offset, sign):
    core, x, z = dev % 2, (dev // 2) % 4, dev // 8
    dz, dx, dc = offset
    return ((z + sign * dz + 4) % 4 * 4 + (x + sign * dx + 4) % 4) * 2 + (core + dc) % 2


def partners(pool, dev):
    near = pool + 1 - 2 * (pool % 2)
    far = 3 - pool
    odd = dev % 2
    return near + odd * (far - near), far + odd * (near - far)


def list_pages(pool, dev, key_partner, owner_ref, table_ref, n_a):
    n_pairs = len(OFFSETS)
    width = 4 * n_pairs
    owners = owner_ref[...]
    entries = owners.shape[1]
    entry = lax.broadcasted_iota(jnp.int32, (1, entries), 1)
    pair = lax.broadcasted_iota(jnp.int32, (2 * n_pairs, 1), 0)
    source = jnp.zeros((2 * n_pairs, 1), jnp.int32)
    for j, offset in enumerate(OFFSETS):
        source = jnp.where(pair % n_pairs == j, shifted(dev, offset, -1), source)
    source = source + n_pairs * jnp.where(pair < n_pairs, pool, key_partner)
    hit = owners == source
    head = jnp.min(jnp.where(hit, entry, entries), axis=1, keepdims=True)
    tail = jnp.max(jnp.where(hit, entry, -1), axis=1, keepdims=True)
    nobody = entries // 64
    low = head // 64
    high = jnp.where(tail > head, tail // 64, nobody)
    request = jnp.concatenate([low, high], axis=0)
    place = lax.broadcasted_iota(jnp.int32, (width, 1), 0)
    late = place % (2 * n_pairs) >= n_pairs + n_a
    lane = lax.broadcasted_iota(jnp.int32, (1, width), 1)
    rows = []
    for wanted in (jnp.logical_not(late), late, None):
        mine = request if wanted is None else jnp.where(wanted, request, nobody)
        key = (mine * width + place).astype(jnp.float32)
        key = jnp.broadcast_to(key, (width, width))
        rank = jnp.sum((key.T < key).astype(jnp.float32), axis=1, keepdims=True).astype(jnp.int32)
        rows.append(jnp.sum(jnp.where(rank == lane, place, 0), axis=0, keepdims=True))
        rows.append(jnp.sum((mine < lane).astype(jnp.int32), axis=0, keepdims=True))
    for i, row in enumerate(rows):
        table_ref[i : i + 1, :] = row


def exchange_kernel(
    slot_ref, ql_ref, hidden_ref, gain_ref, owner_ref, cos_ref, sin_ref, lcos_ref, lsin_ref,
    store_ref, wd_ref, qup_ref, wuk_ref,
    arr_a, arr_b, pass_a, q_own, q_other, new_own, new_keys, table_ref,
    store_v, packed, ql_in, wd_v, qup_v, wuk_v, q_s, new_s, new_in, q_full,
    load_sem, ql_send, ql_recv, page_send, page_recv, pass_send, pass_recv, pair_send, pair_recv,
):
    pool, dev = lax.axis_index("pool"), lax.axis_index("dev")
    head_partner, key_partner = partners(pool, dev)
    req, key_dim, own_rows = q_s.shape
    heads, nope, lat = wuk_v.shape
    rope = key_dim - lat
    half_rope = rope // 2
    quarter = ql_in.shape[1] // req
    new_len = 4 * quarter
    page = store_v.shape[1]
    n_send = len(OFFSETS)
    n_a = arr_a.shape[0]

    load_store = pltpu.make_async_copy(store_ref, store_v, load_sem.at[6])
    load_store.start()
    loads = [
        pltpu.make_async_copy(wd_ref, wd_v, load_sem.at[0]),
        pltpu.make_async_copy(qup_ref, qup_v, load_sem.at[1]),
        pltpu.make_async_copy(wuk_ref, wuk_v, load_sem.at[2]),
    ]
    for copy in loads:
        copy.start()

    barrier = pltpu.get_barrier_semaphore()
    for offset in OFFSETS[1:]:
        pl.semaphore_signal(
            barrier, inc=1, device_id=(pool, shifted(dev, offset, 1)), device_id_type=MESH
        )
    for step in range(1, 4):
        pl.semaphore_signal(
            barrier, inc=1, device_id=((pool + step) % 4, dev), device_id_type=MESH
        )

    def pack(j):
        target = shifted(dev, OFFSETS[j], 1)
        pages = [store_v[slot_ref[2 * target + k]] for k in range(2)]
        for k in range(2):
            packed[j, k * page : (k + 1) * page, :] = pages[k][:, :lat]
        keys = jnp.concatenate([p[:, lat:] for p in pages], axis=1)
        step = page * 2 * rope // lat
        packed[j, 2 * page :, :] = jnp.concatenate(
            [keys[i * step : (i + 1) * step] for i in range(page // step)], axis=1
        )

    load_store.wait()
    pack(0)
    pack(1)
    pl.semaphore_wait(barrier, n_send - 1 + 3)

    def remote(src, dst, send, recv, target):
        return pltpu.make_async_remote_copy(
            src_ref=src, dst_ref=dst, send_sem=send, recv_sem=recv, device_id=target, device_id_type=MESH
        )

    ql_sends = [
        remote(ql_ref, ql_in.at[pool], ql_send.at[s - 1], ql_recv.at[s - 1], ((pool + s) % 4, dev))
        for s in range(1, 4)
    ]
    ql_gets = [
        remote(
            ql_ref, ql_in.at[(pool + 4 - s) % 4], ql_send.at[s - 1], ql_recv.at[s - 1], (head_partner, dev)
        )
        for s in range(1, 4)
    ]
    for copy in ql_sends:
        copy.start()

    def landing(j):
        return arr_a.at[j] if j < n_a else arr_b.at[j - n_a]

    passes = [
        remote(
            packed.at[0] if j == 0 else arr_a.at[j],
            pass_a.at[j],
            pass_send.at[j],
            pass_recv.at[j],
            (key_partner, dev),
        )
        for j in range(n_a)
    ]
    sends = [None]
    for j in range(1, n_send):
        if j > 1:
            pack(j)
        copy = remote(
            packed.at[j],
            landing(j),
            page_send.at[j],
            page_recv.at[j],
            (pool, shifted(dev, OFFSETS[j], 1)),
        )
        copy.start()
        sends.append(copy)
        if j == 1:
            passes[0].start()
    own_pages = pltpu.make_async_copy(packed.at[0], arr_a.at[0], load_sem.at[3])
    own_pages.start()

    def pass_on(first, last):
        for j in range(first, last):
            sends[j].wait_recv()
            if j < n_a:
                passes[j].start()

    loads[0].wait()
    projected = lax.dot_general(
        wd_v[...], hidden_ref[...], (((1,), (1,)), ((), ())), preferred_element_type=jnp.float32
    )
    latent = projected[:lat]
    latent = latent * lax.rsqrt(jnp.mean(latent * latent, axis=0, keepdims=True) + 1e-06)
    first, second = projected[lat : lat + half_rope], projected[lat + half_rope :]
    lcos, lsin = lcos_ref[...], lsin_ref[...]
    rotated = jnp.concatenate([first * lcos - second * lsin, first * lsin + second * lcos], axis=0)
    new_s[...] = jnp.concatenate(
        [latent.T * gain_ref[...].astype(jnp.float32)[None, :], rotated.T], axis=1
    ).astype(jnp.bfloat16)
    new_send = remote(new_s, new_in, pair_send.at[0], pair_recv.at[0], (key_partner, dev))
    new_send.start()
    new_keep = pltpu.make_async_copy(new_s, new_own, load_sem.at[4])
    new_keep.start()
    pass_on(1, 3)
    list_pages(pool, dev, key_partner, owner_ref, table_ref, n_a)

    ql_in[pool] = ql_ref[...]
    for copy in ql_gets:
        copy.wait_recv()
    for y in range(4):
        rows = ql_in[y].astype(jnp.float32)
        for r in range(req):
            q_full[pl.ds(r * new_len + y * quarter, quarter), :] = rows[
                r * quarter : (r + 1) * quarter
            ]
    for copy in loads[1:]:
        copy.wait()
    group = 128 // new_len
    width = nope + rope

    def project(g):
        raw = jnp.dot(
            q_full[...].astype(jnp.bfloat16),
            qup_v[:, g * group * width : (g + 1) * group * width],
            preferred_element_type=jnp.float32,
        ).T
        cos, sin = cos_ref[...], sin_ref[...]
        built = []
        for j in range(group):
            at = j * width
            q_nope = raw[at : at + nope].astype(jnp.bfloat16)
            q_abs = lax.dot_general(
                wuk_v[g * group + j],
                q_nope,
                (((0,), (0,)), ((), ())),
                preferred_element_type=jnp.float32,
            )
            x = raw[at + nope : at + nope + half_rope]
            y = raw[at + nope + half_rope : at + width]
            built.append(
                jnp.concatenate([q_abs, x * cos - y * sin, x * sin + y * cos], axis=0).astype(
                    jnp.bfloat16
                )
            )
        for r in range(req):
            q_s[r, :, g * 128 : (g + 1) * 128] = jnp.concatenate(
                [b[:, r * new_len : (r + 1) * new_len] for b in built], axis=1
            )

    done = 3
    for g in range(heads // group):
        project(g)
        if g < heads // group - 1:
            pass_on(done, done + 2)
            done += 2

    q_send = remote(q_s, q_other, pair_send.at[1], pair_recv.at[1], (head_partner, dev))
    q_send.start()
    q_keep = pltpu.make_async_copy(q_s, q_own, load_sem.at[5])
    q_keep.start()

    pass_on(done, n_send)
    for copy in ql_sends:
        copy.wait_send()
    for copy in sends[1:]:
        copy.wait_send()
    own_pages.wait()
    new_keep.wait()
    q_keep.wait()
    new_send.wait()
    own_new, got_new = new_s[...].astype(jnp.float32), new_in[...].astype(jnp.float32)
    for r in range(req):
        rows = slice(r * quarter, (r + 1) * quarter)
        new_keys[r] = jnp.concatenate([own_new[rows], got_new[rows]], axis=0).astype(jnp.bfloat16)
    q_send.wait()
    for copy in passes:
        copy.wait()


def exchange(slots, ql, hidden, gain, owners, angles, store, wd, qup, wuk, req):
    n_cols = slots.shape[0] // 2
    n_slots, page, key_dim = store.shape
    heads, nope, lat = wuk.shape
    tokens = ql.shape[0]
    new_len = 4 * tokens // req
    bf16 = jnp.bfloat16
    any_spec = pl.BlockSpec(memory_space=pl.ANY)
    vmem = pl.BlockSpec(memory_space=pltpu.VMEM)
    own_rows = heads * new_len
    pair = (2 * page * key_dim // lat, lat)
    query = jax.ShapeDtypeStruct((req, key_dim, own_rows), bf16)
    new = jax.ShapeDtypeStruct((tokens, key_dim), bf16)
    near = jax.ShapeDtypeStruct((FORWARDED,) + pair, bf16)
    far = jax.ShapeDtypeStruct((n_cols - FORWARDED,) + pair, bf16)
    dma = pltpu.SemaphoreType.DMA
    return pl.pallas_call(
        exchange_kernel,
        in_specs=[pl.BlockSpec(memory_space=pltpu.SMEM)] + [vmem] * 8 + [any_spec] * 4,
        out_specs=[any_spec] * 6 + [vmem] * 2,
        out_shape=[
            near,
            far,
            near,
            query,
            query,
            new,
            jax.ShapeDtypeStruct((req, 2 * tokens // req, key_dim), bf16),
            jax.ShapeDtypeStruct((8, 4 * n_cols), jnp.int32),
        ],
        scratch_shapes=[
            pltpu.VMEM(store.shape, bf16),
            pltpu.VMEM((n_cols,) + pair, bf16),
            pltpu.VMEM((4,) + ql.shape, bf16),
            pltpu.VMEM(wd.shape, bf16),
            pltpu.VMEM(qup.shape, bf16),
            pltpu.VMEM(wuk.shape, bf16),
            pltpu.VMEM(query.shape, bf16),
            pltpu.VMEM(new.shape, bf16),
            pltpu.VMEM(new.shape, bf16),
            pltpu.VMEM((req * new_len, ql.shape[1]), jnp.float32),
            dma((7,)),
            dma((3,)),
            dma((3,)),
            dma((n_cols,)),
            dma((n_cols,)),
            dma((FORWARDED,)),
            dma((FORWARDED,)),
            dma((2,)),
            dma((2,)),
        ],
        compiler_params=pltpu.CompilerParams(
            collective_id=1, has_side_effects=True, vmem_limit_bytes=VMEM_BYTES
        ),
        cost_estimate=pl.CostEstimate(flops=10**10, bytes_accessed=10**8, transcendentals=0),
        name="exchange",
    )(slots, ql, hidden, gain, owners, *angles, store, wd, qup, wuk)


def up_project(columns, weights):
    return lax.dot_general(
        columns, weights, (((0,), (0,)), ((), ())), preferred_element_type=jnp.float32
    )


def attention_step(table_ref, *refs, call, sizes, base, first, kind, scale, page, new_len):
    n_blocks = len(sizes)
    blocks, refs = refs[:n_blocks], refs[n_blocks:]
    q_ref, refs = refs[0], refs[1:]
    inputs, refs = refs[:2], refs[2:]
    if kind == "own":
        wuv_ref, refs = refs[0], refs[1:]
    result, mass, refs = refs[0], refs[1], refs[2:]
    pairs, sem, even, odd = refs[:4]
    acc = result.at[0] if kind == "state" else refs[4]
    lat, rows = acc.shape
    request = pl.program_id(0)

    @pl.when(request == 0)
    def _():
        copies, at = [], 0
        for i, block in enumerate(blocks):
            copies.append(pltpu.make_async_copy(block, pairs.at[pl.ds(at, sizes[i])], sem.at[i]))
            at += sizes[i]
        for copy in copies:
            copy.start()
        for copy in copies:
            copy.wait()

    factor = scale * math.log2(math.e)
    rope = q_ref.shape[1] - lat
    pad = 128 - rope
    bias_rows = jnp.where(
        lax.broadcasted_iota(jnp.int32, (pad, rows), 0) == 0, 1.0, 0.0
    ).astype(jnp.bfloat16)
    key_lane = lax.broadcasted_iota(jnp.int32, (page, pad), 1)

    def weigh(keys, weights):
        return lax.dot_general(
            keys[:, :lat], weights, (((0,), (0,)), ((), ())), preferred_element_type=jnp.float32
        )

    if first:
        new_ref, new_pos_ref = inputs
        new_keys = new_ref[0]
        score = jnp.dot(new_keys, q_ref[0], preferred_element_type=jnp.float32)
        token = lax.broadcasted_iota(jnp.int32, score.shape, 1) % new_len
        live = new_pos_ref[:, :1] <= token
        score = jnp.where(live, score, LOW)
        top = jnp.max(score, axis=0, keepdims=True)
        weights = jnp.where(live, jnp.exp2((score - top) * factor), 0.0)
        total = jnp.sum(weights, axis=0, keepdims=True)
        acc[...] = weigh(new_keys, weights.astype(jnp.bfloat16))
    else:
        acc_in, mass_in = inputs
        top, total = mass_in[0, 0:1, :], mass_in[0, 1:2, :]
        acc[...] = acc_in[0]

    begin = table_ref[2 * call + 1, request]
    end = table_ref[2 * call + 1, request + 1]
    tiles = (end - begin + TILE - 1) // TILE

    def keys_of(tile):
        parts = []
        for g in range(TILE):
            spot = begin + tile * TILE + g
            index = table_ref[2 * call, jnp.maximum(jnp.minimum(spot, end - 1), 0)]
            half = table_ref.shape[1] // 2
            pair, turn = index % half - base, index // half
            latent = pairs[pair, pl.ds(pl.multiple_of(turn * page, page), page), :]
            both = pairs[pair, pl.ds(2 * page, 2 * page * rope // lat), :]
            both = jnp.concatenate([both[:, i * 128 : (i + 1) * 128] for i in range(lat // 128)], axis=0)
            rotary = jnp.where(turn == 0, both[:, :rope], both[:, rope:])
            bias = jnp.where((key_lane == 0) & (spot >= end), LOW, 0.0).astype(jnp.bfloat16)
            parts.append(jnp.concatenate([latent, rotary, bias], axis=1))
        return jnp.concatenate(parts, axis=0)

    def scores_of(keys):
        query = jnp.concatenate([q_ref[0], bias_rows], axis=0)
        return jnp.dot(keys, query, preferred_element_type=jnp.float32)

    def take(sheet, keys, top, total):
        score = sheet[...]
        new_top = jnp.maximum(top, jnp.max(score, axis=0, keepdims=True))
        shrink = jnp.exp2((top - new_top) * factor)
        weights = jnp.exp2((score - new_top) * factor)
        total = total * shrink + jnp.sum(weights, axis=0, keepdims=True)
        acc[...] = acc[...] * shrink + weigh(keys, weights.astype(jnp.bfloat16))
        return new_top, total

    @pl.when(tiles > 0)
    def _():
        even[...] = scores_of(keys_of(0))

    def body(step, carry):
        tile = 2 * step
        later = keys_of(tile + 1)
        odd[...] = scores_of(later)
        carry = take(even, keys_of(tile), *carry)
        even[...] = scores_of(keys_of(jnp.minimum(tile + 2, tiles - 1)))
        return take(odd, later, *carry)

    carry = lax.fori_loop(0, tiles // 2, body, (top, total))
    top, total = lax.cond(
        tiles % 2 == 1,
        lambda c: take(even, keys_of(tiles - 1), *c),
        lambda c: c,
        carry,
    )

    if kind == "state":
        mass[0, 0:1, :] = top
        mass[0, 1:2, :] = total
        return
    live = total > 0
    inverse = jnp.where(live, 1.0 / total, 0.0)
    log_mass = jnp.where(live, top * factor + jnp.log(total) * math.log2(math.e), LOW)
    mass[request] = log_mass
    groups = rows // 128
    for g in range(groups):
        lanes = slice(g * 128, (g + 1) * 128)
        mixed = acc[:, lanes] * inverse[:, lanes]
        if kind == "own":
            high_v, low_v = refs[5], refs[6]
            high = mixed.astype(jnp.bfloat16)
            high_v[request, :, lanes] = high
            low_v[request, :, lanes] = (mixed - high.astype(jnp.float32)).astype(jnp.bfloat16)
        else:
            result[g, 0, :lat, :] = mixed.astype(jnp.bfloat16)
            high = log_mass[:, lanes].astype(jnp.bfloat16)
            rest = log_mass[:, lanes] - high.astype(jnp.float32)
            middle = rest.astype(jnp.bfloat16)
            low = (rest - middle.astype(jnp.float32)).astype(jnp.bfloat16)
            row = lax.broadcasted_iota(jnp.int32, (16, 128), 0)
            terms = [t.astype(jnp.float32) for t in (high, middle, low)]
            result[g, 0, lat:, :] = jnp.where(
                row == 0, terms[0], jnp.where(row == 1, terms[1], jnp.where(row == 2, terms[2], 0.0))
            ).astype(jnp.bfloat16)
    if kind == "own":

        @pl.when(request == pl.num_programs(0) - 1)
        def _():
            req = high_v.shape[0]
            head_v = wuv_ref.shape[2]
            for head in range(wuv_ref.shape[0]):
                cols = slice(head * new_len, (head + 1) * new_len)
                total = None
                for part in (high_v, low_v):
                    rows_of = jnp.concatenate([part[r, :, cols] for r in range(req)], axis=1)
                    term = up_project(rows_of, wuv_ref[head])
                    total = term if total is None else total + term
                for r in range(req):
                    result[r, :, head * head_v : (head + 1) * head_v] = total[
                        r * new_len : (r + 1) * new_len
                    ]


def attend(call, table, base, blocks, query, inputs, kind, scale, lat, new_len, w_uv=None, vmem=VMEM_BYTES):
    first = inputs[0].dtype == jnp.bfloat16
    req, key_dim, rows = query.shape
    sizes = [b.shape[0] for b in blocks]
    count = sum(sizes)
    page = blocks[0].shape[1] * lat // key_dim // 2
    groups = rows // 128
    kernel = functools.partial(
        attention_step, call=call, sizes=sizes, base=base, first=first, kind=kind, scale=scale, page=page, new_len=new_len
    )
    acc_spec = pl.BlockSpec((1, lat, rows), lambda r, *_: (r, 0, 0))
    mass_spec = pl.BlockSpec((1, 2, rows), lambda r, *_: (r, 0, 0))
    in_specs = [pl.BlockSpec(memory_space=pl.ANY)] * len(blocks)
    in_specs += [pl.BlockSpec((1, key_dim, rows), lambda r, *_: (r, 0, 0))]
    if first:
        in_specs += [
            pl.BlockSpec((1,) + inputs[0].shape[1:], lambda r, *_: (r, 0, 0)),
            pl.BlockSpec(inputs[1].shape, lambda r, *_: (0, 0)),
        ]
    else:
        in_specs += [acc_spec, mass_spec]
    scratch = [
        pltpu.VMEM((count,) + blocks[0].shape[1:], jnp.bfloat16),
        pltpu.SemaphoreType.DMA((len(blocks),)),
        pltpu.VMEM((TILE * page, rows), jnp.float32),
        pltpu.VMEM((TILE * page, rows), jnp.float32),
    ]
    if kind == "state":
        out_specs = [acc_spec, mass_spec]
        out_shape = [
            jax.ShapeDtypeStruct((req, lat, rows), jnp.float32),
            jax.ShapeDtypeStruct((req, 2, rows), jnp.float32),
        ]
    else:
        scratch.append(pltpu.VMEM((lat, rows), jnp.float32))
        out_specs = [None, pl.BlockSpec((req, 1, rows), lambda r, *_: (0, 0, 0))]
        out_shape = [None, jax.ShapeDtypeStruct((req, 1, rows), jnp.float32)]
        if kind == "partner":
            out_specs[0] = pl.BlockSpec((groups, 1, lat + 16, 128), lambda r, *_: (0, r, 0, 0))
            out_shape[0] = jax.ShapeDtypeStruct((groups, req, lat + 16, 128), jnp.bfloat16)
        else:
            heads, _, head_v = w_uv.shape
            in_specs.append(pl.BlockSpec(w_uv.shape, lambda r, *_: (0, 0, 0)))
            scratch += [pltpu.VMEM((req, lat, rows), jnp.bfloat16)] * 2
            out_specs[0] = pl.BlockSpec((req, new_len, heads * head_v), lambda r, *_: (0, 0, 0))
            out_shape[0] = jax.ShapeDtypeStruct((req, new_len, heads * head_v), jnp.float32)
    more = [w_uv] if kind == "own" else []
    return pl.pallas_call(
        kernel,
        grid_spec=pltpu.PrefetchScalarGridSpec(
            num_scalar_prefetch=1,
            grid=(req,),
            in_specs=in_specs,
            out_specs=out_specs,
            scratch_shapes=scratch,
        ),
        out_shape=out_shape,
        compiler_params=pltpu.CompilerParams(
            dimension_semantics=("arbitrary",), vmem_limit_bytes=vmem
        ),
        cost_estimate=pl.CostEstimate(
            flops=8 * rows * count * page * (key_dim + lat),
            bytes_accessed=4 * req * lat * rows * 2 + count * page * key_dim * 2,
            transcendentals=2 * rows * count * page,
        ),
        name=f"attend_{call}_{kind}",
    )(table, *blocks, query, *inputs, *more)


def merge_step(turn_ref, got_ref, own_ref, mass_ref, wuv_ref, new_ref, out_ref, handed_ref):
    _, req, deep, _ = got_ref.shape
    group, lat, head_v = wuv_ref.shape
    new_len = 128 // group

    @pl.when(pl.program_id(0) == 0)
    def _():
        for i in range(req):
            handed_ref[i] = new_ref[turn_ref[i]]

    shares = []
    for r in range(req):
        tail = got_ref[0, r, lat:, :].astype(jnp.float32)
        got_mass = tail[0:1] + tail[1:2] + tail[2:3]
        share = 1.0 / (1.0 + jnp.exp2(mass_ref[r] - got_mass))
        shares.append(jnp.broadcast_to(share, (128, 128)).T)
    for j in range(group):
        rows = slice(j * new_len, (j + 1) * new_len)
        columns = jnp.concatenate([got_ref[0, r, :lat, rows] for r in range(req)], axis=1)
        got = up_project(columns, wuv_ref[j])
        for r in range(req):
            share = shares[r][rows]
            lanes = slice(j * head_v, (j + 1) * head_v)
            own = own_ref[r, :, lanes]
            out_ref[r, :, lanes] = (
                own * (1.0 - share) + got[r * new_len : (r + 1) * new_len] * share
            ).astype(jnp.bfloat16)


def merge(turns, got, own, mass, w_uv, new_rows):
    groups, req, deep, _ = got.shape
    heads, lat, head_v = w_uv.shape
    group = heads // groups
    new_len = 128 // group
    wide = pl.BlockSpec((req, new_len, group * head_v), lambda g, *_: (0, 0, g))
    whole = pl.BlockSpec(new_rows.shape, lambda g, *_: (0, 0, 0))
    return pl.pallas_call(
        merge_step,
        grid_spec=pltpu.PrefetchScalarGridSpec(
            num_scalar_prefetch=1,
            grid=(groups,),
            in_specs=[
                pl.BlockSpec((1, req, deep, 128), lambda g, *_: (g, 0, 0, 0)),
                wide,
                pl.BlockSpec((req, 1, 128), lambda g, *_: (0, 0, g)),
                pl.BlockSpec((group, lat, head_v), lambda g, *_: (g, 0, 0)),
                whole,
            ],
            out_specs=[wide, whole],
        ),
        out_shape=[
            jax.ShapeDtypeStruct((req, new_len, heads * head_v), jnp.bfloat16),
            jax.ShapeDtypeStruct(new_rows.shape, jnp.bfloat16),
        ],
        compiler_params=pltpu.CompilerParams(
            dimension_semantics=("arbitrary",), vmem_limit_bytes=24 * 2**20
        ),
        name="merge",
    )(turns, got, own, mass, w_uv, new_rows)


def partner_pairs(pool_count, dev_count, which):
    return [
        (pool * dev_count + dev, partners(pool, dev)[which] * dev_count + dev)
        for pool in range(pool_count)
        for dev in range(dev_count)
    ]


def on_device(
    hidden,
    query_latent_rows,
    store,
    w_down,
    kv_gain,
    query_up_weight,
    w_uk,
    w_uv,
    prefix_pages,
    page_owner,
    page_slot,
    decode_order,
):
    pool_count = lax.axis_size("pool")
    dev_count = lax.axis_size("dev")
    pool_index = lax.axis_index("pool")
    column = lax.axis_index("dev")
    req_col, quarter, model_width = hidden.shape
    new_len = quarter * pool_count
    lat_dim = kv_gain.shape[0]
    key_dim = w_down.shape[1]
    heads_local, nope_dim, _ = w_uk.shape
    rope_dim = key_dim - lat_dim
    page_len = store.shape[2]
    n_slots = store.shape[1]
    max_pages = page_owner.shape[1]
    list_len = req_col * max_pages
    first_row = column * req_col
    score_scale = (nope_dim + rope_dim) ** (-0.5)
    head_partner, key_partner = partners(pool_index, column)

    owner_t, slot_t = page_owner.T, page_slot.T
    page_of = jnp.arange(max_pages, dtype=jnp.int32)
    within = jnp.arange(prefix_pages.shape[0], dtype=jnp.int32) % req_col
    entry = within[None, :] * max_pages + page_of[:, None]
    used = page_of[:, None] < prefix_pages[None, :]
    mine = jnp.logical_and(owner_t == pool_index * dev_count + column, used)
    code = entry * n_slots + slot_t
    low = jnp.min(jnp.where(mine, code, list_len * n_slots), axis=0)
    high = jnp.max(jnp.where(mine, code, 0), axis=0)
    low = jnp.min(low.reshape(dev_count, req_col), axis=1)
    high = jnp.max(high.reshape(dev_count, req_col), axis=1)
    send_slots = (jnp.stack([low, high], axis=1) % n_slots).reshape(-1)

    prefix_mine = lax.dynamic_slice_in_dim(prefix_pages, first_row, req_col)
    frequency = jnp.exp(
        jnp.arange(rope_dim // 2, dtype=jnp.float32) * (-2.0 * jnp.log(50000.0) / rope_dim)
    )
    positions = prefix_mine[:, None] * page_len + jnp.arange(new_len, dtype=jnp.int32)[None, :]
    local_pos = (
        prefix_mine[:, None] * page_len
        + pool_index * quarter
        + jnp.arange(quarter, dtype=jnp.int32)[None, :]
    )
    angles = frequency[:, None] * positions.reshape(-1).astype(jnp.float32)[None, :]
    local_angles = frequency[:, None] * local_pos.reshape(-1).astype(jnp.float32)[None, :]

    own_rows = lax.dynamic_slice_in_dim(page_owner, first_row, req_col)
    own_rows = jnp.where(page_of[None, :] < prefix_mine[:, None], own_rows, -1)

    near, far, passed, query, query_other, new_local, new_keys, table = exchange(
        send_slots,
        query_latent_rows.reshape(req_col * quarter, -1),
        hidden.reshape(req_col * quarter, model_width),
        kv_gain,
        own_rows.reshape(1, list_len),
        (jnp.cos(angles), jnp.sin(angles), jnp.cos(local_angles), jnp.sin(local_angles)),
        store[0],
        w_down.T,
        query_up_weight,
        w_uk,
        req_col,
    )
    axes = ("pool", "dev")
    passed_far = lax.ppermute(far, axes, partner_pairs(pool_count, dev_count, 1))

    turn = jnp.arange(quarter, dtype=jnp.int32)
    new_pos = jnp.concatenate([pool_index * quarter + turn, key_partner * quarter + turn])
    new = (new_keys, jnp.broadcast_to(new_pos[:, None], (2 * quarter, 128)))
    common = dict(scale=score_scale, lat=lat_dim, new_len=new_len)
    early_blocks = [near, far, passed]
    state = attend(0, table, 0, early_blocks, query_other, new, "state", **common)
    part, part_mass = attend(
        1,
        table,
        dev_count + FORWARDED,
        [passed_far],
        query_other,
        state,
        "partner",
        vmem=32 * 2**20,
        **common,
    )
    got = lax.ppermute(part, axes, partner_pairs(pool_count, dev_count, 0))
    table, part_mass = lax.optimization_barrier((table, part_mass))
    own, own_mass = attend(
        2, table, 0, early_blocks + [passed_far], query, new, "own", w_uv=w_uv, **common
    )
    turns = lax.dynamic_slice_in_dim(decode_order, first_row, req_col) - first_row
    attended, handed = merge(
        turns, got, own, own_mass, w_uv, new_local.reshape(req_col, quarter, key_dim)
    )
    return (attended, handed)


def solution(mesh):
    in_specs = (
        P("dev", "pool", None),
        P("dev", "pool", None),
        P(("pool", "dev"), None, None, None),
        P(),
        P(),
        P(None, "pool"),
        P("pool", None, None),
        P("pool", None, None),
        P(),
        P(),
        P(),
        P(),
    )
    out_specs = (P("dev", None, "pool"), P("dev", "pool", None))
    return jax.shard_map(
        on_device, mesh=mesh, in_specs=in_specs, out_specs=out_specs, check_vma=False
    )
```

```python
import functools
import math

import jax
import jax.numpy as jnp
import numpy as np
from jax import lax
from jax.experimental import pallas as pl
from jax.experimental.pallas import tpu as pltpu
from jax.sharding import PartitionSpec as P

TILE = 4
LOW = -1e30
FORWARDED = 24
DIRECT = 3
VMEM_BYTES = 60 * 2**20
MESH = pl.DeviceIdType.MESH
STEPS = [
    (0, 1), (1, 0), (0, 3), (3, 0), (1, 1), (3, 3), (1, 3), (3, 1),
    (0, 2), (2, 0), (1, 2), (2, 1), (3, 2), (2, 3), (2, 2),
]
OFFSETS = [(0, 0, 0)] + [(z, x, 0) for z, x in STEPS] + [(0, 0, 1)] + [(z, x, 1) for z, x in STEPS]


def shifted(dev, offset, sign):
    core, x, z = dev % 2, (dev // 2) % 4, dev // 8
    dz, dx, dc = offset
    return ((z + sign * dz + 4) % 4 * 4 + (x + sign * dx + 4) % 4) * 2 + (core + dc) % 2


def partners(pool, dev):
    near = pool + 1 - 2 * (pool % 2)
    far = 3 - pool
    odd = dev % 2
    return near + odd * (far - near), far + odd * (near - far)


def list_pages(pool, dev, key_partner, owners, table_ref, n_a, quarter):
    n_pairs = len(OFFSETS)
    width = 4 * n_pairs
    entries = owners.shape[1]
    entry = lax.broadcasted_iota(jnp.int32, (1, entries), 1)
    pair = lax.broadcasted_iota(jnp.int32, (2 * n_pairs, 1), 0)
    source = jnp.zeros((2 * n_pairs, 1), jnp.int32)
    for j, offset in enumerate(OFFSETS):
        source = jnp.where(pair % n_pairs == j, shifted(dev, offset, -1), source)
    source = source + n_pairs * jnp.where(pair < n_pairs, pool, key_partner)
    hit = owners == source
    head = jnp.min(jnp.where(hit, entry, entries), axis=1, keepdims=True)
    tail = jnp.max(jnp.where(hit, entry, -1), axis=1, keepdims=True)
    nobody = entries // 64
    low = head // 64
    high = jnp.where(tail > head, tail // 64, nobody)
    request = jnp.concatenate([low, high], axis=0)
    place = lax.broadcasted_iota(jnp.int32, (width, 1), 0)
    late = place % (2 * n_pairs) >= n_pairs + n_a
    lane = lax.broadcasted_iota(jnp.int32, (1, width), 1)
    rows = []
    for wanted in (jnp.logical_not(late), late, None):
        mine = request if wanted is None else jnp.where(wanted, request, nobody)
        key = (mine * width + place).astype(jnp.float32)
        key = jnp.broadcast_to(key, (width, width))
        rank = jnp.sum((key.T < key).astype(jnp.float32), axis=1, keepdims=True).astype(jnp.int32)
        rows.append(jnp.sum(jnp.where(rank == lane, place, 0), axis=0, keepdims=True))
        rows.append(jnp.sum((mine < lane).astype(jnp.int32), axis=0, keepdims=True))
    rows.append(
        jnp.where(lane < quarter, pool * quarter + lane, key_partner * quarter + lane - quarter)
    )
    for i, row in enumerate(rows):
        table_ref[i : i + 1, :] = row


def exchange_kernel(
    prefix_ref, ql_ref, hidden_ref, gain_ref, prefix_row, owner_ref, slot_ref, frequency_ref,
    store_ref, wd_ref, qup_ref, wuk_ref,
    arr_a, arr_b, pass_a, q_own, q_other, new_own, new_keys, table_ref,
    store_v, packed, ql_in, wd_v, qup_v, wuk_v, q_s, new_s, new_in, q_full, picks_v, picks,
    load_sem, ql_send, ql_recv, page_send, page_recv, pass_send, pass_recv, pair_send, pair_recv,
):
    pool, dev = lax.axis_index("pool"), lax.axis_index("dev")
    head_partner, key_partner = partners(pool, dev)
    req, key_dim, own_rows = q_s.shape
    heads, nope, lat = wuk_v.shape
    rope = key_dim - lat
    half_rope = rope // 2
    quarter = ql_in.shape[1] // req
    new_len = 4 * quarter
    page = store_v.shape[1]
    n_send = len(OFFSETS)
    n_a = arr_a.shape[0]

    load_store = pltpu.make_async_copy(store_ref, store_v, load_sem.at[6])
    load_store.start()
    loads = [
        pltpu.make_async_copy(wd_ref, wd_v, load_sem.at[0]),
        pltpu.make_async_copy(qup_ref, qup_v, load_sem.at[1]),
        pltpu.make_async_copy(wuk_ref, wuk_v, load_sem.at[2]),
    ]
    for copy in loads:
        copy.start()

    n_relay = n_a - DIRECT
    direct = range(n_relay, n_a)

    def direct_target(j):
        column = shifted(dev, OFFSETS[j], 1)
        return partners(pool, column)[1], column

    barrier = pltpu.get_barrier_semaphore()
    for offset in OFFSETS[1:]:
        pl.semaphore_signal(
            barrier, inc=1, device_id=(pool, shifted(dev, offset, 1)), device_id_type=MESH
        )
    for j in direct:
        for peer in (direct_target(j), (key_partner, shifted(dev, OFFSETS[j], -1))):
            pl.semaphore_signal(barrier, inc=1, device_id=peer, device_id_type=MESH)
    for step in range(1, 4):
        pl.semaphore_signal(
            barrier, inc=1, device_id=((pool + step) % 4, dev), device_id_type=MESH
        )

    prefix = prefix_row[...][None, :]
    owners = owner_ref[...]
    page_of = lax.broadcasted_iota(jnp.int32, owners.shape, 0)
    lane_of = lax.broadcasted_iota(jnp.int32, owners.shape, 1)
    n_slots, max_pages = store_v.shape[0], owners.shape[0]
    used = page_of < prefix
    mine = used & (owners == pool * n_send + dev)
    code = (lane_of % req * max_pages + page_of) * n_slots + slot_ref[...]
    low = jnp.min(jnp.where(mine, code, req * max_pages * n_slots), axis=0, keepdims=True)
    high = jnp.max(jnp.where(mine, code, 0), axis=0, keepdims=True)
    n_lanes = owners.shape[1]
    for step in (1, 2):
        low = jnp.minimum(low, pltpu.roll(low, n_lanes - step, 1))
        high = jnp.maximum(high, pltpu.roll(high, n_lanes - step, 1))
    picks_v[0:1, :] = low % n_slots
    picks_v[1:2, :] = high % n_slots
    load_picks = pltpu.make_async_copy(picks_v, picks, load_sem.at[7])
    load_picks.start()

    def pack(j):
        target = shifted(dev, OFFSETS[j], 1)
        pages = [store_v[picks[k, req * target]] for k in range(2)]
        for k in range(2):
            packed[j, k * page : (k + 1) * page, :] = pages[k][:, :lat]
        keys = jnp.concatenate([p[:, lat:] for p in pages], axis=1)
        step = page * 2 * rope // lat
        packed[j, 2 * page :, :] = jnp.concatenate(
            [keys[i * step : (i + 1) * step] for i in range(page // step)], axis=1
        )

    load_picks.wait()
    load_store.wait()
    for j in (0, 1, *direct):
        pack(j)
    pl.semaphore_wait(barrier, n_send - 1 + 3 + 2 * DIRECT)

    def remote(src, dst, send, recv, target):
        return pltpu.make_async_remote_copy(
            src_ref=src, dst_ref=dst, send_sem=send, recv_sem=recv, device_id=target, device_id_type=MESH
        )

    ql_sends = [
        remote(ql_ref, ql_in.at[pool], ql_send.at[s - 1], ql_recv.at[s - 1], ((pool + s) % 4, dev))
        for s in range(1, 4)
    ]
    ql_gets = [
        remote(
            ql_ref, ql_in.at[(pool + 4 - s) % 4], ql_send.at[s - 1], ql_recv.at[s - 1], (head_partner, dev)
        )
        for s in range(1, 4)
    ]
    for copy in ql_sends:
        copy.start()

    def landing(j):
        return arr_a.at[j] if j < n_a else arr_b.at[j - n_a]

    passes = [
        remote(
            packed.at[j] if j == 0 or j in direct else arr_a.at[j],
            pass_a.at[j],
            pass_send.at[j],
            pass_recv.at[j],
            direct_target(j) if j in direct else (key_partner, dev),
        )
        for j in range(n_a)
    ]
    sends = [None] * n_send
    for j in (*range(1, n_relay), *range(n_a, n_send), *direct):
        if j > 1 and j not in direct:
            pack(j)
        copy = remote(
            packed.at[j],
            landing(j),
            page_send.at[j],
            page_recv.at[j],
            (pool, shifted(dev, OFFSETS[j], 1)),
        )
        copy.start()
        sends[j] = copy
        if j == 1:
            for early in (0, *direct):
                passes[early].start()
    own_pages = pltpu.make_async_copy(packed.at[0], arr_a.at[0], load_sem.at[3])
    own_pages.start()

    def pass_on(first, last):
        for j in range(first, last):
            sends[j].wait_recv()
            if j < n_relay:
                passes[j].start()

    pass_on(1, 2)
    frequency = frequency_ref[...]
    lane = lax.broadcasted_iota(jnp.int32, (1, frequency.shape[1]), 1)
    position = pool * quarter + lane % quarter
    local_position = position
    position = lane % new_len
    for r in range(req):
        begin = prefix_ref[req * dev + r] * page
        local_position = local_position + jnp.where(lane // quarter == r, begin, 0)
        position = position + jnp.where(lane // new_len == r, begin, 0)
    local_angles = (frequency * local_position.astype(jnp.float32))[:, : req * quarter]
    angles = frequency * position.astype(jnp.float32)

    loads[0].wait()
    projected = lax.dot_general(
        wd_v[...], hidden_ref[...], (((1,), (1,)), ((), ())), preferred_element_type=jnp.float32
    )
    latent = projected[:lat]
    latent = latent * lax.rsqrt(jnp.mean(latent * latent, axis=0, keepdims=True) + 1e-06)
    first, second = projected[lat : lat + half_rope], projected[lat + half_rope :]
    lcos, lsin = jnp.cos(local_angles), jnp.sin(local_angles)
    rotated = jnp.concatenate([first * lcos - second * lsin, first * lsin + second * lcos], axis=0)
    new_s[...] = jnp.concatenate(
        [latent.T * gain_ref[...].astype(jnp.float32)[None, :], rotated.T], axis=1
    ).astype(jnp.bfloat16)
    new_send = remote(new_s, new_in, pair_send.at[0], pair_recv.at[0], (key_partner, dev))
    new_send.start()
    new_keep = pltpu.make_async_copy(new_s, new_own, load_sem.at[4])
    new_keep.start()
    pass_on(2, 4)
    own = jnp.where(used, owners, -1).astype(jnp.float32)
    own = pltpu.roll(own, (n_lanes - req * dev) % n_lanes, 1)
    own = jnp.concatenate([own, jnp.zeros((n_lanes - max_pages, n_lanes), jnp.float32)], axis=0).T
    own = jnp.concatenate([own[r : r + 1, :max_pages] for r in range(req)], axis=1)
    list_pages(pool, dev, key_partner, own.astype(jnp.int32), table_ref, n_a, quarter)

    ql_in[pool] = ql_ref[...]
    for copy in ql_gets:
        copy.wait_recv()
    for y in range(4):
        rows = ql_in[y].astype(jnp.float32)
        for r in range(req):
            q_full[pl.ds(r * new_len + y * quarter, quarter), :] = rows[
                r * quarter : (r + 1) * quarter
            ]
    for copy in loads[1:]:
        copy.wait()
    group = 128 // new_len
    width = nope + rope

    cos, sin = jnp.cos(angles), jnp.sin(angles)

    def project(g):
        raw = jnp.dot(
            q_full[...].astype(jnp.bfloat16),
            qup_v[:, g * group * width : (g + 1) * group * width],
            preferred_element_type=jnp.float32,
        ).T
        built = []
        for j in range(group):
            at = j * width
            q_nope = raw[at : at + nope].astype(jnp.bfloat16)
            q_abs = lax.dot_general(
                wuk_v[g * group + j],
                q_nope,
                (((0,), (0,)), ((), ())),
                preferred_element_type=jnp.float32,
            )
            x = raw[at + nope : at + nope + half_rope]
            y = raw[at + nope + half_rope : at + width]
            built.append(
                jnp.concatenate([q_abs, x * cos - y * sin, x * sin + y * cos], axis=0).astype(
                    jnp.bfloat16
                )
            )
        for r in range(req):
            q_s[r, :, g * 128 : (g + 1) * 128] = jnp.concatenate(
                [b[:, r * new_len : (r + 1) * new_len] for b in built], axis=1
            )

    done = 4
    for g in range(heads // group):
        project(g)
        if g < heads // group - 1:
            pass_on(done, done + 2)
            done += 2

    q_send = remote(q_s, q_other, pair_send.at[1], pair_recv.at[1], (head_partner, dev))
    q_send.start()
    q_keep = pltpu.make_async_copy(q_s, q_own, load_sem.at[5])
    q_keep.start()

    pass_on(done, n_send)
    for copy in ql_sends:
        copy.wait_send()
    for copy in sends[1:]:
        copy.wait_send()
    own_pages.wait()
    new_keep.wait()
    q_keep.wait()
    new_send.wait()
    own_new, got_new = new_s[...].astype(jnp.float32), new_in[...].astype(jnp.float32)
    for r in range(req):
        rows = slice(r * quarter, (r + 1) * quarter)
        new_keys[r] = jnp.concatenate([own_new[rows], got_new[rows]], axis=0).astype(jnp.bfloat16)
    q_send.wait()
    for copy in passes:
        copy.wait()


def exchange(prefix, ql, hidden, gain, owner_t, slot_t, frequency, store, wd, qup, wuk, req):
    n_cols = prefix.shape[0] // req
    n_slots, page, key_dim = store.shape
    heads, nope, lat = wuk.shape
    tokens = ql.shape[0]
    new_len = 4 * tokens // req
    bf16 = jnp.bfloat16
    any_spec = pl.BlockSpec(memory_space=pl.ANY)
    vmem = pl.BlockSpec(memory_space=pltpu.VMEM)
    own_rows = heads * new_len
    pair = (2 * page * key_dim // lat, lat)
    query = jax.ShapeDtypeStruct((req, key_dim, own_rows), bf16)
    new = jax.ShapeDtypeStruct((tokens, key_dim), bf16)
    near = jax.ShapeDtypeStruct((FORWARDED,) + pair, bf16)
    far = jax.ShapeDtypeStruct((n_cols - FORWARDED,) + pair, bf16)
    dma = pltpu.SemaphoreType.DMA
    return pl.pallas_call(
        exchange_kernel,
        in_specs=[pl.BlockSpec(memory_space=pltpu.SMEM)] + [vmem] * 7 + [any_spec] * 4,
        out_specs=[any_spec] * 6 + [vmem] * 2,
        out_shape=[
            near,
            far,
            near,
            query,
            query,
            new,
            jax.ShapeDtypeStruct((req, 2 * tokens // req, key_dim), bf16),
            jax.ShapeDtypeStruct((8, 4 * n_cols), jnp.int32),
        ],
        scratch_shapes=[
            pltpu.VMEM(store.shape, bf16),
            pltpu.VMEM((n_cols,) + pair, bf16),
            pltpu.VMEM((4,) + ql.shape, bf16),
            pltpu.VMEM(wd.shape, bf16),
            pltpu.VMEM(qup.shape, bf16),
            pltpu.VMEM(wuk.shape, bf16),
            pltpu.VMEM(query.shape, bf16),
            pltpu.VMEM(new.shape, bf16),
            pltpu.VMEM(new.shape, bf16),
            pltpu.VMEM((req * new_len, ql.shape[1]), jnp.float32),
            pltpu.VMEM((2, prefix.shape[0]), jnp.int32),
            pltpu.SMEM((2, prefix.shape[0]), jnp.int32),
            dma((8,)),
            dma((3,)),
            dma((3,)),
            dma((n_cols,)),
            dma((n_cols,)),
            dma((FORWARDED,)),
            dma((FORWARDED,)),
            dma((2,)),
            dma((2,)),
        ],
        compiler_params=pltpu.CompilerParams(
            collective_id=1, has_side_effects=True, vmem_limit_bytes=VMEM_BYTES
        ),
        cost_estimate=pl.CostEstimate(flops=10**10, bytes_accessed=10**8, transcendentals=0),
        name="exchange",
    )(prefix, ql, hidden, gain, prefix, owner_t, slot_t, frequency, store, wd, qup, wuk)


def up_project(columns, weights):
    return lax.dot_general(
        columns, weights, (((0,), (0,)), ((), ())), preferred_element_type=jnp.float32
    )


def attention_step(table_ref, *refs, call, sizes, base, first, kind, scale, page, new_len):
    n_blocks = len(sizes)
    blocks, refs = refs[:n_blocks], refs[n_blocks:]
    q_ref, refs = refs[0], refs[1:]
    n_inputs = 1 if first else 2
    inputs, refs = refs[:n_inputs], refs[n_inputs:]
    if kind == "own":
        wuv_ref, refs = refs[0], refs[1:]
    result, mass, refs = refs[0], refs[1], refs[2:]
    pairs, sem, even, odd = refs[:4]
    acc = result.at[0] if kind == "state" else refs[4]
    lat, rows = acc.shape
    request = pl.program_id(0)

    @pl.when(request == 0)
    def _():
        copies, at = [], 0
        for i, block in enumerate(blocks):
            copies.append(pltpu.make_async_copy(block, pairs.at[pl.ds(at, sizes[i])], sem.at[i]))
            at += sizes[i]
        for copy in copies:
            copy.start()
        for copy in copies:
            copy.wait()

    factor = scale * math.log2(math.e)
    rope = q_ref.shape[1] - lat
    pad = 128 - rope
    bias_rows = jnp.where(
        lax.broadcasted_iota(jnp.int32, (pad, rows), 0) == 0, 1.0, 0.0
    ).astype(jnp.bfloat16)
    key_lane = lax.broadcasted_iota(jnp.int32, (page, pad), 1)

    def weigh(keys, weights):
        return lax.dot_general(
            keys[:, :lat], weights, (((0,), (0,)), ((), ())), preferred_element_type=jnp.float32
        )

    if first:
        new_keys = inputs[0][0]
        quarter = new_keys.shape[0] // 2
        row = lax.broadcasted_iota(jnp.int32, (2 * quarter, 1), 0)
        new_pos = jnp.where(row < quarter, table_ref[6, 0] + row, table_ref[6, quarter] + row - quarter)
        score = jnp.dot(new_keys, q_ref[0], preferred_element_type=jnp.float32)
        token = lax.broadcasted_iota(jnp.int32, score.shape, 1) % new_len
        live = new_pos <= token
        score = jnp.where(live, score, LOW)
        top = jnp.max(score, axis=0, keepdims=True)
        weights = jnp.where(live, jnp.exp2((score - top) * factor), 0.0)
        total = jnp.sum(weights, axis=0, keepdims=True)
        acc[...] = weigh(new_keys, weights.astype(jnp.bfloat16))
    else:
        acc_in, mass_in = inputs
        top, total = mass_in[0, 0:1, :], mass_in[0, 1:2, :]
        acc[...] = acc_in[0]

    begin = table_ref[2 * call + 1, request]
    end = table_ref[2 * call + 1, request + 1]
    tiles = (end - begin + TILE - 1) // TILE

    def keys_of(tile):
        parts = []
        for g in range(TILE):
            spot = begin + tile * TILE + g
            index = table_ref[2 * call, jnp.maximum(jnp.minimum(spot, end - 1), 0)]
            half = table_ref.shape[1] // 2
            pair, turn = index % half - base, index // half
            latent = pairs[pair, pl.ds(pl.multiple_of(turn * page, page), page), :]
            both = pairs[pair, pl.ds(2 * page, 2 * page * rope // lat), :]
            both = jnp.concatenate([both[:, i * 128 : (i + 1) * 128] for i in range(lat // 128)], axis=0)
            rotary = jnp.where(turn == 0, both[:, :rope], both[:, rope:])
            bias = jnp.where((key_lane == 0) & (spot >= end), LOW, 0.0).astype(jnp.bfloat16)
            parts.append(jnp.concatenate([latent, rotary, bias], axis=1))
        return jnp.concatenate(parts, axis=0)

    def scores_of(keys):
        query = jnp.concatenate([q_ref[0], bias_rows], axis=0)
        return jnp.dot(keys, query, preferred_element_type=jnp.float32)

    def take(sheet, keys, top, total):
        score = sheet[...]
        new_top = jnp.maximum(top, jnp.max(score, axis=0, keepdims=True))
        shrink = jnp.exp2((top - new_top) * factor)
        weights = jnp.exp2((score - new_top) * factor)
        total = total * shrink + jnp.sum(weights, axis=0, keepdims=True)
        acc[...] = acc[...] * shrink + weigh(keys, weights.astype(jnp.bfloat16))
        return new_top, total

    @pl.when(tiles > 0)
    def _():
        even[...] = scores_of(keys_of(0))

    def body(step, carry):
        tile = 2 * step
        later = keys_of(tile + 1)
        odd[...] = scores_of(later)
        carry = take(even, keys_of(tile), *carry)
        even[...] = scores_of(keys_of(jnp.minimum(tile + 2, tiles - 1)))
        return take(odd, later, *carry)

    carry = lax.fori_loop(0, tiles // 2, body, (top, total))
    top, total = lax.cond(
        tiles % 2 == 1,
        lambda c: take(even, keys_of(tiles - 1), *c),
        lambda c: c,
        carry,
    )

    if kind == "state":
        mass[0, 0:1, :] = top
        mass[0, 1:2, :] = total
        return
    live = total > 0
    inverse = jnp.where(live, 1.0 / total, 0.0)
    log_mass = jnp.where(live, top * factor + jnp.log(total) * math.log2(math.e), LOW)
    mass[request] = log_mass
    groups = rows // 128
    for g in range(groups):
        lanes = slice(g * 128, (g + 1) * 128)
        mixed = acc[:, lanes] * inverse[:, lanes]
        if kind == "own":
            high_v, low_v = refs[5], refs[6]
            high = mixed.astype(jnp.bfloat16)
            high_v[request, :, lanes] = high
            low_v[request, :, lanes] = (mixed - high.astype(jnp.float32)).astype(jnp.bfloat16)
        else:
            result[g, 0, :lat, :] = mixed.astype(jnp.bfloat16)
            high = log_mass[:, lanes].astype(jnp.bfloat16)
            rest = log_mass[:, lanes] - high.astype(jnp.float32)
            middle = rest.astype(jnp.bfloat16)
            low = (rest - middle.astype(jnp.float32)).astype(jnp.bfloat16)
            row = lax.broadcasted_iota(jnp.int32, (16, 128), 0)
            terms = [t.astype(jnp.float32) for t in (high, middle, low)]
            result[g, 0, lat:, :] = jnp.where(
                row == 0, terms[0], jnp.where(row == 1, terms[1], jnp.where(row == 2, terms[2], 0.0))
            ).astype(jnp.bfloat16)
    if kind == "own":

        @pl.when(request == pl.num_programs(0) - 1)
        def _():
            req = high_v.shape[0]
            head_v = wuv_ref.shape[2]
            for head in range(wuv_ref.shape[0]):
                cols = slice(head * new_len, (head + 1) * new_len)
                total = None
                for part in (high_v, low_v):
                    rows_of = jnp.concatenate([part[r, :, cols] for r in range(req)], axis=1)
                    term = up_project(rows_of, wuv_ref[head])
                    total = term if total is None else total + term
                for r in range(req):
                    result[r, :, head * head_v : (head + 1) * head_v] = total[
                        r * new_len : (r + 1) * new_len
                    ]


def attend(call, table, base, blocks, query, inputs, kind, scale, lat, new_len, w_uv=None):
    first = inputs[0].dtype == jnp.bfloat16
    req, key_dim, rows = query.shape
    sizes = [b.shape[0] for b in blocks]
    count = sum(sizes)
    page = blocks[0].shape[1] * lat // key_dim // 2
    groups = rows // 128
    kernel = functools.partial(
        attention_step, call=call, sizes=sizes, base=base, first=first, kind=kind, scale=scale, page=page, new_len=new_len
    )
    acc_spec = pl.BlockSpec((1, lat, rows), lambda r, *_: (r, 0, 0))
    mass_spec = pl.BlockSpec((1, 2, rows), lambda r, *_: (r, 0, 0))
    in_specs = [pl.BlockSpec(memory_space=pl.ANY)] * len(blocks)
    in_specs += [pl.BlockSpec((1, key_dim, rows), lambda r, *_: (r, 0, 0))]
    if first:
        in_specs += [pl.BlockSpec((1,) + inputs[0].shape[1:], lambda r, *_: (r, 0, 0))]
    else:
        in_specs += [acc_spec, mass_spec]
    scratch = [
        pltpu.VMEM((count,) + blocks[0].shape[1:], jnp.bfloat16),
        pltpu.SemaphoreType.DMA((len(blocks),)),
        pltpu.VMEM((TILE * page, rows), jnp.float32),
        pltpu.VMEM((TILE * page, rows), jnp.float32),
    ]
    if kind == "state":
        out_specs = [acc_spec, mass_spec]
        out_shape = [
            jax.ShapeDtypeStruct((req, lat, rows), jnp.float32),
            jax.ShapeDtypeStruct((req, 2, rows), jnp.float32),
        ]
    else:
        scratch.append(pltpu.VMEM((lat, rows), jnp.float32))
        out_specs = [None, pl.BlockSpec((req, 1, rows), lambda r, *_: (0, 0, 0))]
        out_shape = [None, jax.ShapeDtypeStruct((req, 1, rows), jnp.float32)]
        if kind == "partner":
            out_specs[0] = pl.BlockSpec((groups, 1, lat + 16, 128), lambda r, *_: (0, r, 0, 0))
            out_shape[0] = jax.ShapeDtypeStruct((groups, req, lat + 16, 128), jnp.bfloat16)
        else:
            heads, _, head_v = w_uv.shape
            in_specs.append(pl.BlockSpec(w_uv.shape, lambda r, *_: (0, 0, 0)))
            scratch += [pltpu.VMEM((req, lat, rows), jnp.bfloat16)] * 2
            out_specs[0] = pl.BlockSpec((req, new_len, heads * head_v), lambda r, *_: (0, 0, 0))
            out_shape[0] = jax.ShapeDtypeStruct((req, new_len, heads * head_v), jnp.float32)
    more = [w_uv] if kind == "own" else []
    return pl.pallas_call(
        kernel,
        grid_spec=pltpu.PrefetchScalarGridSpec(
            num_scalar_prefetch=1,
            grid=(req,),
            in_specs=in_specs,
            out_specs=out_specs,
            scratch_shapes=scratch,
        ),
        out_shape=out_shape,
        compiler_params=pltpu.CompilerParams(
            dimension_semantics=("arbitrary",), vmem_limit_bytes=VMEM_BYTES
        ),
        cost_estimate=pl.CostEstimate(
            flops=8 * rows * count * page * (key_dim + lat),
            bytes_accessed=4 * req * lat * rows * 2 + count * page * key_dim * 2,
            transcendentals=2 * rows * count * page,
        ),
        name=f"attend_{call}_{kind}",
    )(table, *blocks, query, *inputs, *more)


def merge_step(turn_ref, got_ref, own_ref, mass_ref, wuv_ref, new_ref, out_ref, handed_ref):
    _, req, deep, _ = got_ref.shape
    group, lat, head_v = wuv_ref.shape
    new_len = 128 // group

    @pl.when(pl.program_id(0) == 0)
    def _():
        for i in range(req):
            handed_ref[i] = new_ref[turn_ref[i]]

    shares = []
    for r in range(req):
        tail = got_ref[0, r, lat:, :].astype(jnp.float32)
        got_mass = tail[0:1] + tail[1:2] + tail[2:3]
        share = 1.0 / (1.0 + jnp.exp2(mass_ref[r] - got_mass))
        shares.append(jnp.broadcast_to(share, (128, 128)).T)
    for j in range(group):
        rows = slice(j * new_len, (j + 1) * new_len)
        columns = jnp.concatenate([got_ref[0, r, :lat, rows] for r in range(req)], axis=1)
        got = up_project(columns, wuv_ref[j])
        for r in range(req):
            share = shares[r][rows]
            lanes = slice(j * head_v, (j + 1) * head_v)
            own = own_ref[r, :, lanes]
            out_ref[r, :, lanes] = (
                own * (1.0 - share) + got[r * new_len : (r + 1) * new_len] * share
            ).astype(jnp.bfloat16)


def merge(turns, got, own, mass, w_uv, new_rows):
    groups, req, deep, _ = got.shape
    heads, lat, head_v = w_uv.shape
    group = heads // groups
    new_len = 128 // group
    wide = pl.BlockSpec((req, new_len, group * head_v), lambda g, *_: (0, 0, g))
    whole = pl.BlockSpec(new_rows.shape, lambda g, *_: (0, 0, 0))
    return pl.pallas_call(
        merge_step,
        grid_spec=pltpu.PrefetchScalarGridSpec(
            num_scalar_prefetch=1,
            grid=(groups,),
            in_specs=[
                pl.BlockSpec((1, req, deep, 128), lambda g, *_: (g, 0, 0, 0)),
                wide,
                pl.BlockSpec((req, 1, 128), lambda g, *_: (0, 0, g)),
                pl.BlockSpec((group, lat, head_v), lambda g, *_: (g, 0, 0)),
                whole,
            ],
            out_specs=[wide, whole],
        ),
        out_shape=[
            jax.ShapeDtypeStruct((req, new_len, heads * head_v), jnp.bfloat16),
            jax.ShapeDtypeStruct(new_rows.shape, jnp.bfloat16),
        ],
        compiler_params=pltpu.CompilerParams(
            dimension_semantics=("arbitrary",), vmem_limit_bytes=VMEM_BYTES
        ),
        name="merge",
    )(turns, got, own, mass, w_uv, new_rows)


def partner_pairs(pool_count, dev_count, which):
    return [
        (pool * dev_count + dev, partners(pool, dev)[which] * dev_count + dev)
        for pool in range(pool_count)
        for dev in range(dev_count)
    ]


def on_device(
    hidden,
    query_latent_rows,
    store,
    w_down,
    kv_gain,
    query_up_weight,
    w_uk,
    w_uv,
    prefix_pages,
    page_owner,
    page_slot,
    decode_order,
):
    pool_count = lax.axis_size("pool")
    dev_count = lax.axis_size("dev")
    column = lax.axis_index("dev")
    req_col, quarter, model_width = hidden.shape
    new_len = quarter * pool_count
    lat_dim = kv_gain.shape[0]
    key_dim = w_down.shape[1]
    nope_dim = w_uk.shape[1]
    rope_dim = key_dim - lat_dim
    first_row = column * req_col
    score_scale = (nope_dim + rope_dim) ** (-0.5)
    powers = np.exp(np.arange(rope_dim // 2) * (-2.0 * np.log(50000.0) / rope_dim))
    frequency = np.repeat(powers.astype(np.float32)[:, None], req_col * new_len, axis=1)

    near, far, passed, query, query_other, new_local, new_keys, table = exchange(
        prefix_pages,
        query_latent_rows.reshape(req_col * quarter, -1),
        hidden.reshape(req_col * quarter, model_width),
        kv_gain,
        page_owner.T,
        page_slot.T,
        jnp.asarray(frequency),
        store[0],
        w_down.T,
        query_up_weight,
        w_uk,
        req_col,
    )
    axes = ("pool", "dev")
    passed_far = lax.ppermute(far, axes, partner_pairs(pool_count, dev_count, 1))

    new = (new_keys,)
    common = dict(scale=score_scale, lat=lat_dim, new_len=new_len)
    early_blocks = [near, far, passed]
    state = attend(0, table, 0, early_blocks, query_other, new, "state", **common)
    part, part_mass = attend(
        1,
        table,
        dev_count + FORWARDED,
        [passed_far],
        query_other,
        state,
        "partner",
        **common,
    )
    got = lax.ppermute(part, axes, partner_pairs(pool_count, dev_count, 0))
    table, part_mass = lax.optimization_barrier((table, part_mass))
    own, own_mass = attend(
        2, table, 0, early_blocks + [passed_far], query, new, "own", w_uv=w_uv, **common
    )
    turns = lax.dynamic_slice_in_dim(decode_order, first_row, req_col) - first_row
    attended, handed = merge(
        turns, got, own, own_mass, w_uv, new_local.reshape(req_col, quarter, key_dim)
    )
    return (attended, handed)


def solution(mesh):
    in_specs = (
        P("dev", "pool", None),
        P("dev", "pool", None),
        P(("pool", "dev"), None, None, None),
        P(),
        P(),
        P(None, "pool"),
        P("pool", None, None),
        P("pool", None, None),
        P(),
        P(),
        P(),
        P(),
    )
    out_specs = (P("dev", None, "pool"), P("dev", "pool", None))
    return jax.shard_map(
        on_device, mesh=mesh, in_specs=in_specs, out_specs=out_specs, check_vma=False
    )
```

```python
import functools
import math

import jax
import jax.numpy as jnp
import numpy as np
from jax import lax
from jax.experimental import pallas as pl
from jax.experimental.pallas import tpu as pltpu
from jax.sharding import PartitionSpec as P

TILE = 4
LOW = -1e30
FORWARDED = 24
DIRECT = 0
VMEM_BYTES = 60 * 2**20
MESH = pl.DeviceIdType.MESH
STEPS = [
    (0, 1), (1, 0), (0, 3), (3, 0), (1, 1), (3, 3), (1, 3), (3, 1),
    (0, 2), (2, 0), (1, 2), (2, 1), (3, 2), (2, 3), (2, 2),
]
OFFSETS = [(0, 0, 0)] + [(z, x, 0) for z, x in STEPS] + [(0, 0, 1)] + [(z, x, 1) for z, x in STEPS]


def shifted(dev, offset, sign):
    core, x, z = dev % 2, (dev // 2) % 4, dev // 8
    dz, dx, dc = offset
    return ((z + sign * dz + 4) % 4 * 4 + (x + sign * dx + 4) % 4) * 2 + (core + dc) % 2


def partners(pool, dev):
    near = pool + 1 - 2 * (pool % 2)
    far = 3 - pool
    odd = dev % 2
    return near + odd * (far - near), far + odd * (near - far)


def list_pages(pool, dev, key_partner, owners, table_ref, n_a, quarter):
    n_pairs = len(OFFSETS)
    width = 4 * n_pairs
    entries = owners.shape[1]
    entry = lax.broadcasted_iota(jnp.int32, (1, entries), 1)
    pair = lax.broadcasted_iota(jnp.int32, (2 * n_pairs, 1), 0)
    source = jnp.zeros((2 * n_pairs, 1), jnp.int32)
    for j, offset in enumerate(OFFSETS):
        source = jnp.where(pair % n_pairs == j, shifted(dev, offset, -1), source)
    source = source + n_pairs * jnp.where(pair < n_pairs, pool, key_partner)
    hit = owners == source
    head = jnp.min(jnp.where(hit, entry, entries), axis=1, keepdims=True)
    tail = jnp.max(jnp.where(hit, entry, -1), axis=1, keepdims=True)
    nobody = entries // 64
    low = head // 64
    high = jnp.where(tail > head, tail // 64, nobody)
    request = jnp.concatenate([low, high], axis=0)
    place = lax.broadcasted_iota(jnp.int32, (width, 1), 0)
    late = place % (2 * n_pairs) >= n_pairs + n_a
    lane = lax.broadcasted_iota(jnp.int32, (1, width), 1)
    rows = []
    for wanted in (jnp.logical_not(late), late, None):
        mine = request if wanted is None else jnp.where(wanted, request, nobody)
        key = (mine * width + place).astype(jnp.float32)
        key = jnp.broadcast_to(key, (width, width))
        rank = jnp.sum((key.T < key).astype(jnp.float32), axis=1, keepdims=True).astype(jnp.int32)
        rows.append(jnp.sum(jnp.where(rank == lane, place, 0), axis=0, keepdims=True))
        rows.append(jnp.sum((mine < lane).astype(jnp.int32), axis=0, keepdims=True))
    rows.append(
        jnp.where(lane < quarter, pool * quarter + lane, key_partner * quarter + lane - quarter)
    )
    for i, row in enumerate(rows):
        table_ref[i : i + 1, :] = row


def exchange_kernel(
    prefix_ref, ql_ref, hidden_ref, gain_ref, prefix_row, owner_ref, slot_ref, frequency_ref,
    store_ref, wd_ref, qup_ref, wuk_ref,
    arr_a, arr_b, pass_a, q_own, q_other, new_own, new_keys, table_ref,
    store_v, packed, ql_in, wd_v, qup_v, wuk_v, q_s, new_s, new_in, q_full, picks_v, picks,
    load_sem, ql_send, ql_recv, page_send, page_recv, pass_send, pass_recv, pair_send, pair_recv,
):
    pool, dev = lax.axis_index("pool"), lax.axis_index("dev")
    head_partner, key_partner = partners(pool, dev)
    req, key_dim, own_rows = q_s.shape
    heads, nope, lat = wuk_v.shape
    rope = key_dim - lat
    half_rope = rope // 2
    quarter = ql_in.shape[1] // req
    new_len = 4 * quarter
    page = store_v.shape[1]
    n_send = len(OFFSETS)
    n_a = arr_a.shape[0]

    load_store = pltpu.make_async_copy(store_ref, store_v, load_sem.at[6])
    load_store.start()
    loads = [
        pltpu.make_async_copy(wd_ref, wd_v, load_sem.at[0]),
        pltpu.make_async_copy(qup_ref, qup_v, load_sem.at[1]),
        pltpu.make_async_copy(wuk_ref, wuk_v, load_sem.at[2]),
    ]
    for copy in loads:
        copy.start()

    n_relay = n_a - DIRECT
    direct = range(n_relay, n_a)

    def direct_target(j):
        column = shifted(dev, OFFSETS[j], 1)
        return partners(pool, column)[1], column

    barrier = pltpu.get_barrier_semaphore()
    for offset in OFFSETS[1:]:
        pl.semaphore_signal(
            barrier, inc=1, device_id=(pool, shifted(dev, offset, 1)), device_id_type=MESH
        )
    for j in direct:
        for peer in (direct_target(j), (key_partner, shifted(dev, OFFSETS[j], -1))):
            pl.semaphore_signal(barrier, inc=1, device_id=peer, device_id_type=MESH)
    for step in range(1, 4):
        pl.semaphore_signal(
            barrier, inc=1, device_id=((pool + step) % 4, dev), device_id_type=MESH
        )

    prefix = prefix_row[...][None, :]
    owners = owner_ref[...]
    page_of = lax.broadcasted_iota(jnp.int32, owners.shape, 0)
    lane_of = lax.broadcasted_iota(jnp.int32, owners.shape, 1)
    n_slots, max_pages = store_v.shape[0], owners.shape[0]
    used = page_of < prefix
    mine = used & (owners == pool * n_send + dev)
    code = (lane_of % req * max_pages + page_of) * n_slots + slot_ref[...]
    low = jnp.min(jnp.where(mine, code, req * max_pages * n_slots), axis=0, keepdims=True)
    high = jnp.max(jnp.where(mine, code, 0), axis=0, keepdims=True)
    n_lanes = owners.shape[1]
    for step in (1, 2):
        low = jnp.minimum(low, pltpu.roll(low, n_lanes - step, 1))
        high = jnp.maximum(high, pltpu.roll(high, n_lanes - step, 1))
    picks_v[0:1, :] = low % n_slots
    picks_v[1:2, :] = high % n_slots
    load_picks = pltpu.make_async_copy(picks_v, picks, load_sem.at[7])
    load_picks.start()

    def pack(j):
        target = shifted(dev, OFFSETS[j], 1)
        pages = [store_v[picks[k, req * target]] for k in range(2)]
        for k in range(2):
            packed[j, k * page : (k + 1) * page, :] = pages[k][:, :lat]
        keys = jnp.concatenate([p[:, lat:] for p in pages], axis=1)
        step = page * 2 * rope // lat
        packed[j, 2 * page :, :] = jnp.concatenate(
            [keys[i * step : (i + 1) * step] for i in range(page // step)], axis=1
        )

    load_picks.wait()
    load_store.wait()
    for j in (0, 1, *direct):
        pack(j)
    pl.semaphore_wait(barrier, n_send - 1 + 3 + 2 * DIRECT)

    def remote(src, dst, send, recv, target):
        return pltpu.make_async_remote_copy(
            src_ref=src, dst_ref=dst, send_sem=send, recv_sem=recv, device_id=target, device_id_type=MESH
        )

    ql_sends = [
        remote(ql_ref, ql_in.at[pool], ql_send.at[s - 1], ql_recv.at[s - 1], ((pool + s) % 4, dev))
        for s in range(1, 4)
    ]
    ql_gets = [
        remote(
            ql_ref, ql_in.at[(pool + 4 - s) % 4], ql_send.at[s - 1], ql_recv.at[s - 1], (head_partner, dev)
        )
        for s in range(1, 4)
    ]
    for copy in ql_sends:
        copy.start()

    def landing(j):
        return arr_a.at[j] if j < n_a else arr_b.at[j - n_a]

    passes = [
        remote(
            packed.at[j] if j == 0 or j in direct else arr_a.at[j],
            pass_a.at[j],
            pass_send.at[j],
            pass_recv.at[j],
            direct_target(j) if j in direct else (key_partner, dev),
        )
        for j in range(n_a)
    ]
    sends = [None] * n_send
    for j in (*range(1, n_relay), *range(n_a, n_send), *direct):
        if j > 1 and j not in direct:
            pack(j)
        copy = remote(
            packed.at[j],
            landing(j),
            page_send.at[j],
            page_recv.at[j],
            (pool, shifted(dev, OFFSETS[j], 1)),
        )
        copy.start()
        sends[j] = copy
        if j == 1:
            for early in (0, *direct):
                passes[early].start()
    own_pages = pltpu.make_async_copy(packed.at[0], arr_a.at[0], load_sem.at[3])
    own_pages.start()

    def pass_on(first, last):
        for j in range(first, last):
            sends[j].wait_recv()
            if j < n_relay:
                passes[j].start()

    pass_on(1, 2)
    frequency = frequency_ref[...]
    lane = lax.broadcasted_iota(jnp.int32, (1, frequency.shape[1]), 1)
    position = pool * quarter + lane % quarter
    local_position = position
    position = lane % new_len
    for r in range(req):
        begin = prefix_ref[req * dev + r] * page
        local_position = local_position + jnp.where(lane // quarter == r, begin, 0)
        position = position + jnp.where(lane // new_len == r, begin, 0)
    local_angles = (frequency * local_position.astype(jnp.float32))[:, : req * quarter]
    angles = frequency * position.astype(jnp.float32)

    loads[0].wait()
    projected = lax.dot_general(
        wd_v[...], hidden_ref[...], (((1,), (1,)), ((), ())), preferred_element_type=jnp.float32
    )
    latent = projected[:lat]
    latent = latent * lax.rsqrt(jnp.mean(latent * latent, axis=0, keepdims=True) + 1e-06)
    first, second = projected[lat : lat + half_rope], projected[lat + half_rope :]
    lcos, lsin = jnp.cos(local_angles), jnp.sin(local_angles)
    rotated = jnp.concatenate([first * lcos - second * lsin, first * lsin + second * lcos], axis=0)
    new_s[...] = jnp.concatenate(
        [latent.T * gain_ref[...].astype(jnp.float32)[None, :], rotated.T], axis=1
    ).astype(jnp.bfloat16)
    new_send = remote(new_s, new_in, pair_send.at[0], pair_recv.at[0], (key_partner, dev))
    new_send.start()
    new_keep = pltpu.make_async_copy(new_s, new_own, load_sem.at[4])
    new_keep.start()
    pass_on(2, 4)
    own = jnp.where(used, owners, -1).astype(jnp.float32)
    own = pltpu.roll(own, (n_lanes - req * dev) % n_lanes, 1)
    own = jnp.concatenate([own, jnp.zeros((n_lanes - max_pages, n_lanes), jnp.float32)], axis=0).T
    own = jnp.concatenate([own[r : r + 1, :max_pages] for r in range(req)], axis=1)
    list_pages(pool, dev, key_partner, own.astype(jnp.int32), table_ref, n_a, quarter)

    ql_in[pool] = ql_ref[...]
    for copy in ql_gets:
        copy.wait_recv()
    for y in range(4):
        rows = ql_in[y].astype(jnp.float32)
        for r in range(req):
            q_full[pl.ds(r * new_len + y * quarter, quarter), :] = rows[
                r * quarter : (r + 1) * quarter
            ]
    for copy in loads[1:]:
        copy.wait()
    group = 128 // new_len
    width = nope + rope

    cos, sin = jnp.cos(angles), jnp.sin(angles)

    def project(g):
        raw = jnp.dot(
            q_full[...].astype(jnp.bfloat16),
            qup_v[:, g * group * width : (g + 1) * group * width],
            preferred_element_type=jnp.float32,
        ).T
        built = []
        for j in range(group):
            at = j * width
            q_nope = raw[at : at + nope].astype(jnp.bfloat16)
            q_abs = lax.dot_general(
                wuk_v[g * group + j],
                q_nope,
                (((0,), (0,)), ((), ())),
                preferred_element_type=jnp.float32,
            )
            x = raw[at + nope : at + nope + half_rope]
            y = raw[at + nope + half_rope : at + width]
            built.append(
                jnp.concatenate([q_abs, x * cos - y * sin, x * sin + y * cos], axis=0).astype(
                    jnp.bfloat16
                )
            )
        for r in range(req):
            q_s[r, :, g * 128 : (g + 1) * 128] = jnp.concatenate(
                [b[:, r * new_len : (r + 1) * new_len] for b in built], axis=1
            )

    done = 4
    for g in range(heads // group):
        project(g)
        if g < heads // group - 1:
            pass_on(done, done + 2)
            done += 2

    q_send = remote(q_s, q_other, pair_send.at[1], pair_recv.at[1], (head_partner, dev))
    q_send.start()
    q_keep = pltpu.make_async_copy(q_s, q_own, load_sem.at[5])
    q_keep.start()

    pass_on(done, n_send)
    for copy in ql_sends:
        copy.wait_send()
    for copy in sends[1:]:
        copy.wait_send()
    own_pages.wait()
    new_keep.wait()
    q_keep.wait()
    new_send.wait()
    own_new, got_new = new_s[...].astype(jnp.float32), new_in[...].astype(jnp.float32)
    for r in range(req):
        rows = slice(r * quarter, (r + 1) * quarter)
        new_keys[r] = jnp.concatenate([own_new[rows], got_new[rows]], axis=0).astype(jnp.bfloat16)
    q_send.wait()
    for copy in passes:
        copy.wait()


def exchange(prefix, ql, hidden, gain, owner_t, slot_t, frequency, store, wd, qup, wuk, req):
    n_cols = prefix.shape[0] // req
    n_slots, page, key_dim = store.shape
    heads, nope, lat = wuk.shape
    tokens = ql.shape[0]
    new_len = 4 * tokens // req
    bf16 = jnp.bfloat16
    any_spec = pl.BlockSpec(memory_space=pl.ANY)
    vmem = pl.BlockSpec(memory_space=pltpu.VMEM)
    own_rows = heads * new_len
    pair = (2 * page * key_dim // lat, lat)
    query = jax.ShapeDtypeStruct((req, key_dim, own_rows), bf16)
    new = jax.ShapeDtypeStruct((tokens, key_dim), bf16)
    near = jax.ShapeDtypeStruct((FORWARDED,) + pair, bf16)
    far = jax.ShapeDtypeStruct((n_cols - FORWARDED,) + pair, bf16)
    dma = pltpu.SemaphoreType.DMA
    return pl.pallas_call(
        exchange_kernel,
        in_specs=[pl.BlockSpec(memory_space=pltpu.SMEM)] + [vmem] * 7 + [any_spec] * 4,
        out_specs=[any_spec] * 6 + [vmem] * 2,
        out_shape=[
            near,
            far,
            near,
            query,
            query,
            new,
            jax.ShapeDtypeStruct((req, 2 * tokens // req, key_dim), bf16),
            jax.ShapeDtypeStruct((8, 4 * n_cols), jnp.int32),
        ],
        scratch_shapes=[
            pltpu.VMEM(store.shape, bf16),
            pltpu.VMEM((n_cols,) + pair, bf16),
            pltpu.VMEM((4,) + ql.shape, bf16),
            pltpu.VMEM(wd.shape, bf16),
            pltpu.VMEM(qup.shape, bf16),
            pltpu.VMEM(wuk.shape, bf16),
            pltpu.VMEM(query.shape, bf16),
            pltpu.VMEM(new.shape, bf16),
            pltpu.VMEM(new.shape, bf16),
            pltpu.VMEM((req * new_len, ql.shape[1]), jnp.float32),
            pltpu.VMEM((2, prefix.shape[0]), jnp.int32),
            pltpu.SMEM((2, prefix.shape[0]), jnp.int32),
            dma((8,)),
            dma((3,)),
            dma((3,)),
            dma((n_cols,)),
            dma((n_cols,)),
            dma((FORWARDED,)),
            dma((FORWARDED,)),
            dma((2,)),
            dma((2,)),
        ],
        compiler_params=pltpu.CompilerParams(
            collective_id=1, has_side_effects=True, vmem_limit_bytes=VMEM_BYTES
        ),
        cost_estimate=pl.CostEstimate(flops=10**10, bytes_accessed=10**8, transcendentals=0),
        name="exchange",
    )(prefix, ql, hidden, gain, prefix, owner_t, slot_t, frequency, store, wd, qup, wuk)


def gather_rows(parts, first, last):
    return jnp.concatenate([part[first:last] for part in parts], axis=0)


def attention_step(table_ref, *refs, call, sizes, base, first, kind, scale, page, new_len):
    n_blocks = len(sizes)
    blocks, refs = refs[:n_blocks], refs[n_blocks:]
    q_ref, refs = refs[0], refs[1:]
    n_inputs = 1 if first else 2
    inputs, refs = refs[:n_inputs], refs[n_inputs:]
    if kind == "own":
        wuv_ref, refs = refs[0], refs[1:]
    result, mass, refs = refs[0], refs[1], refs[2:]
    pairs, sem, even, odd, even_keys, odd_keys, query = refs[:7]
    acc = result.at[0] if kind == "state" else refs[7]
    lat, rows = acc.shape
    request = pl.program_id(0)

    copies, at = [], 0
    for i, block in enumerate(blocks):
        copies.append(pltpu.make_async_copy(block, pairs.at[pl.ds(at, sizes[i])], sem.at[i]))
        at += sizes[i]

    @pl.when(request == 0)
    def _():
        for copy in copies:
            copy.start()

    factor = scale * math.log2(math.e)
    rope = q_ref.shape[1] - lat
    pad = 128 - rope
    bias_rows = jnp.where(
        lax.broadcasted_iota(jnp.int32, (pad, rows), 0) == 0, 1.0, 0.0
    ).astype(jnp.bfloat16)
    key_lane = lax.broadcasted_iota(jnp.int32, (page, pad), 1)

    query[: lat + rope, :] = q_ref[0]
    query[lat + rope :, :] = bias_rows

    def weigh(keys, weights):
        return lax.dot_general(
            keys, weights, (((0,), (0,)), ((), ())), preferred_element_type=jnp.float32
        )

    if first:
        new_keys = inputs[0][0]
        quarter = new_keys.shape[0] // 2
        row = lax.broadcasted_iota(jnp.int32, (2 * quarter, 1), 0)
        new_pos = jnp.where(row < quarter, table_ref[6, 0] + row, table_ref[6, quarter] + row - quarter)
        score = jnp.dot(new_keys, q_ref[0], preferred_element_type=jnp.float32)
        token = lax.broadcasted_iota(jnp.int32, score.shape, 1) % new_len
        live = new_pos <= token
        score = jnp.where(live, score, LOW)
        top = jnp.max(score, axis=0, keepdims=True)
        weights = jnp.where(live, jnp.exp2((score - top) * factor), 0.0)
        total = jnp.sum(weights, axis=0, keepdims=True)
        acc[...] = weigh(new_keys[:, :lat], weights.astype(jnp.bfloat16))
    else:
        acc_in, mass_in = inputs
        top, total = mass_in[0, 0:1, :], mass_in[0, 1:2, :]
        acc[...] = acc_in[0]

    @pl.when(request == 0)
    def _():
        for copy in copies:
            copy.wait()

    begin = table_ref[2 * call + 1, request]
    end = table_ref[2 * call + 1, request + 1]
    tiles = (end - begin + TILE - 1) // TILE

    def fetch(tile, keys, sheet):
        for g in range(TILE):
            spot = begin + tile * TILE + g
            index = table_ref[2 * call, jnp.maximum(jnp.minimum(spot, end - 1), 0)]
            half = table_ref.shape[1] // 2
            pair, turn = index % half - base, index // half
            rows = slice(g * page, (g + 1) * page)
            keys[rows, :lat] = pairs[pair, pl.ds(pl.multiple_of(turn * page, page), page), :]
            both = pairs[pair, pl.ds(2 * page, 2 * page * rope // lat), :]
            both = jnp.concatenate([both[:, i * 128 : (i + 1) * 128] for i in range(lat // 128)], axis=0)
            rotary = jnp.where(turn == 0, both[:, :rope], both[:, rope:])
            bias = jnp.where((key_lane == 0) & (spot >= end), LOW, 0.0).astype(jnp.bfloat16)
            keys[rows, lat:] = jnp.concatenate([rotary, bias], axis=1)
        sheet[...] = jnp.dot(keys[...], query[...], preferred_element_type=jnp.float32)

    def take(sheet, keys, top, total):
        score = sheet[...]
        new_top = jnp.maximum(top, jnp.max(score, axis=0, keepdims=True))
        shrink = jnp.exp2((top - new_top) * factor)
        weights = jnp.exp2((score - new_top) * factor)
        total = total * shrink + jnp.sum(weights, axis=0, keepdims=True)
        acc[...] = acc[...] * shrink + weigh(keys[:, :lat], weights.astype(jnp.bfloat16))
        return new_top, total

    @pl.when(tiles > 0)
    def _():
        fetch(0, even_keys, even)

    def body(step, carry):
        tile = 2 * step
        fetch(tile + 1, odd_keys, odd)
        carry = take(even, even_keys, *carry)
        fetch(jnp.minimum(tile + 2, tiles - 1), even_keys, even)
        return take(odd, odd_keys, *carry)

    carry = lax.fori_loop(0, tiles // 2, body, (top, total))
    top, total = lax.cond(
        tiles % 2 == 1,
        lambda c: take(even, even_keys, *c),
        lambda c: c,
        carry,
    )

    if kind == "state":
        mass[0, 0:1, :] = top
        mass[0, 1:2, :] = total
        return
    live = total > 0
    inverse = jnp.where(live, 1.0 / total, 0.0)
    log_mass = jnp.where(live, top * factor + jnp.log(total) * math.log2(math.e), LOW)
    mass[request] = log_mass
    mixed = (acc[...] * inverse).T
    high = mixed.astype(jnp.bfloat16)
    if kind == "partner":
        result[0, :rows, :] = high
        terms, rest = [], log_mass
        for _ in range(3):
            terms.append(rest.astype(jnp.bfloat16).astype(jnp.float32))
            rest = rest - terms[-1]
        row = lax.broadcasted_iota(jnp.int32, (16, rows), 0)
        tail = jnp.where(row == 2, terms[2], 0.0)
        tail = jnp.where(row == 0, terms[0], jnp.where(row == 1, terms[1], tail))
        result[0, rows:, :] = tail.astype(jnp.bfloat16)
    else:
        high_v, low_v = refs[8], refs[9]
        high_v[request] = high
        low_v[request] = (mixed - high.astype(jnp.float32)).astype(jnp.bfloat16)

    if kind == "own":

        @pl.when(request == pl.num_programs(0) - 1)
        def _():
            req = high_v.shape[0]
            head_v = wuv_ref.shape[2]
            for head in range(wuv_ref.shape[0]):
                first_row, last_row = head * new_len, (head + 1) * new_len
                total = None
                for part in (high_v, low_v):
                    rows_of = gather_rows([part.at[r] for r in range(req)], first_row, last_row)
                    term = jnp.dot(rows_of, wuv_ref[head], preferred_element_type=jnp.float32)
                    total = term if total is None else total + term
                for r in range(req):
                    result[r, :, head * head_v : (head + 1) * head_v] = total[
                        r * new_len : (r + 1) * new_len
                    ]


def attend(call, table, base, blocks, query, inputs, kind, scale, lat, new_len, w_uv=None):
    first = inputs[0].dtype == jnp.bfloat16
    req, key_dim, rows = query.shape
    sizes = [b.shape[0] for b in blocks]
    count = sum(sizes)
    page = blocks[0].shape[1] * lat // key_dim // 2
    kernel = functools.partial(
        attention_step, call=call, sizes=sizes, base=base, first=first, kind=kind, scale=scale, page=page, new_len=new_len
    )
    acc_spec = pl.BlockSpec((1, lat, rows), lambda r, *_: (r, 0, 0))
    mass_spec = pl.BlockSpec((1, 2, rows), lambda r, *_: (r, 0, 0))
    in_specs = [pl.BlockSpec(memory_space=pl.ANY)] * len(blocks)
    in_specs += [pl.BlockSpec((1, key_dim, rows), lambda r, *_: (r, 0, 0))]
    if first:
        in_specs += [pl.BlockSpec((1,) + inputs[0].shape[1:], lambda r, *_: (r, 0, 0))]
    else:
        in_specs += [acc_spec, mass_spec]
    scratch = [
        pltpu.VMEM((count,) + blocks[0].shape[1:], jnp.bfloat16),
        pltpu.SemaphoreType.DMA((len(blocks),)),
        pltpu.VMEM((TILE * page, rows), jnp.float32),
        pltpu.VMEM((TILE * page, rows), jnp.float32),
        pltpu.VMEM((TILE * page, lat + 128), jnp.bfloat16),
        pltpu.VMEM((TILE * page, lat + 128), jnp.bfloat16),
        pltpu.VMEM((lat + 128, rows), jnp.bfloat16),
    ]
    if kind == "state":
        out_specs = [acc_spec, mass_spec]
        out_shape = [
            jax.ShapeDtypeStruct((req, lat, rows), jnp.float32),
            jax.ShapeDtypeStruct((req, 2, rows), jnp.float32),
        ]
    else:
        scratch.append(pltpu.VMEM((lat, rows), jnp.float32))
        out_specs = [None, pl.BlockSpec((req, 1, rows), lambda r, *_: (0, 0, 0))]
        out_shape = [None, jax.ShapeDtypeStruct((req, 1, rows), jnp.float32)]
        if kind == "partner":
            out_specs[0] = pl.BlockSpec((1, rows + 16, lat), lambda r, *_: (r, 0, 0))
            out_shape[0] = jax.ShapeDtypeStruct((req, rows + 16, lat), jnp.bfloat16)
        else:
            heads, _, head_v = w_uv.shape
            in_specs.append(pl.BlockSpec(w_uv.shape, lambda r, *_: (0, 0, 0)))
            scratch += [pltpu.VMEM((req, lat, rows), jnp.bfloat16)] * 2
            out_specs[0] = pl.BlockSpec((req, new_len, heads * head_v), lambda r, *_: (0, 0, 0))
            out_shape[0] = jax.ShapeDtypeStruct((req, new_len, heads * head_v), jnp.float32)
    more = [w_uv] if kind == "own" else []
    return pl.pallas_call(
        kernel,
        grid_spec=pltpu.PrefetchScalarGridSpec(
            num_scalar_prefetch=1,
            grid=(req,),
            in_specs=in_specs,
            out_specs=out_specs,
            scratch_shapes=scratch,
        ),
        out_shape=out_shape,
        compiler_params=pltpu.CompilerParams(
            dimension_semantics=("arbitrary",), vmem_limit_bytes=VMEM_BYTES
        ),
        cost_estimate=pl.CostEstimate(
            flops=8 * rows * count * page * (key_dim + lat),
            bytes_accessed=4 * req * lat * rows * 2 + count * page * key_dim * 2,
            transcendentals=2 * rows * count * page,
        ),
        name=f"attend_{call}_{kind}",
    )(table, *blocks, query, *inputs, *more)


def merge_step(turn_ref, got_ref, got_mass_ref, own_ref, mass_ref, wuv_ref, new_ref, out_ref, handed_ref):
    req, width, lat = got_ref.shape
    group, _, head_v = wuv_ref.shape
    new_len = width // group

    @pl.when(pl.program_id(0) == 0)
    def _():
        for i in range(req):
            handed_ref[i] = new_ref[turn_ref[i]]

    shares = []
    for r in range(req):
        tail = got_mass_ref[r].astype(jnp.float32)
        got_mass = tail[0:1] + tail[1:2] + tail[2:3]
        share = 1.0 / (1.0 + jnp.exp2(mass_ref[r] - got_mass))
        shares.append(jnp.broadcast_to(share, (width, width)).T)
    for j in range(group):
        first, last = j * new_len, (j + 1) * new_len
        rows = gather_rows([got_ref.at[r] for r in range(req)], first, last)
        got = jnp.dot(rows, wuv_ref[j], preferred_element_type=jnp.float32)
        lanes = slice(j * head_v, (j + 1) * head_v)
        for r in range(req):
            share = shares[r][first:last]
            own = own_ref[r, :, lanes]
            out_ref[r, :, lanes] = (
                own * (1.0 - share) + got[r * new_len : (r + 1) * new_len] * share
            ).astype(jnp.bfloat16)


def merge(turns, got, own, mass, w_uv, new_rows):
    req, deep, lat = got.shape
    heads, _, head_v = w_uv.shape
    groups = (deep - 16) // 128
    group = heads // groups
    new_len = 128 // group
    wide = pl.BlockSpec((req, new_len, group * head_v), lambda g, *_: (0, 0, g))
    whole = pl.BlockSpec(new_rows.shape, lambda g, *_: (0, 0, 0))
    return pl.pallas_call(
        merge_step,
        grid_spec=pltpu.PrefetchScalarGridSpec(
            num_scalar_prefetch=1,
            grid=(groups,),
            in_specs=[
                pl.BlockSpec((req, 128, lat), lambda g, *_: (0, g, 0)),
                pl.BlockSpec((req, 16, 128), lambda g, *_: (0, (deep - 16) // 16, g)),
                wide,
                pl.BlockSpec((req, 1, 128), lambda g, *_: (0, 0, g)),
                pl.BlockSpec((group, lat, head_v), lambda g, *_: (g, 0, 0)),
                whole,
            ],
            out_specs=[wide, whole],
        ),
        out_shape=[
            jax.ShapeDtypeStruct((req, new_len, heads * head_v), jnp.bfloat16),
            jax.ShapeDtypeStruct(new_rows.shape, jnp.bfloat16),
        ],
        compiler_params=pltpu.CompilerParams(
            dimension_semantics=("arbitrary",), vmem_limit_bytes=VMEM_BYTES
        ),
        name="merge",
    )(turns, got, got, own, mass, w_uv, new_rows)


def partner_pairs(pool_count, dev_count, which):
    return [
        (pool * dev_count + dev, partners(pool, dev)[which] * dev_count + dev)
        for pool in range(pool_count)
        for dev in range(dev_count)
    ]


def on_device(
    hidden,
    query_latent_rows,
    store,
    w_down,
    kv_gain,
    query_up_weight,
    w_uk,
    w_uv,
    prefix_pages,
    page_owner,
    page_slot,
    decode_order,
):
    pool_count = lax.axis_size("pool")
    dev_count = lax.axis_size("dev")
    column = lax.axis_index("dev")
    req_col, quarter, model_width = hidden.shape
    new_len = quarter * pool_count
    lat_dim = kv_gain.shape[0]
    key_dim = w_down.shape[1]
    nope_dim = w_uk.shape[1]
    rope_dim = key_dim - lat_dim
    first_row = column * req_col
    score_scale = (nope_dim + rope_dim) ** (-0.5)
    powers = np.exp(np.arange(rope_dim // 2) * (-2.0 * np.log(50000.0) / rope_dim))
    frequency = np.repeat(powers.astype(np.float32)[:, None], req_col * new_len, axis=1)

    near, far, passed, query, query_other, new_local, new_keys, table = exchange(
        prefix_pages,
        query_latent_rows.reshape(req_col * quarter, -1),
        hidden.reshape(req_col * quarter, model_width),
        kv_gain,
        page_owner.T,
        page_slot.T,
        jnp.asarray(frequency),
        store[0],
        w_down.T,
        query_up_weight,
        w_uk,
        req_col,
    )
    axes = ("pool", "dev")
    passed_far = lax.ppermute(far, axes, partner_pairs(pool_count, dev_count, 1))

    new = (new_keys,)
    common = dict(scale=score_scale, lat=lat_dim, new_len=new_len)
    early_blocks = [near, far, passed]
    state = attend(0, table, 0, early_blocks, query_other, new, "state", **common)
    part, part_mass = attend(
        1,
        table,
        dev_count + FORWARDED,
        [passed_far],
        query_other,
        state,
        "partner",
        **common,
    )
    got = lax.ppermute(part, axes, partner_pairs(pool_count, dev_count, 0))
    table, part_mass = lax.optimization_barrier((table, part_mass))
    own, own_mass = attend(
        2, table, 0, early_blocks + [passed_far], query, new, "own", w_uv=w_uv, **common
    )
    turns = lax.dynamic_slice_in_dim(decode_order, first_row, req_col) - first_row
    attended, handed = merge(
        turns, got, own, own_mass, w_uv, new_local.reshape(req_col, quarter, key_dim)
    )
    return (attended, handed)


def solution(mesh):
    in_specs = (
        P("dev", "pool", None),
        P("dev", "pool", None),
        P(("pool", "dev"), None, None, None),
        P(),
        P(),
        P(None, "pool"),
        P("pool", None, None),
        P("pool", None, None),
        P(),
        P(),
        P(),
        P(),
    )
    out_specs = (P("dev", None, "pool"), P("dev", "pool", None))
    return jax.shard_map(
        on_device, mesh=mesh, in_specs=in_specs, out_specs=out_specs, check_vma=False
    )
```

```python
import functools
import math

import jax
import jax.numpy as jnp
import numpy as np
from jax import lax
from jax.experimental import pallas as pl
from jax.experimental.pallas import tpu as pltpu
from jax.sharding import PartitionSpec as P

TILES = (8, 4, 8)
LOW = -1e30
FORWARDED = 20
VMEM_BYTES = 60 * 2**20
MESH = pl.DeviceIdType.MESH
STEPS = [
    (0, 1), (1, 0), (0, 3), (3, 0), (1, 1), (3, 3), (1, 3), (3, 1),
    (0, 2), (2, 0), (1, 2), (2, 1), (3, 2), (2, 3), (2, 2),
]
OFFSETS = [(0, 0, 0), (0, 0, 1)] + [(z, x, c) for z, x in STEPS for c in (0, 1)]


def shifted(dev, offset, sign):
    core, x, z = dev % 2, (dev // 2) % 4, dev // 8
    dz, dx, dc = offset
    return ((z + sign * dz + 4) % 4 * 4 + (x + sign * dx + 4) % 4) * 2 + (core + dc) % 2


def partners(pool, dev):
    near = pool + 1 - 2 * (pool % 2)
    far = 3 - pool
    odd = dev % 2
    return near + odd * (far - near), far + odd * (near - far)


def list_pages(pool, dev, key_partner, owners, table_ref, n_a, quarter):
    n_pairs = len(OFFSETS)
    width = 4 * n_pairs
    entries = owners.shape[1]
    entry = lax.broadcasted_iota(jnp.int32, (1, entries), 1)
    pair = lax.broadcasted_iota(jnp.int32, (2 * n_pairs, 1), 0)
    source = jnp.zeros((2 * n_pairs, 1), jnp.int32)
    for j, offset in enumerate(OFFSETS):
        source = jnp.where(pair % n_pairs == j, shifted(dev, offset, -1), source)
    source = source + n_pairs * jnp.where(pair < n_pairs, pool, key_partner)
    hit = owners == source
    head = jnp.min(jnp.where(hit, entry, entries), axis=1, keepdims=True)
    tail = jnp.max(jnp.where(hit, entry, -1), axis=1, keepdims=True)
    nobody = entries // 64
    low = head // 64
    high = jnp.where(tail > head, tail // 64, nobody)
    request = jnp.concatenate([low, high], axis=0)
    place = lax.broadcasted_iota(jnp.int32, (width, 1), 0)
    late = place % (2 * n_pairs) >= n_pairs + n_a
    lane = lax.broadcasted_iota(jnp.int32, (1, width), 1)
    rows = []
    for wanted in (jnp.logical_not(late), late, None):
        mine = request if wanted is None else jnp.where(wanted, request, nobody)
        key = (mine * width + place).astype(jnp.float32)
        key = jnp.broadcast_to(key, (width, width))
        rank = jnp.sum((key.T < key).astype(jnp.float32), axis=1, keepdims=True).astype(jnp.int32)
        rows.append(jnp.sum(jnp.where(rank == lane, place, 0), axis=0, keepdims=True))
        rows.append(jnp.sum((mine < lane).astype(jnp.int32), axis=0, keepdims=True))
    rows.append(
        jnp.where(lane < quarter, pool * quarter + lane, key_partner * quarter + lane - quarter)
    )
    for i, row in enumerate(rows):
        table_ref[i : i + 1, :] = row


def exchange_kernel(
    prefix_ref, ql_ref, hidden_ref, gain_ref, prefix_row, owner_ref, slot_ref, frequency_ref,
    store_ref, wd_ref, qup_ref, wuk_ref,
    arr_a, arr_b, pass_a, q_own, q_other, new_own, new_keys, table_ref,
    store_v, packed, ql_in, wd_v, qup_v, wuk_v, q_s, new_s, new_in, q_full, picks_v, picks,
    load_sem, ql_send, ql_recv, page_send, page_recv, pass_send, pass_recv, pair_send, pair_recv,
):
    pool, dev = lax.axis_index("pool"), lax.axis_index("dev")
    head_partner, key_partner = partners(pool, dev)
    req, key_dim, own_rows = q_s.shape
    heads, nope, lat = wuk_v.shape
    rope = key_dim - lat
    half_rope = rope // 2
    quarter = ql_in.shape[1] // req
    new_len = 4 * quarter
    page = store_v.shape[1]
    n_send = len(OFFSETS)
    n_a = arr_a.shape[0]

    load_store = pltpu.make_async_copy(store_ref, store_v, load_sem.at[6])
    load_store.start()
    loads = [
        pltpu.make_async_copy(wd_ref, wd_v, load_sem.at[0]),
        pltpu.make_async_copy(qup_ref, qup_v, load_sem.at[1]),
        pltpu.make_async_copy(wuk_ref, wuk_v, load_sem.at[2]),
    ]
    for copy in loads:
        copy.start()

    barrier = pltpu.get_barrier_semaphore()
    for offset in OFFSETS[1:]:
        pl.semaphore_signal(
            barrier, inc=1, device_id=(pool, shifted(dev, offset, 1)), device_id_type=MESH
        )
    for step in range(1, 4):
        pl.semaphore_signal(
            barrier, inc=1, device_id=((pool + step) % 4, dev), device_id_type=MESH
        )

    prefix = prefix_row[...][None, :]
    owners = owner_ref[...]
    page_of = lax.broadcasted_iota(jnp.int32, owners.shape, 0)
    lane_of = lax.broadcasted_iota(jnp.int32, owners.shape, 1)
    n_slots, max_pages = store_v.shape[0], owners.shape[0]
    used = page_of < prefix
    mine = used & (owners == pool * n_send + dev)
    code = (lane_of % req * max_pages + page_of) * n_slots + slot_ref[...]
    low = jnp.min(jnp.where(mine, code, req * max_pages * n_slots), axis=0, keepdims=True)
    high = jnp.max(jnp.where(mine, code, 0), axis=0, keepdims=True)
    n_lanes = owners.shape[1]
    for step in (1, 2):
        low = jnp.minimum(low, pltpu.roll(low, n_lanes - step, 1))
        high = jnp.maximum(high, pltpu.roll(high, n_lanes - step, 1))
    picks_v[0:1, :] = low % n_slots
    picks_v[1:2, :] = high % n_slots
    load_picks = pltpu.make_async_copy(picks_v, picks, load_sem.at[7])
    load_picks.start()

    def pack(j):
        target = shifted(dev, OFFSETS[j], 1)
        pages = [store_v[picks[k, req * target]] for k in range(2)]
        for k in range(2):
            packed[j, k * page : (k + 1) * page, :] = pages[k][:, :lat]
        keys = jnp.concatenate([p[:, lat:] for p in pages], axis=1)
        step = page * 2 * rope // lat
        packed[j, 2 * page :, :] = jnp.concatenate(
            [keys[i * step : (i + 1) * step] for i in range(page // step)], axis=1
        )

    load_picks.wait()
    load_store.wait()
    for j in (0, 1):
        pack(j)
    pl.semaphore_wait(barrier, n_send - 1 + 3)

    def remote(src, dst, send, recv, target):
        return pltpu.make_async_remote_copy(
            src_ref=src, dst_ref=dst, send_sem=send, recv_sem=recv, device_id=target, device_id_type=MESH
        )

    ql_sends = [
        remote(ql_ref, ql_in.at[pool], ql_send.at[s - 1], ql_recv.at[s - 1], ((pool + s) % 4, dev))
        for s in range(1, 4)
    ]
    ql_gets = [
        remote(
            ql_ref, ql_in.at[(pool + 4 - s) % 4], ql_send.at[s - 1], ql_recv.at[s - 1], (head_partner, dev)
        )
        for s in range(1, 4)
    ]
    for copy in ql_sends:
        copy.start()

    def landing(j):
        return arr_a.at[j] if j < n_a else arr_b.at[j - n_a]

    passes = [
        remote(
            packed.at[0] if j == 0 else arr_a.at[j],
            pass_a.at[j],
            pass_send.at[j],
            pass_recv.at[j],
            (key_partner, dev),
        )
        for j in range(n_a)
    ]
    sends = [None] * n_send
    for j in range(1, n_send):
        if j > 1:
            pack(j)
        copy = remote(
            packed.at[j],
            landing(j),
            page_send.at[j],
            page_recv.at[j],
            (pool, shifted(dev, OFFSETS[j], 1)),
        )
        copy.start()
        sends[j] = copy
        if j == 1:
            passes[0].start()
    own_pages = pltpu.make_async_copy(packed.at[0], arr_a.at[0], load_sem.at[3])
    own_pages.start()

    def pass_on(first, last):
        for j in range(first, last):
            sends[j].wait_recv()
            if j < n_a:
                passes[j].start()

    pass_on(1, 2)
    frequency = frequency_ref[...]
    lane = lax.broadcasted_iota(jnp.int32, (1, frequency.shape[1]), 1)
    position = pool * quarter + lane % quarter
    local_position = position
    position = lane % new_len
    for r in range(req):
        begin = prefix_ref[req * dev + r] * page
        local_position = local_position + jnp.where(lane // quarter == r, begin, 0)
        position = position + jnp.where(lane // new_len == r, begin, 0)
    local_angles = (frequency * local_position.astype(jnp.float32))[:, : req * quarter]
    angles = frequency * position.astype(jnp.float32)

    loads[0].wait()
    projected = lax.dot_general(
        wd_v[...], hidden_ref[...], (((1,), (1,)), ((), ())), preferred_element_type=jnp.float32
    )
    latent = projected[:lat]
    latent = latent * lax.rsqrt(jnp.mean(latent * latent, axis=0, keepdims=True) + 1e-06)
    first, second = projected[lat : lat + half_rope], projected[lat + half_rope :]
    lcos, lsin = jnp.cos(local_angles), jnp.sin(local_angles)
    rotated = jnp.concatenate([first * lcos - second * lsin, first * lsin + second * lcos], axis=0)
    new_s[...] = jnp.concatenate(
        [latent.T * gain_ref[...].astype(jnp.float32)[None, :], rotated.T], axis=1
    ).astype(jnp.bfloat16)
    new_send = remote(new_s, new_in, pair_send.at[0], pair_recv.at[0], (key_partner, dev))
    new_send.start()
    new_keep = pltpu.make_async_copy(new_s, new_own, load_sem.at[4])
    new_keep.start()
    pass_on(2, 4)
    own = jnp.where(used, owners, -1).astype(jnp.float32)
    own = pltpu.roll(own, (n_lanes - req * dev) % n_lanes, 1)
    own = jnp.concatenate([own, jnp.zeros((n_lanes - max_pages, n_lanes), jnp.float32)], axis=0).T
    own = jnp.concatenate([own[r : r + 1, :max_pages] for r in range(req)], axis=1)
    list_pages(pool, dev, key_partner, own.astype(jnp.int32), table_ref, n_a, quarter)

    ql_in[pool] = ql_ref[...]
    for copy in ql_gets:
        copy.wait_recv()
    for y in range(4):
        rows = ql_in[y].astype(jnp.float32)
        for r in range(req):
            q_full[pl.ds(r * new_len + y * quarter, quarter), :] = rows[
                r * quarter : (r + 1) * quarter
            ]
    for copy in loads[1:]:
        copy.wait()
    group = 128 // new_len
    width = nope + rope

    cos, sin = jnp.cos(angles), jnp.sin(angles)

    def project(g):
        raw = jnp.dot(
            q_full[...].astype(jnp.bfloat16),
            qup_v[:, g * group * width : (g + 1) * group * width],
            preferred_element_type=jnp.float32,
        ).T
        built = []
        for j in range(group):
            at = j * width
            q_nope = raw[at : at + nope].astype(jnp.bfloat16)
            q_abs = lax.dot_general(
                wuk_v[g * group + j],
                q_nope,
                (((0,), (0,)), ((), ())),
                preferred_element_type=jnp.float32,
            )
            x = raw[at + nope : at + nope + half_rope]
            y = raw[at + nope + half_rope : at + width]
            built.append(
                jnp.concatenate([q_abs, x * cos - y * sin, x * sin + y * cos], axis=0).astype(
                    jnp.bfloat16
                )
            )
        for r in range(req):
            q_s[r, :, g * 128 : (g + 1) * 128] = jnp.concatenate(
                [b[:, r * new_len : (r + 1) * new_len] for b in built], axis=1
            )

    done = 4
    for g in range(heads // group):
        project(g)
        if g < heads // group - 1:
            pass_on(done, done + 2)
            done += 2

    q_send = remote(q_s, q_other, pair_send.at[1], pair_recv.at[1], (head_partner, dev))
    q_send.start()
    q_keep = pltpu.make_async_copy(q_s, q_own, load_sem.at[5])
    q_keep.start()

    pass_on(done, n_send)
    for copy in ql_sends:
        copy.wait_send()
    for copy in sends[1:]:
        copy.wait_send()
    own_pages.wait()
    new_keep.wait()
    q_keep.wait()
    new_send.wait()
    own_new, got_new = new_s[...].astype(jnp.float32), new_in[...].astype(jnp.float32)
    for r in range(req):
        rows = slice(r * quarter, (r + 1) * quarter)
        new_keys[r] = jnp.concatenate([own_new[rows], got_new[rows]], axis=0).astype(jnp.bfloat16)
    q_send.wait()
    for copy in passes:
        copy.wait()


def exchange(prefix, ql, hidden, gain, owner_t, slot_t, frequency, store, wd, qup, wuk, req):
    n_cols = prefix.shape[0] // req
    n_slots, page, key_dim = store.shape
    heads, nope, lat = wuk.shape
    tokens = ql.shape[0]
    new_len = 4 * tokens // req
    bf16 = jnp.bfloat16
    any_spec = pl.BlockSpec(memory_space=pl.ANY)
    vmem = pl.BlockSpec(memory_space=pltpu.VMEM)
    own_rows = heads * new_len
    pair = (2 * page * key_dim // lat, lat)
    query = jax.ShapeDtypeStruct((req, key_dim, own_rows), bf16)
    new = jax.ShapeDtypeStruct((tokens, key_dim), bf16)
    near = jax.ShapeDtypeStruct((FORWARDED,) + pair, bf16)
    far = jax.ShapeDtypeStruct((n_cols - FORWARDED,) + pair, bf16)
    dma = pltpu.SemaphoreType.DMA
    return pl.pallas_call(
        exchange_kernel,
        in_specs=[pl.BlockSpec(memory_space=pltpu.SMEM)] + [vmem] * 7 + [any_spec] * 4,
        out_specs=[any_spec] * 6 + [vmem] * 2,
        out_shape=[
            near,
            far,
            near,
            query,
            query,
            new,
            jax.ShapeDtypeStruct((req, 2 * tokens // req, key_dim), bf16),
            jax.ShapeDtypeStruct((8, 4 * n_cols), jnp.int32),
        ],
        scratch_shapes=[
            pltpu.VMEM(store.shape, bf16),
            pltpu.VMEM((n_cols,) + pair, bf16),
            pltpu.VMEM((4,) + ql.shape, bf16),
            pltpu.VMEM(wd.shape, bf16),
            pltpu.VMEM(qup.shape, bf16),
            pltpu.VMEM(wuk.shape, bf16),
            pltpu.VMEM(query.shape, bf16),
            pltpu.VMEM(new.shape, bf16),
            pltpu.VMEM(new.shape, bf16),
            pltpu.VMEM((req * new_len, ql.shape[1]), jnp.float32),
            pltpu.VMEM((2, prefix.shape[0]), jnp.int32),
            pltpu.SMEM((2, prefix.shape[0]), jnp.int32),
            dma((8,)),
            dma((3,)),
            dma((3,)),
            dma((n_cols,)),
            dma((n_cols,)),
            dma((FORWARDED,)),
            dma((FORWARDED,)),
            dma((2,)),
            dma((2,)),
        ],
        compiler_params=pltpu.CompilerParams(
            collective_id=1, has_side_effects=True, vmem_limit_bytes=VMEM_BYTES
        ),
        cost_estimate=pl.CostEstimate(flops=10**10, bytes_accessed=10**8, transcendentals=0),
        name="exchange",
    )(prefix, ql, hidden, gain, prefix, owner_t, slot_t, frequency, store, wd, qup, wuk)


def gather_rows(parts, first, last):
    return jnp.concatenate([part[first:last] for part in parts], axis=0)


def attention_step(table_ref, *refs, call, sizes, base, first, kind, scale, page, new_len):
    n_blocks = len(sizes)
    blocks, refs = refs[:n_blocks], refs[n_blocks:]
    q_ref, refs = refs[0], refs[1:]
    n_inputs = 1 if first else 2
    inputs, refs = refs[:n_inputs], refs[n_inputs:]
    if kind == "own":
        wuv_ref, refs = refs[0], refs[1:]
    result, mass, refs = refs[0], refs[1], refs[2:]
    pairs, sem, even, odd, even_keys, odd_keys, query = refs[:7]
    acc = result.at[0] if kind == "state" else refs[7]
    lat, rows = acc.shape
    request = pl.program_id(0)

    copies, at = [], 0
    for i, block in enumerate(blocks):
        copies.append(pltpu.make_async_copy(block, pairs.at[pl.ds(at, sizes[i])], sem.at[i]))
        at += sizes[i]

    @pl.when(request == 0)
    def _():
        for copy in copies:
            copy.start()

    tile_slots = TILES[call]
    factor = scale * math.log2(math.e)
    rope = q_ref.shape[1] - lat
    pad = 128 - rope
    bias_rows = jnp.where(
        lax.broadcasted_iota(jnp.int32, (pad, rows), 0) == 0, 1.0, 0.0
    ).astype(jnp.bfloat16)
    key_lane = lax.broadcasted_iota(jnp.int32, (page, pad), 1)

    query[: lat + rope, :] = q_ref[0]
    query[lat + rope :, :] = bias_rows

    def weigh(keys, weights):
        return lax.dot_general(
            keys, weights, (((0,), (0,)), ((), ())), preferred_element_type=jnp.float32
        )

    if first:
        new_keys = inputs[0][0]
        quarter = new_keys.shape[0] // 2
        row = lax.broadcasted_iota(jnp.int32, (2 * quarter, 1), 0)
        new_pos = jnp.where(row < quarter, table_ref[6, 0] + row, table_ref[6, quarter] + row - quarter)
        score = jnp.dot(new_keys, q_ref[0], preferred_element_type=jnp.float32)
        token = lax.broadcasted_iota(jnp.int32, score.shape, 1) % new_len
        live = new_pos <= token
        score = jnp.where(live, score, LOW)
        top = jnp.max(score, axis=0, keepdims=True)
        weights = jnp.where(live, jnp.exp2((score - top) * factor), 0.0)
        total = jnp.sum(weights, axis=0, keepdims=True)
        acc[...] = weigh(new_keys[:, :lat], weights.astype(jnp.bfloat16))
    else:
        acc_in, mass_in = inputs
        top, total = mass_in[0, 0:1, :], mass_in[0, 1:2, :]
        acc[...] = acc_in[0]

    @pl.when(request == 0)
    def _():
        for copy in copies:
            copy.wait()

    begin = table_ref[2 * call + 1, request]
    end = table_ref[2 * call + 1, request + 1]
    tiles = (end - begin + tile_slots - 1) // tile_slots

    def fetch(tile, keys, sheet):
        for g in range(tile_slots):
            spot = begin + tile * tile_slots + g
            index = table_ref[2 * call, jnp.maximum(jnp.minimum(spot, end - 1), 0)]
            half = table_ref.shape[1] // 2
            pair, turn = index % half - base, index // half
            rows = slice(g * page, (g + 1) * page)
            keys[rows, :lat] = pairs[pair, pl.ds(pl.multiple_of(turn * page, page), page), :]
            both = pairs[pair, pl.ds(2 * page, 2 * page * rope // lat), :]
            both = jnp.concatenate([both[:, i * 128 : (i + 1) * 128] for i in range(lat // 128)], axis=0)
            rotary = jnp.where(turn == 0, both[:, :rope], both[:, rope:])
            bias = jnp.where((key_lane == 0) & (spot >= end), LOW, 0.0).astype(jnp.bfloat16)
            keys[rows, lat:] = jnp.concatenate([rotary, bias], axis=1)
        sheet[...] = jnp.dot(keys[...], query[...], preferred_element_type=jnp.float32)

    def take(sheet, keys, top, total):
        score = sheet[...]
        new_top = jnp.maximum(top, jnp.max(score, axis=0, keepdims=True))
        shrink = jnp.exp2((top - new_top) * factor)
        weights = jnp.exp2((score - new_top) * factor)
        total = total * shrink + jnp.sum(weights, axis=0, keepdims=True)
        acc[...] = acc[...] * shrink + weigh(keys[:, :lat], weights.astype(jnp.bfloat16))
        return new_top, total

    @pl.when(tiles > 0)
    def _():
        fetch(0, even_keys, even)

    def body(step, carry):
        tile = 2 * step
        fetch(tile + 1, odd_keys, odd)
        carry = take(even, even_keys, *carry)
        fetch(jnp.minimum(tile + 2, tiles - 1), even_keys, even)
        return take(odd, odd_keys, *carry)

    carry = lax.fori_loop(0, tiles // 2, body, (top, total))
    top, total = lax.cond(
        tiles % 2 == 1,
        lambda c: take(even, even_keys, *c),
        lambda c: c,
        carry,
    )

    if kind == "state":
        mass[0, 0:1, :] = top
        mass[0, 1:2, :] = total
        return
    live = total > 0
    inverse = jnp.where(live, 1.0 / total, 0.0)
    log_mass = jnp.where(live, top * factor + jnp.log(total) * math.log2(math.e), LOW)
    mass[request] = log_mass
    mixed = (acc[...] * inverse).T
    high = mixed.astype(jnp.bfloat16)
    if kind == "partner":
        result[0, :rows, :] = high
        terms, rest = [], log_mass
        for _ in range(3):
            terms.append(rest.astype(jnp.bfloat16).astype(jnp.float32))
            rest = rest - terms[-1]
        row = lax.broadcasted_iota(jnp.int32, (16, rows), 0)
        tail = jnp.where(row == 2, terms[2], 0.0)
        tail = jnp.where(row == 0, terms[0], jnp.where(row == 1, terms[1], tail))
        result[0, rows:, :] = tail.astype(jnp.bfloat16)
    else:
        high_v, low_v = refs[8], refs[9]
        high_v[request] = high
        low_v[request] = (mixed - high.astype(jnp.float32)).astype(jnp.bfloat16)

    if kind == "own":

        @pl.when(request == pl.num_programs(0) - 1)
        def _():
            req = high_v.shape[0]
            head_v = wuv_ref.shape[2]
            for head in range(wuv_ref.shape[0]):
                first_row, last_row = head * new_len, (head + 1) * new_len
                total = None
                for part in (high_v, low_v):
                    rows_of = gather_rows([part.at[r] for r in range(req)], first_row, last_row)
                    term = jnp.dot(rows_of, wuv_ref[head], preferred_element_type=jnp.float32)
                    total = term if total is None else total + term
                for r in range(req):
                    result[r, :, head * head_v : (head + 1) * head_v] = total[
                        r * new_len : (r + 1) * new_len
                    ]


def attend(call, table, base, blocks, query, inputs, kind, scale, lat, new_len, w_uv=None):
    first = inputs[0].dtype == jnp.bfloat16
    req, key_dim, rows = query.shape
    sizes = [b.shape[0] for b in blocks]
    count = sum(sizes)
    page = blocks[0].shape[1] * lat // key_dim // 2
    kernel = functools.partial(
        attention_step, call=call, sizes=sizes, base=base, first=first, kind=kind, scale=scale, page=page, new_len=new_len
    )
    acc_spec = pl.BlockSpec((1, lat, rows), lambda r, *_: (r, 0, 0))
    mass_spec = pl.BlockSpec((1, 2, rows), lambda r, *_: (r, 0, 0))
    in_specs = [pl.BlockSpec(memory_space=pl.ANY)] * len(blocks)
    in_specs += [pl.BlockSpec((1, key_dim, rows), lambda r, *_: (r, 0, 0))]
    if first:
        in_specs += [pl.BlockSpec((1,) + inputs[0].shape[1:], lambda r, *_: (r, 0, 0))]
    else:
        in_specs += [acc_spec, mass_spec]
    scratch = [
        pltpu.VMEM((count,) + blocks[0].shape[1:], jnp.bfloat16),
        pltpu.SemaphoreType.DMA((len(blocks),)),
        pltpu.VMEM((TILES[call] * page, rows), jnp.float32),
        pltpu.VMEM((TILES[call] * page, rows), jnp.float32),
        pltpu.VMEM((TILES[call] * page, lat + 128), jnp.bfloat16),
        pltpu.VMEM((TILES[call] * page, lat + 128), jnp.bfloat16),
        pltpu.VMEM((lat + 128, rows), jnp.bfloat16),
    ]
    if kind == "state":
        out_specs = [acc_spec, mass_spec]
        out_shape = [
            jax.ShapeDtypeStruct((req, lat, rows), jnp.float32),
            jax.ShapeDtypeStruct((req, 2, rows), jnp.float32),
        ]
    else:
        scratch.append(pltpu.VMEM((lat, rows), jnp.float32))
        out_specs = [None, pl.BlockSpec((req, 1, rows), lambda r, *_: (0, 0, 0))]
        out_shape = [None, jax.ShapeDtypeStruct((req, 1, rows), jnp.float32)]
        if kind == "partner":
            out_specs[0] = pl.BlockSpec((1, rows + 16, lat), lambda r, *_: (r, 0, 0))
            out_shape[0] = jax.ShapeDtypeStruct((req, rows + 16, lat), jnp.bfloat16)
        else:
            heads, _, head_v = w_uv.shape
            in_specs.append(pl.BlockSpec(w_uv.shape, lambda r, *_: (0, 0, 0)))
            scratch += [pltpu.VMEM((req, lat, rows), jnp.bfloat16)] * 2
            out_specs[0] = pl.BlockSpec((req, new_len, heads * head_v), lambda r, *_: (0, 0, 0))
            out_shape[0] = jax.ShapeDtypeStruct((req, new_len, heads * head_v), jnp.float32)
    more = [w_uv] if kind == "own" else []
    return pl.pallas_call(
        kernel,
        grid_spec=pltpu.PrefetchScalarGridSpec(
            num_scalar_prefetch=1,
            grid=(req,),
            in_specs=in_specs,
            out_specs=out_specs,
            scratch_shapes=scratch,
        ),
        out_shape=out_shape,
        compiler_params=pltpu.CompilerParams(
            dimension_semantics=("arbitrary",), vmem_limit_bytes=VMEM_BYTES
        ),
        cost_estimate=pl.CostEstimate(
            flops=8 * rows * count * page * (key_dim + lat),
            bytes_accessed=4 * req * lat * rows * 2 + count * page * key_dim * 2,
            transcendentals=2 * rows * count * page,
        ),
        name=f"attend_{call}_{kind}",
    )(table, *blocks, query, *inputs, *more)


def merge_step(turn_ref, got_ref, got_mass_ref, own_ref, mass_ref, wuv_ref, new_ref, out_ref, handed_ref):
    req, width, lat = got_ref.shape
    group, _, head_v = wuv_ref.shape
    new_len = width // group

    @pl.when(pl.program_id(0) == 0)
    def _():
        for i in range(req):
            handed_ref[i] = new_ref[turn_ref[i]]

    shares = []
    for r in range(req):
        tail = got_mass_ref[r].astype(jnp.float32)
        got_mass = tail[0:1] + tail[1:2] + tail[2:3]
        share = 1.0 / (1.0 + jnp.exp2(mass_ref[r] - got_mass))
        shares.append(jnp.broadcast_to(share, (width, width)).T)
    for j in range(group):
        first, last = j * new_len, (j + 1) * new_len
        rows = gather_rows([got_ref.at[r] for r in range(req)], first, last)
        got = jnp.dot(rows, wuv_ref[j], preferred_element_type=jnp.float32)
        lanes = slice(j * head_v, (j + 1) * head_v)
        for r in range(req):
            share = shares[r][first:last]
            own = own_ref[r, :, lanes]
            out_ref[r, :, lanes] = (
                own * (1.0 - share) + got[r * new_len : (r + 1) * new_len] * share
            ).astype(jnp.bfloat16)


def merge(turns, got, own, mass, w_uv, new_rows):
    req, deep, lat = got.shape
    heads, _, head_v = w_uv.shape
    groups = (deep - 16) // 128
    group = heads // groups
    new_len = 128 // group
    wide = pl.BlockSpec((req, new_len, group * head_v), lambda g, *_: (0, 0, g))
    whole = pl.BlockSpec(new_rows.shape, lambda g, *_: (0, 0, 0))
    return pl.pallas_call(
        merge_step,
        grid_spec=pltpu.PrefetchScalarGridSpec(
            num_scalar_prefetch=1,
            grid=(groups,),
            in_specs=[
                pl.BlockSpec((req, 128, lat), lambda g, *_: (0, g, 0)),
                pl.BlockSpec((req, 16, 128), lambda g, *_: (0, (deep - 16) // 16, g)),
                wide,
                pl.BlockSpec((req, 1, 128), lambda g, *_: (0, 0, g)),
                pl.BlockSpec((group, lat, head_v), lambda g, *_: (g, 0, 0)),
                whole,
            ],
            out_specs=[wide, whole],
        ),
        out_shape=[
            jax.ShapeDtypeStruct((req, new_len, heads * head_v), jnp.bfloat16),
            jax.ShapeDtypeStruct(new_rows.shape, jnp.bfloat16),
        ],
        compiler_params=pltpu.CompilerParams(
            dimension_semantics=("arbitrary",), vmem_limit_bytes=VMEM_BYTES
        ),
        name="merge",
    )(turns, got, got, own, mass, w_uv, new_rows)


def partner_pairs(pool_count, dev_count, which):
    return [
        (pool * dev_count + dev, partners(pool, dev)[which] * dev_count + dev)
        for pool in range(pool_count)
        for dev in range(dev_count)
    ]


def on_device(
    hidden,
    query_latent_rows,
    store,
    w_down,
    kv_gain,
    query_up_weight,
    w_uk,
    w_uv,
    prefix_pages,
    page_owner,
    page_slot,
    decode_order,
):
    pool_count = lax.axis_size("pool")
    dev_count = lax.axis_size("dev")
    column = lax.axis_index("dev")
    req_col, quarter, model_width = hidden.shape
    new_len = quarter * pool_count
    lat_dim = kv_gain.shape[0]
    key_dim = w_down.shape[1]
    nope_dim = w_uk.shape[1]
    rope_dim = key_dim - lat_dim
    first_row = column * req_col
    score_scale = (nope_dim + rope_dim) ** (-0.5)
    powers = np.exp(np.arange(rope_dim // 2) * (-2.0 * np.log(50000.0) / rope_dim))
    frequency = np.repeat(powers.astype(np.float32)[:, None], req_col * new_len, axis=1)

    near, far, passed, query, query_other, new_local, new_keys, table = exchange(
        prefix_pages,
        query_latent_rows.reshape(req_col * quarter, -1),
        hidden.reshape(req_col * quarter, model_width),
        kv_gain,
        page_owner.T,
        page_slot.T,
        jnp.asarray(frequency),
        store[0],
        w_down.T,
        query_up_weight,
        w_uk,
        req_col,
    )
    axes = ("pool", "dev")
    passed_far = lax.ppermute(far, axes, partner_pairs(pool_count, dev_count, 1))

    new = (new_keys,)
    common = dict(scale=score_scale, lat=lat_dim, new_len=new_len)
    early_blocks = [near, far, passed]
    state = attend(0, table, 0, early_blocks, query_other, new, "state", **common)
    part, part_mass = attend(
        1,
        table,
        dev_count + FORWARDED,
        [passed_far],
        query_other,
        state,
        "partner",
        **common,
    )
    got = lax.ppermute(part, axes, partner_pairs(pool_count, dev_count, 0))
    table, part_mass = lax.optimization_barrier((table, part_mass))
    own, own_mass = attend(
        2, table, 0, early_blocks + [passed_far], query, new, "own", w_uv=w_uv, **common
    )
    turns = lax.dynamic_slice_in_dim(decode_order, first_row, req_col) - first_row
    attended, handed = merge(
        turns, got, own, own_mass, w_uv, new_local.reshape(req_col, quarter, key_dim)
    )
    return (attended, handed)


def solution(mesh):
    in_specs = (
        P("dev", "pool", None),
        P("dev", "pool", None),
        P(("pool", "dev"), None, None, None),
        P(),
        P(),
        P(None, "pool"),
        P("pool", None, None),
        P("pool", None, None),
        P(),
        P(),
        P(),
        P(),
    )
    out_specs = (P("dev", None, "pool"), P("dev", "pool", None))
    return jax.shard_map(
        on_device, mesh=mesh, in_specs=in_specs, out_specs=out_specs, check_vma=False
    )
```

```python
import functools
import math

import jax
import jax.numpy as jnp
import numpy as np
from jax import lax
from jax.experimental import pallas as pl
from jax.experimental.pallas import tpu as pltpu
from jax.sharding import PartitionSpec as P

TILES = (8, 4, 8)
LOW = -1e30
FORWARDED = 20
VMEM_BYTES = (24 * 2**20, 24 * 2**20, 32 * 2**20)
MESH = pl.DeviceIdType.MESH
STEPS = [
    (0, 1), (1, 0), (0, 3), (3, 0), (1, 1), (3, 3), (1, 3), (3, 1),
    (0, 2), (2, 0), (1, 2), (2, 1), (3, 2), (2, 3), (2, 2),
]
OFFSETS = [(0, 0, 0), (0, 0, 1)] + [(z, x, c) for z, x in STEPS for c in (0, 1)]


def shifted(dev, offset, sign):
    core, x, z = dev % 2, (dev // 2) % 4, dev // 8
    dz, dx, dc = offset
    return ((z + sign * dz + 4) % 4 * 4 + (x + sign * dx + 4) % 4) * 2 + (core + dc) % 2


def partners(pool, dev):
    near = pool + 1 - 2 * (pool % 2)
    far = 3 - pool
    odd = dev % 2
    return near + odd * (far - near), far + odd * (near - far)


def list_pages(pool, dev, key_partner, owners, table_ref, n_a, quarter):
    n_pairs = len(OFFSETS)
    width = 4 * n_pairs
    entries = owners.shape[1]
    entry = lax.broadcasted_iota(jnp.int32, (1, entries), 1)
    pair = lax.broadcasted_iota(jnp.int32, (2 * n_pairs, 1), 0)
    source = jnp.zeros((2 * n_pairs, 1), jnp.int32)
    for j, offset in enumerate(OFFSETS):
        source = jnp.where(pair % n_pairs == j, shifted(dev, offset, -1), source)
    source = source + n_pairs * jnp.where(pair < n_pairs, pool, key_partner)
    hit = owners == source
    head = jnp.min(jnp.where(hit, entry, entries), axis=1, keepdims=True)
    tail = jnp.max(jnp.where(hit, entry, -1), axis=1, keepdims=True)
    nobody = entries // 64
    low = head // 64
    high = jnp.where(tail > head, tail // 64, nobody)
    request = jnp.concatenate([low, high], axis=0)
    place = lax.broadcasted_iota(jnp.int32, (width, 1), 0)
    late = place % (2 * n_pairs) >= n_pairs + n_a
    lane = lax.broadcasted_iota(jnp.int32, (1, width), 1)
    rows = []
    for wanted in (jnp.logical_not(late), late, None):
        mine = request if wanted is None else jnp.where(wanted, request, nobody)
        key = (mine * width + place).astype(jnp.float32)
        key = jnp.broadcast_to(key, (width, width))
        rank = jnp.sum((key.T < key).astype(jnp.float32), axis=1, keepdims=True).astype(jnp.int32)
        rows.append(jnp.sum(jnp.where(rank == lane, place, 0), axis=0, keepdims=True))
        rows.append(jnp.sum((mine < lane).astype(jnp.int32), axis=0, keepdims=True))
    rows.append(
        jnp.where(lane < quarter, pool * quarter + lane, key_partner * quarter + lane - quarter)
    )
    for i, row in enumerate(rows):
        table_ref[i : i + 1, :] = row


def exchange_kernel(
    prefix_ref, ql_ref, hidden_ref, gain_ref, prefix_row, owner_ref, slot_ref, frequency_ref,
    store_ref, wd_ref, qup_ref, wuk_ref,
    arr_a, arr_b, pass_a, q_own, q_other, new_own, new_keys, table_ref,
    store_v, packed, ql_in, wd_v, qup_v, wuk_v, q_s, new_s, new_in, q_full, picks_v, picks,
    load_sem, ql_send, ql_recv, page_send, page_recv, pass_send, pass_recv, pair_send, pair_recv,
):
    pool, dev = lax.axis_index("pool"), lax.axis_index("dev")
    head_partner, key_partner = partners(pool, dev)
    req, key_dim, own_rows = q_s.shape
    heads, nope, lat = wuk_v.shape
    rope = key_dim - lat
    half_rope = rope // 2
    quarter = ql_in.shape[1] // req
    new_len = 4 * quarter
    page = store_v.shape[1]
    n_send = len(OFFSETS)
    n_a = arr_a.shape[0]

    load_store = pltpu.make_async_copy(store_ref, store_v, load_sem.at[6])
    load_store.start()
    loads = [
        pltpu.make_async_copy(wd_ref, wd_v, load_sem.at[0]),
        pltpu.make_async_copy(qup_ref, qup_v, load_sem.at[1]),
        pltpu.make_async_copy(wuk_ref, wuk_v, load_sem.at[2]),
    ]
    for copy in loads:
        copy.start()

    barrier = pltpu.get_barrier_semaphore()
    for offset in OFFSETS[1:]:
        pl.semaphore_signal(
            barrier, inc=1, device_id=(pool, shifted(dev, offset, 1)), device_id_type=MESH
        )
    for step in range(1, 4):
        pl.semaphore_signal(
            barrier, inc=1, device_id=((pool + step) % 4, dev), device_id_type=MESH
        )

    prefix = prefix_row[...][None, :]
    owners = owner_ref[...]
    page_of = lax.broadcasted_iota(jnp.int32, owners.shape, 0)
    lane_of = lax.broadcasted_iota(jnp.int32, owners.shape, 1)
    n_slots, max_pages = store_v.shape[0], owners.shape[0]
    used = page_of < prefix
    mine = used & (owners == pool * n_send + dev)
    code = (lane_of % req * max_pages + page_of) * n_slots + slot_ref[...]
    low = jnp.min(jnp.where(mine, code, req * max_pages * n_slots), axis=0, keepdims=True)
    high = jnp.max(jnp.where(mine, code, 0), axis=0, keepdims=True)
    n_lanes = owners.shape[1]
    for step in (1, 2):
        low = jnp.minimum(low, pltpu.roll(low, n_lanes - step, 1))
        high = jnp.maximum(high, pltpu.roll(high, n_lanes - step, 1))
    picks_v[0:1, :] = low % n_slots
    picks_v[1:2, :] = high % n_slots
    load_picks = pltpu.make_async_copy(picks_v, picks, load_sem.at[7])
    load_picks.start()

    def pack(j):
        target = shifted(dev, OFFSETS[j], 1)
        pages = [store_v[picks[k, req * target]] for k in range(2)]
        for k in range(2):
            packed[j, k * page : (k + 1) * page, :] = pages[k][:, :lat]
        keys = jnp.concatenate([p[:, lat:] for p in pages], axis=1)
        step = page * 2 * rope // lat
        packed[j, 2 * page :, :] = jnp.concatenate(
            [keys[i * step : (i + 1) * step] for i in range(page // step)], axis=1
        )

    load_picks.wait()
    load_store.wait()
    for j in (0, 1):
        pack(j)
    pl.semaphore_wait(barrier, n_send - 1 + 3)

    def remote(src, dst, send, recv, target):
        return pltpu.make_async_remote_copy(
            src_ref=src, dst_ref=dst, send_sem=send, recv_sem=recv, device_id=target, device_id_type=MESH
        )

    ql_sends = [
        remote(ql_ref, ql_in.at[pool], ql_send.at[s - 1], ql_recv.at[s - 1], ((pool + s) % 4, dev))
        for s in range(1, 4)
    ]
    ql_gets = [
        remote(
            ql_ref, ql_in.at[(pool + 4 - s) % 4], ql_send.at[s - 1], ql_recv.at[s - 1], (head_partner, dev)
        )
        for s in range(1, 4)
    ]
    for copy in ql_sends:
        copy.start()

    def landing(j):
        return arr_a.at[j] if j < n_a else arr_b.at[j - n_a]

    passes = [
        remote(
            packed.at[0] if j == 0 else arr_a.at[j],
            pass_a.at[j],
            pass_send.at[j],
            pass_recv.at[j],
            (key_partner, dev),
        )
        for j in range(n_a)
    ]
    sends = [None] * n_send
    for j in range(1, n_send):
        if j > 1:
            pack(j)
        copy = remote(
            packed.at[j],
            landing(j),
            page_send.at[j],
            page_recv.at[j],
            (pool, shifted(dev, OFFSETS[j], 1)),
        )
        copy.start()
        sends[j] = copy
        if j == 1:
            passes[0].start()
    own_pages = pltpu.make_async_copy(packed.at[0], arr_a.at[0], load_sem.at[3])
    own_pages.start()

    def pass_on(first, last):
        for j in range(first, last):
            sends[j].wait_recv()
            if j < n_a:
                passes[j].start()

    pass_on(1, 2)
    frequency = frequency_ref[...]
    lane = lax.broadcasted_iota(jnp.int32, (1, frequency.shape[1]), 1)
    position = pool * quarter + lane % quarter
    local_position = position
    position = lane % new_len
    for r in range(req):
        begin = prefix_ref[req * dev + r] * page
        local_position = local_position + jnp.where(lane // quarter == r, begin, 0)
        position = position + jnp.where(lane // new_len == r, begin, 0)
    local_angles = (frequency * local_position.astype(jnp.float32))[:, : req * quarter]
    angles = frequency * position.astype(jnp.float32)

    loads[0].wait()
    projected = lax.dot_general(
        wd_v[...], hidden_ref[...], (((1,), (1,)), ((), ())), preferred_element_type=jnp.float32
    )
    latent = projected[:lat]
    latent = latent * lax.rsqrt(jnp.mean(latent * latent, axis=0, keepdims=True) + 1e-06)
    first, second = projected[lat : lat + half_rope], projected[lat + half_rope :]
    lcos, lsin = jnp.cos(local_angles), jnp.sin(local_angles)
    rotated = jnp.concatenate([first * lcos - second * lsin, first * lsin + second * lcos], axis=0)
    new_s[...] = jnp.concatenate(
        [latent.T * gain_ref[...].astype(jnp.float32)[None, :], rotated.T], axis=1
    ).astype(jnp.bfloat16)
    new_send = remote(new_s, new_in, pair_send.at[0], pair_recv.at[0], (key_partner, dev))
    new_send.start()
    new_keep = pltpu.make_async_copy(new_s, new_own, load_sem.at[4])
    new_keep.start()
    pass_on(2, 4)
    own = jnp.where(used, owners, -1).astype(jnp.float32)
    own = pltpu.roll(own, (n_lanes - req * dev) % n_lanes, 1)
    own = jnp.concatenate([own, jnp.zeros((n_lanes - max_pages, n_lanes), jnp.float32)], axis=0).T
    own = jnp.concatenate([own[r : r + 1, :max_pages] for r in range(req)], axis=1)
    list_pages(pool, dev, key_partner, own.astype(jnp.int32), table_ref, n_a, quarter)

    ql_in[pool] = ql_ref[...]
    for copy in ql_gets:
        copy.wait_recv()
    for y in range(4):
        rows = ql_in[y].astype(jnp.float32)
        for r in range(req):
            q_full[pl.ds(r * new_len + y * quarter, quarter), :] = rows[
                r * quarter : (r + 1) * quarter
            ]
    for copy in loads[1:]:
        copy.wait()
    group = 128 // new_len
    width = nope + rope

    cos, sin = jnp.cos(angles), jnp.sin(angles)

    def project(g):
        raw = jnp.dot(
            q_full[...].astype(jnp.bfloat16),
            qup_v[:, g * group * width : (g + 1) * group * width],
            preferred_element_type=jnp.float32,
        ).T
        built = []
        for j in range(group):
            at = j * width
            q_nope = raw[at : at + nope].astype(jnp.bfloat16)
            q_abs = lax.dot_general(
                wuk_v[g * group + j],
                q_nope,
                (((0,), (0,)), ((), ())),
                preferred_element_type=jnp.float32,
            )
            x = raw[at + nope : at + nope + half_rope]
            y = raw[at + nope + half_rope : at + width]
            built.append(
                jnp.concatenate([q_abs, x * cos - y * sin, x * sin + y * cos], axis=0).astype(
                    jnp.bfloat16
                )
            )
        for r in range(req):
            q_s[r, :, g * 128 : (g + 1) * 128] = jnp.concatenate(
                [b[:, r * new_len : (r + 1) * new_len] for b in built], axis=1
            )

    done = 4
    for g in range(heads // group):
        project(g)
        if g < heads // group - 1:
            pass_on(done, done + 2)
            done += 2

    q_send = remote(q_s, q_other, pair_send.at[1], pair_recv.at[1], (head_partner, dev))
    q_send.start()
    q_keep = pltpu.make_async_copy(q_s, q_own, load_sem.at[5])
    q_keep.start()

    pass_on(done, n_send)
    for copy in ql_sends:
        copy.wait_send()
    for copy in sends[1:]:
        copy.wait_send()
    own_pages.wait()
    new_keep.wait()
    q_keep.wait()
    new_send.wait()
    own_new, got_new = new_s[...].astype(jnp.float32), new_in[...].astype(jnp.float32)
    for r in range(req):
        rows = slice(r * quarter, (r + 1) * quarter)
        new_keys[r] = jnp.concatenate([own_new[rows], got_new[rows]], axis=0).astype(jnp.bfloat16)
    q_send.wait()
    for copy in passes:
        copy.wait()


def exchange(prefix, ql, hidden, gain, owner_t, slot_t, frequency, store, wd, qup, wuk, req):
    n_cols = prefix.shape[0] // req
    n_slots, page, key_dim = store.shape
    heads, nope, lat = wuk.shape
    tokens = ql.shape[0]
    new_len = 4 * tokens // req
    bf16 = jnp.bfloat16
    any_spec = pl.BlockSpec(memory_space=pl.ANY)
    vmem = pl.BlockSpec(memory_space=pltpu.VMEM)
    own_rows = heads * new_len
    pair = (2 * page * key_dim // lat, lat)
    query = jax.ShapeDtypeStruct((req, key_dim, own_rows), bf16)
    new = jax.ShapeDtypeStruct((tokens, key_dim), bf16)
    near = jax.ShapeDtypeStruct((FORWARDED,) + pair, bf16)
    far = jax.ShapeDtypeStruct((n_cols - FORWARDED,) + pair, bf16)
    dma = pltpu.SemaphoreType.DMA
    return pl.pallas_call(
        exchange_kernel,
        in_specs=[pl.BlockSpec(memory_space=pltpu.SMEM)] + [vmem] * 7 + [any_spec] * 4,
        out_specs=[any_spec] * 6 + [vmem] * 2,
        out_shape=[
            near,
            far,
            near,
            query,
            query,
            new,
            jax.ShapeDtypeStruct((req, 2 * tokens // req, key_dim), bf16),
            jax.ShapeDtypeStruct((8, 4 * n_cols), jnp.int32),
        ],
        scratch_shapes=[
            pltpu.VMEM(store.shape, bf16),
            pltpu.VMEM((n_cols,) + pair, bf16),
            pltpu.VMEM((4,) + ql.shape, bf16),
            pltpu.VMEM(wd.shape, bf16),
            pltpu.VMEM(qup.shape, bf16),
            pltpu.VMEM(wuk.shape, bf16),
            pltpu.VMEM(query.shape, bf16),
            pltpu.VMEM(new.shape, bf16),
            pltpu.VMEM(new.shape, bf16),
            pltpu.VMEM((req * new_len, ql.shape[1]), jnp.float32),
            pltpu.VMEM((2, prefix.shape[0]), jnp.int32),
            pltpu.SMEM((2, prefix.shape[0]), jnp.int32),
            dma((8,)),
            dma((3,)),
            dma((3,)),
            dma((n_cols,)),
            dma((n_cols,)),
            dma((FORWARDED,)),
            dma((FORWARDED,)),
            dma((2,)),
            dma((2,)),
        ],
        compiler_params=pltpu.CompilerParams(
            collective_id=1, has_side_effects=True, vmem_limit_bytes=40 * 2**20
        ),
        cost_estimate=pl.CostEstimate(flops=10**10, bytes_accessed=10**8, transcendentals=0),
        name="exchange",
    )(prefix, ql, hidden, gain, prefix, owner_t, slot_t, frequency, store, wd, qup, wuk)


def gather_rows(parts, first, last):
    return jnp.concatenate([part[first:last] for part in parts], axis=0)


def attention_step(table_ref, *refs, call, sizes, base, first, kind, scale, page, new_len):
    n_blocks = len(sizes)
    blocks, refs = refs[:n_blocks], refs[n_blocks:]
    q_ref, refs = refs[0], refs[1:]
    n_inputs = 1 if first else 2
    inputs, refs = refs[:n_inputs], refs[n_inputs:]
    if kind == "own":
        wuv_ref, refs = refs[0], refs[1:]
    result, mass, refs = refs[0], refs[1], refs[2:]
    pairs, sem, even, odd, even_keys, odd_keys, query = refs[:7]
    acc = result.at[0] if kind == "state" else refs[7]
    lat, rows = acc.shape
    request = pl.program_id(0)

    copies, at = [], 0
    for i, block in enumerate(blocks):
        copies.append(pltpu.make_async_copy(block, pairs.at[pl.ds(at, sizes[i])], sem.at[i]))
        at += sizes[i]

    @pl.when(request == 0)
    def _():
        for copy in copies:
            copy.start()

    tile_slots = TILES[call]
    factor = scale * math.log2(math.e)
    rope = q_ref.shape[1] - lat
    pad = 128 - rope
    bias_rows = jnp.where(
        lax.broadcasted_iota(jnp.int32, (pad, rows), 0) == 0, 1.0, 0.0
    ).astype(jnp.bfloat16)
    key_lane = lax.broadcasted_iota(jnp.int32, (page, pad), 1)

    query[: lat + rope, :] = q_ref[0]
    query[lat + rope :, :] = bias_rows

    def weigh(keys, weights):
        return lax.dot_general(
            keys, weights, (((0,), (0,)), ((), ())), preferred_element_type=jnp.float32
        )

    if first:
        new_keys = inputs[0][0]
        quarter = new_keys.shape[0] // 2
        row = lax.broadcasted_iota(jnp.int32, (2 * quarter, 1), 0)
        new_pos = jnp.where(row < quarter, table_ref[6, 0] + row, table_ref[6, quarter] + row - quarter)
        score = jnp.dot(new_keys, q_ref[0], preferred_element_type=jnp.float32)
        token = lax.broadcasted_iota(jnp.int32, score.shape, 1) % new_len
        live = new_pos <= token
        score = jnp.where(live, score, LOW)
        top = jnp.max(score, axis=0, keepdims=True)
        weights = jnp.where(live, jnp.exp2((score - top) * factor), 0.0)
        total = jnp.sum(weights, axis=0, keepdims=True)
        acc[...] = weigh(new_keys[:, :lat], weights.astype(jnp.bfloat16))
    else:
        acc_in, mass_in = inputs
        top, total = mass_in[0, 0:1, :], mass_in[0, 1:2, :]
        acc[...] = acc_in[0]

    @pl.when(request == 0)
    def _():
        for copy in copies:
            copy.wait()

    begin = table_ref[2 * call + 1, request]
    end = table_ref[2 * call + 1, request + 1]
    tiles = (end - begin + tile_slots - 1) // tile_slots

    def fetch(tile, keys, sheet):
        for g in range(tile_slots):
            spot = begin + tile * tile_slots + g
            index = table_ref[2 * call, jnp.maximum(jnp.minimum(spot, end - 1), 0)]
            half = table_ref.shape[1] // 2
            pair, turn = index % half - base, index // half
            rows = slice(g * page, (g + 1) * page)
            keys[rows, :lat] = pairs[pair, pl.ds(pl.multiple_of(turn * page, page), page), :]
            both = pairs[pair, pl.ds(2 * page, 2 * page * rope // lat), :]
            both = jnp.concatenate([both[:, i * 128 : (i + 1) * 128] for i in range(lat // 128)], axis=0)
            rotary = jnp.where(turn == 0, both[:, :rope], both[:, rope:])
            bias = jnp.where((key_lane == 0) & (spot >= end), LOW, 0.0).astype(jnp.bfloat16)
            keys[rows, lat:] = jnp.concatenate([rotary, bias], axis=1)
        sheet[...] = jnp.dot(keys[...], query[...], preferred_element_type=jnp.float32)

    def take(sheet, keys, top, total):
        score = sheet[...]
        new_top = jnp.maximum(top, jnp.max(score, axis=0, keepdims=True))
        shrink = jnp.exp2((top - new_top) * factor)
        weights = jnp.exp2((score - new_top) * factor)
        total = total * shrink + jnp.sum(weights, axis=0, keepdims=True)
        acc[...] = acc[...] * shrink + weigh(keys[:, :lat], weights.astype(jnp.bfloat16))
        return new_top, total

    @pl.when(tiles > 0)
    def _():
        fetch(0, even_keys, even)

    def body(step, carry):
        tile = 2 * step
        fetch(tile + 1, odd_keys, odd)
        carry = take(even, even_keys, *carry)
        fetch(jnp.minimum(tile + 2, tiles - 1), even_keys, even)
        return take(odd, odd_keys, *carry)

    carry = lax.fori_loop(0, tiles // 2, body, (top, total))
    top, total = lax.cond(
        tiles % 2 == 1,
        lambda c: take(even, even_keys, *c),
        lambda c: c,
        carry,
    )

    if kind == "state":
        mass[0, 0:1, :] = top
        mass[0, 1:2, :] = total
        return
    live = total > 0
    inverse = jnp.where(live, 1.0 / total, 0.0)
    log_mass = jnp.where(live, top * factor + jnp.log(total) * math.log2(math.e), LOW)
    mass[request] = log_mass
    mixed = (acc[...] * inverse).T
    high = mixed.astype(jnp.bfloat16)
    if kind == "partner":
        result[0, :rows, :] = high
        terms, rest = [], log_mass
        for _ in range(3):
            terms.append(rest.astype(jnp.bfloat16).astype(jnp.float32))
            rest = rest - terms[-1]
        row = lax.broadcasted_iota(jnp.int32, (16, rows), 0)
        tail = jnp.where(row == 2, terms[2], 0.0)
        tail = jnp.where(row == 0, terms[0], jnp.where(row == 1, terms[1], tail))
        result[0, rows:, :] = tail.astype(jnp.bfloat16)
    else:
        high_v, low_v = refs[8], refs[9]
        high_v[request] = high
        low_v[request] = (mixed - high.astype(jnp.float32)).astype(jnp.bfloat16)

    if kind == "own":

        @pl.when(request == pl.num_programs(0) - 1)
        def _():
            req = high_v.shape[0]
            head_v = wuv_ref.shape[2]
            for head in range(wuv_ref.shape[0]):
                first_row, last_row = head * new_len, (head + 1) * new_len
                total = None
                for part in (high_v, low_v):
                    rows_of = gather_rows([part.at[r] for r in range(req)], first_row, last_row)
                    term = jnp.dot(rows_of, wuv_ref[head], preferred_element_type=jnp.float32)
                    total = term if total is None else total + term
                for r in range(req):
                    result[r, :, head * head_v : (head + 1) * head_v] = total[
                        r * new_len : (r + 1) * new_len
                    ]


def attend(call, table, base, blocks, query, inputs, kind, scale, lat, new_len, w_uv=None):
    first = inputs[0].dtype == jnp.bfloat16
    req, key_dim, rows = query.shape
    sizes = [b.shape[0] for b in blocks]
    count = sum(sizes)
    page = blocks[0].shape[1] * lat // key_dim // 2
    kernel = functools.partial(
        attention_step, call=call, sizes=sizes, base=base, first=first, kind=kind, scale=scale, page=page, new_len=new_len
    )
    acc_spec = pl.BlockSpec((1, lat, rows), lambda r, *_: (r, 0, 0))
    mass_spec = pl.BlockSpec((1, 2, rows), lambda r, *_: (r, 0, 0))
    in_specs = [pl.BlockSpec(memory_space=pl.ANY)] * len(blocks)
    in_specs += [pl.BlockSpec((1, key_dim, rows), lambda r, *_: (r, 0, 0))]
    if first:
        in_specs += [pl.BlockSpec((1,) + inputs[0].shape[1:], lambda r, *_: (r, 0, 0))]
    else:
        in_specs += [acc_spec, mass_spec]
    scratch = [
        pltpu.VMEM((count,) + blocks[0].shape[1:], jnp.bfloat16),
        pltpu.SemaphoreType.DMA((len(blocks),)),
        pltpu.VMEM((TILES[call] * page, rows), jnp.float32),
        pltpu.VMEM((TILES[call] * page, rows), jnp.float32),
        pltpu.VMEM((TILES[call] * page, lat + 128), jnp.bfloat16),
        pltpu.VMEM((TILES[call] * page, lat + 128), jnp.bfloat16),
        pltpu.VMEM((lat + 128, rows), jnp.bfloat16),
    ]
    if kind == "state":
        out_specs = [acc_spec, mass_spec]
        out_shape = [
            jax.ShapeDtypeStruct((req, lat, rows), jnp.float32),
            jax.ShapeDtypeStruct((req, 2, rows), jnp.float32),
        ]
    else:
        scratch.append(pltpu.VMEM((lat, rows), jnp.float32))
        out_specs = [None, pl.BlockSpec((req, 1, rows), lambda r, *_: (0, 0, 0))]
        out_shape = [None, jax.ShapeDtypeStruct((req, 1, rows), jnp.float32)]
        if kind == "partner":
            out_specs[0] = pl.BlockSpec((1, rows + 16, lat), lambda r, *_: (r, 0, 0))
            out_shape[0] = jax.ShapeDtypeStruct((req, rows + 16, lat), jnp.bfloat16)
        else:
            heads, _, head_v = w_uv.shape
            in_specs.append(pl.BlockSpec(w_uv.shape, lambda r, *_: (0, 0, 0)))
            scratch += [pltpu.VMEM((req, lat, rows), jnp.bfloat16)] * 2
            out_specs[0] = pl.BlockSpec((req, new_len, heads * head_v), lambda r, *_: (0, 0, 0))
            out_shape[0] = jax.ShapeDtypeStruct((req, new_len, heads * head_v), jnp.float32)
    more = [w_uv] if kind == "own" else []
    return pl.pallas_call(
        kernel,
        grid_spec=pltpu.PrefetchScalarGridSpec(
            num_scalar_prefetch=1,
            grid=(req,),
            in_specs=in_specs,
            out_specs=out_specs,
            scratch_shapes=scratch,
        ),
        out_shape=out_shape,
        compiler_params=pltpu.CompilerParams(
            dimension_semantics=("arbitrary",), vmem_limit_bytes=VMEM_BYTES[call]
        ),
        cost_estimate=pl.CostEstimate(
            flops=8 * rows * count * page * (key_dim + lat),
            bytes_accessed=4 * req * lat * rows * 2 + count * page * key_dim * 2,
            transcendentals=2 * rows * count * page,
        ),
        name=f"attend_{call}_{kind}",
    )(table, *blocks, query, *inputs, *more)


def merge_step(turn_ref, got_ref, got_mass_ref, own_ref, mass_ref, wuv_ref, new_ref, out_ref, handed_ref):
    req, width, lat = got_ref.shape
    group, _, head_v = wuv_ref.shape
    new_len = width // group

    @pl.when(pl.program_id(0) == 0)
    def _():
        for i in range(req):
            handed_ref[i] = new_ref[turn_ref[i]]

    shares = []
    for r in range(req):
        tail = got_mass_ref[r].astype(jnp.float32)
        got_mass = tail[0:1] + tail[1:2] + tail[2:3]
        share = 1.0 / (1.0 + jnp.exp2(mass_ref[r] - got_mass))
        shares.append(jnp.broadcast_to(share, (width, width)).T)
    for j in range(group):
        first, last = j * new_len, (j + 1) * new_len
        rows = gather_rows([got_ref.at[r] for r in range(req)], first, last)
        got = jnp.dot(rows, wuv_ref[j], preferred_element_type=jnp.float32)
        lanes = slice(j * head_v, (j + 1) * head_v)
        for r in range(req):
            share = shares[r][first:last]
            own = own_ref[r, :, lanes]
            out_ref[r, :, lanes] = (
                own * (1.0 - share) + got[r * new_len : (r + 1) * new_len] * share
            ).astype(jnp.bfloat16)


def merge(turns, got, own, mass, w_uv, new_rows):
    req, deep, lat = got.shape
    heads, _, head_v = w_uv.shape
    groups = (deep - 16) // 128
    group = heads // groups
    new_len = 128 // group
    wide = pl.BlockSpec((req, new_len, group * head_v), lambda g, *_: (0, 0, g))
    whole = pl.BlockSpec(new_rows.shape, lambda g, *_: (0, 0, 0))
    return pl.pallas_call(
        merge_step,
        grid_spec=pltpu.PrefetchScalarGridSpec(
            num_scalar_prefetch=1,
            grid=(groups,),
            in_specs=[
                pl.BlockSpec((req, 128, lat), lambda g, *_: (0, g, 0)),
                pl.BlockSpec((req, 16, 128), lambda g, *_: (0, (deep - 16) // 16, g)),
                wide,
                pl.BlockSpec((req, 1, 128), lambda g, *_: (0, 0, g)),
                pl.BlockSpec((group, lat, head_v), lambda g, *_: (g, 0, 0)),
                whole,
            ],
            out_specs=[wide, whole],
        ),
        out_shape=[
            jax.ShapeDtypeStruct((req, new_len, heads * head_v), jnp.bfloat16),
            jax.ShapeDtypeStruct(new_rows.shape, jnp.bfloat16),
        ],
        compiler_params=pltpu.CompilerParams(
            dimension_semantics=("arbitrary",), vmem_limit_bytes=24 * 2**20
        ),
        name="merge",
    )(turns, got, got, own, mass, w_uv, new_rows)


def partner_pairs(pool_count, dev_count, which):
    return [
        (pool * dev_count + dev, partners(pool, dev)[which] * dev_count + dev)
        for pool in range(pool_count)
        for dev in range(dev_count)
    ]


def on_device(
    hidden,
    query_latent_rows,
    store,
    w_down,
    kv_gain,
    query_up_weight,
    w_uk,
    w_uv,
    prefix_pages,
    page_owner,
    page_slot,
    decode_order,
):
    pool_count = lax.axis_size("pool")
    dev_count = lax.axis_size("dev")
    column = lax.axis_index("dev")
    req_col, quarter, model_width = hidden.shape
    new_len = quarter * pool_count
    lat_dim = kv_gain.shape[0]
    key_dim = w_down.shape[1]
    nope_dim = w_uk.shape[1]
    rope_dim = key_dim - lat_dim
    first_row = column * req_col
    score_scale = (nope_dim + rope_dim) ** (-0.5)
    powers = np.exp(np.arange(rope_dim // 2) * (-2.0 * np.log(50000.0) / rope_dim))
    frequency = np.repeat(powers.astype(np.float32)[:, None], req_col * new_len, axis=1)

    near, far, passed, query, query_other, new_local, new_keys, table = exchange(
        prefix_pages,
        query_latent_rows.reshape(req_col * quarter, -1),
        hidden.reshape(req_col * quarter, model_width),
        kv_gain,
        page_owner.T,
        page_slot.T,
        jnp.asarray(frequency),
        store[0],
        w_down.T,
        query_up_weight,
        w_uk,
        req_col,
    )
    axes = ("pool", "dev")
    passed_far = lax.ppermute(far, axes, partner_pairs(pool_count, dev_count, 1))

    new = (new_keys,)
    common = dict(scale=score_scale, lat=lat_dim, new_len=new_len)
    early_blocks = [near, far, passed]
    state = attend(0, table, 0, early_blocks, query_other, new, "state", **common)
    part, part_mass = attend(
        1,
        table,
        dev_count + FORWARDED,
        [passed_far],
        query_other,
        state,
        "partner",
        **common,
    )
    got = lax.ppermute(part, axes, partner_pairs(pool_count, dev_count, 0))
    table, part_mass = lax.optimization_barrier((table, part_mass))
    own, own_mass = attend(
        2, table, 0, early_blocks + [passed_far], query, new, "own", w_uv=w_uv, **common
    )
    turns = lax.dynamic_slice_in_dim(decode_order, first_row, req_col) - first_row
    attended, handed = merge(
        turns, got, own, own_mass, w_uv, new_local.reshape(req_col, quarter, key_dim)
    )
    return (attended, handed)


def solution(mesh):
    in_specs = (
        P("dev", "pool", None),
        P("dev", "pool", None),
        P(("pool", "dev"), None, None, None),
        P(),
        P(),
        P(None, "pool"),
        P("pool", None, None),
        P("pool", None, None),
        P(),
        P(),
        P(),
        P(),
    )
    out_specs = (P("dev", None, "pool"), P("dev", "pool", None))
    return jax.shard_map(
        on_device, mesh=mesh, in_specs=in_specs, out_specs=out_specs, check_vma=False
    )
```

```python
import functools
import math

import jax
import jax.numpy as jnp
import numpy as np
from jax import lax
from jax.experimental import pallas as pl
from jax.experimental.pallas import tpu as pltpu
from jax.sharding import PartitionSpec as P

TILES = (8, 4, 8)
LOW = -1e30
FORWARDED = 20
EXCHANGE_VMEM = 60 * 2**20
ATTEND_VMEM = (60 * 2**20, 52 * 2**20, 52 * 2**20)
MERGE_VMEM = 24 * 2**20
MESH = pl.DeviceIdType.MESH
STEPS = [
    (0, 1), (1, 0), (0, 3), (3, 0), (1, 1), (3, 3), (1, 3), (3, 1),
    (0, 2), (2, 0), (1, 2), (2, 1), (3, 2), (2, 3), (2, 2),
]
OFFSETS = [(0, 0, 0), (0, 0, 1)] + [(z, x, c) for z, x in STEPS for c in (0, 1)]


def shifted(dev, offset, sign):
    core, x, z = dev % 2, (dev // 2) % 4, dev // 8
    dz, dx, dc = offset
    return ((z + sign * dz + 4) % 4 * 4 + (x + sign * dx + 4) % 4) * 2 + (core + dc) % 2


def partners(pool, dev):
    near = pool + 1 - 2 * (pool % 2)
    far = 3 - pool
    odd = dev % 2
    return near + odd * (far - near), far + odd * (near - far)


def list_pages(pool, dev, key_partner, owners, table_ref, n_a, quarter):
    n_pairs = len(OFFSETS)
    width = 4 * n_pairs
    entries = owners.shape[1]
    entry = lax.broadcasted_iota(jnp.int32, (1, entries), 1)
    pair = lax.broadcasted_iota(jnp.int32, (2 * n_pairs, 1), 0)
    source = jnp.zeros((2 * n_pairs, 1), jnp.int32)
    for j, offset in enumerate(OFFSETS):
        source = jnp.where(pair % n_pairs == j, shifted(dev, offset, -1), source)
    source = source + n_pairs * jnp.where(pair < n_pairs, pool, key_partner)
    hit = owners == source
    head = jnp.min(jnp.where(hit, entry, entries), axis=1, keepdims=True)
    tail = jnp.max(jnp.where(hit, entry, -1), axis=1, keepdims=True)
    nobody = entries // 64
    low = head // 64
    high = jnp.where(tail > head, tail // 64, nobody)
    request = jnp.concatenate([low, high], axis=0)
    place = lax.broadcasted_iota(jnp.int32, (width, 1), 0)
    late = place % (2 * n_pairs) >= n_pairs + n_a
    lane = lax.broadcasted_iota(jnp.int32, (1, width), 1)
    rows = []
    for wanted in (jnp.logical_not(late), late, None):
        mine = request if wanted is None else jnp.where(wanted, request, nobody)
        key = (mine * width + place).astype(jnp.float32)
        key = jnp.broadcast_to(key, (width, width))
        rank = jnp.sum((key.T < key).astype(jnp.float32), axis=1, keepdims=True).astype(jnp.int32)
        rows.append(jnp.sum(jnp.where(rank == lane, place, 0), axis=0, keepdims=True))
        rows.append(jnp.sum((mine < lane).astype(jnp.int32), axis=0, keepdims=True))
    rows.append(
        jnp.where(lane < quarter, pool * quarter + lane, key_partner * quarter + lane - quarter)
    )
    for i, row in enumerate(rows):
        table_ref[i : i + 1, :] = row


def exchange_kernel(
    prefix_ref, ql_ref, hidden_ref, gain_ref, prefix_row, owner_ref, slot_ref, frequency_ref,
    store_ref, wd_ref, qup_ref, wuk_ref,
    arr_a, arr_b, pass_a, q_own, q_other, new_own, new_keys, table_ref,
    store_v, packed, ql_in, wd_v, qup_v, wuk_v, q_s, new_s, new_in, q_full, picks_v, picks,
    load_sem, ql_send, ql_recv, page_send, page_recv, pass_send, pass_recv, pair_send, pair_recv,
):
    pool, dev = lax.axis_index("pool"), lax.axis_index("dev")
    head_partner, key_partner = partners(pool, dev)
    req, key_dim, own_rows = q_s.shape
    heads, nope, lat = wuk_v.shape
    rope = key_dim - lat
    half_rope = rope // 2
    quarter = ql_in.shape[1] // req
    new_len = 4 * quarter
    page = store_v.shape[1]
    n_send = len(OFFSETS)
    n_a = arr_a.shape[0]

    load_store = pltpu.make_async_copy(store_ref, store_v, load_sem.at[6])
    load_store.start()
    loads = [
        pltpu.make_async_copy(wd_ref, wd_v, load_sem.at[0]),
        pltpu.make_async_copy(qup_ref, qup_v, load_sem.at[1]),
        pltpu.make_async_copy(wuk_ref, wuk_v, load_sem.at[2]),
    ]
    for copy in loads:
        copy.start()

    barrier = pltpu.get_barrier_semaphore()
    for offset in OFFSETS[1:]:
        pl.semaphore_signal(
            barrier, inc=1, device_id=(pool, shifted(dev, offset, 1)), device_id_type=MESH
        )
    for step in range(1, 4):
        pl.semaphore_signal(
            barrier, inc=1, device_id=((pool + step) % 4, dev), device_id_type=MESH
        )

    prefix = prefix_row[...][None, :]
    owners = owner_ref[...]
    page_of = lax.broadcasted_iota(jnp.int32, owners.shape, 0)
    lane_of = lax.broadcasted_iota(jnp.int32, owners.shape, 1)
    n_slots, max_pages = store_v.shape[0], owners.shape[0]
    used = page_of < prefix
    mine = used & (owners == pool * n_send + dev)
    code = (lane_of % req * max_pages + page_of) * n_slots + slot_ref[...]
    low = jnp.min(jnp.where(mine, code, req * max_pages * n_slots), axis=0, keepdims=True)
    high = jnp.max(jnp.where(mine, code, 0), axis=0, keepdims=True)
    n_lanes = owners.shape[1]
    for step in (1, 2):
        low = jnp.minimum(low, pltpu.roll(low, n_lanes - step, 1))
        high = jnp.maximum(high, pltpu.roll(high, n_lanes - step, 1))
    picks_v[0:1, :] = low % n_slots
    picks_v[1:2, :] = high % n_slots
    load_picks = pltpu.make_async_copy(picks_v, picks, load_sem.at[7])
    load_picks.start()

    def pack(j):
        target = shifted(dev, OFFSETS[j], 1)
        pages = [store_v[picks[k, req * target]] for k in range(2)]
        for k in range(2):
            packed[j, k * page : (k + 1) * page, :] = pages[k][:, :lat]
        keys = jnp.concatenate([p[:, lat:] for p in pages], axis=1)
        step = page * 2 * rope // lat
        packed[j, 2 * page :, :] = jnp.concatenate(
            [keys[i * step : (i + 1) * step] for i in range(page // step)], axis=1
        )

    load_picks.wait()
    load_store.wait()
    for j in (0, 1):
        pack(j)
    pl.semaphore_wait(barrier, n_send - 1 + 3)

    def remote(src, dst, send, recv, target):
        return pltpu.make_async_remote_copy(
            src_ref=src, dst_ref=dst, send_sem=send, recv_sem=recv, device_id=target, device_id_type=MESH
        )

    ql_sends = [
        remote(ql_ref, ql_in.at[pool], ql_send.at[s - 1], ql_recv.at[s - 1], ((pool + s) % 4, dev))
        for s in range(1, 4)
    ]
    ql_gets = [
        remote(
            ql_ref, ql_in.at[(pool + 4 - s) % 4], ql_send.at[s - 1], ql_recv.at[s - 1], (head_partner, dev)
        )
        for s in range(1, 4)
    ]
    for copy in ql_sends:
        copy.start()

    def landing(j):
        return arr_a.at[j] if j < n_a else arr_b.at[j - n_a]

    passes = [
        remote(
            packed.at[0] if j == 0 else arr_a.at[j],
            pass_a.at[j],
            pass_send.at[j],
            pass_recv.at[j],
            (key_partner, dev),
        )
        for j in range(n_a)
    ]
    sends = [None] * n_send
    for j in range(1, n_send):
        if j > 1:
            pack(j)
        copy = remote(
            packed.at[j],
            landing(j),
            page_send.at[j],
            page_recv.at[j],
            (pool, shifted(dev, OFFSETS[j], 1)),
        )
        copy.start()
        sends[j] = copy
        if j == 1:
            passes[0].start()
    own_pages = pltpu.make_async_copy(packed.at[0], arr_a.at[0], load_sem.at[3])
    own_pages.start()

    def pass_on(first, last):
        for j in range(first, last):
            sends[j].wait_recv()
            if j < n_a:
                passes[j].start()

    pass_on(1, 2)
    frequency = frequency_ref[...]
    lane = lax.broadcasted_iota(jnp.int32, (1, frequency.shape[1]), 1)
    position = pool * quarter + lane % quarter
    local_position = position
    position = lane % new_len
    for r in range(req):
        begin = prefix_ref[req * dev + r] * page
        local_position = local_position + jnp.where(lane // quarter == r, begin, 0)
        position = position + jnp.where(lane // new_len == r, begin, 0)
    local_angles = (frequency * local_position.astype(jnp.float32))[:, : req * quarter]
    angles = frequency * position.astype(jnp.float32)

    loads[0].wait()
    projected = lax.dot_general(
        wd_v[...], hidden_ref[...], (((1,), (1,)), ((), ())), preferred_element_type=jnp.float32
    )
    latent = projected[:lat]
    latent = latent * lax.rsqrt(jnp.mean(latent * latent, axis=0, keepdims=True) + 1e-06)
    first, second = projected[lat : lat + half_rope], projected[lat + half_rope :]
    lcos, lsin = jnp.cos(local_angles), jnp.sin(local_angles)
    rotated = jnp.concatenate([first * lcos - second * lsin, first * lsin + second * lcos], axis=0)
    new_s[...] = jnp.concatenate(
        [latent.T * gain_ref[...].astype(jnp.float32)[None, :], rotated.T], axis=1
    ).astype(jnp.bfloat16)
    new_send = remote(new_s, new_in, pair_send.at[0], pair_recv.at[0], (key_partner, dev))
    new_send.start()
    new_keep = pltpu.make_async_copy(new_s, new_own, load_sem.at[4])
    new_keep.start()
    pass_on(2, 4)
    own = jnp.where(used, owners, -1).astype(jnp.float32)
    own = pltpu.roll(own, (n_lanes - req * dev) % n_lanes, 1)
    own = jnp.concatenate([own, jnp.zeros((n_lanes - max_pages, n_lanes), jnp.float32)], axis=0).T
    own = jnp.concatenate([own[r : r + 1, :max_pages] for r in range(req)], axis=1)
    list_pages(pool, dev, key_partner, own.astype(jnp.int32), table_ref, n_a, quarter)

    ql_in[pool] = ql_ref[...]
    for copy in ql_gets:
        copy.wait_recv()
    for y in range(4):
        rows = ql_in[y].astype(jnp.float32)
        for r in range(req):
            q_full[pl.ds(r * new_len + y * quarter, quarter), :] = rows[
                r * quarter : (r + 1) * quarter
            ]
    for copy in loads[1:]:
        copy.wait()
    group = 128 // new_len
    width = nope + rope

    cos, sin = jnp.cos(angles), jnp.sin(angles)

    def project(g):
        raw = jnp.dot(
            q_full[...].astype(jnp.bfloat16),
            qup_v[:, g * group * width : (g + 1) * group * width],
            preferred_element_type=jnp.float32,
        ).T
        built = []
        for j in range(group):
            at = j * width
            q_nope = raw[at : at + nope].astype(jnp.bfloat16)
            q_abs = lax.dot_general(
                wuk_v[g * group + j],
                q_nope,
                (((0,), (0,)), ((), ())),
                preferred_element_type=jnp.float32,
            )
            x = raw[at + nope : at + nope + half_rope]
            y = raw[at + nope + half_rope : at + width]
            built.append(
                jnp.concatenate([q_abs, x * cos - y * sin, x * sin + y * cos], axis=0).astype(
                    jnp.bfloat16
                )
            )
        for r in range(req):
            q_s[r, :, g * 128 : (g + 1) * 128] = jnp.concatenate(
                [b[:, r * new_len : (r + 1) * new_len] for b in built], axis=1
            )

    done = 4
    for g in range(heads // group):
        project(g)
        if g < heads // group - 1:
            pass_on(done, done + 2)
            done += 2

    q_send = remote(q_s, q_other, pair_send.at[1], pair_recv.at[1], (head_partner, dev))
    q_send.start()
    q_keep = pltpu.make_async_copy(q_s, q_own, load_sem.at[5])
    q_keep.start()

    pass_on(done, n_send)
    for copy in ql_sends:
        copy.wait_send()
    for copy in sends[1:]:
        copy.wait_send()
    own_pages.wait()
    new_keep.wait()
    q_keep.wait()
    new_send.wait()
    own_new, got_new = new_s[...].astype(jnp.float32), new_in[...].astype(jnp.float32)
    for r in range(req):
        rows = slice(r * quarter, (r + 1) * quarter)
        new_keys[r] = jnp.concatenate([own_new[rows], got_new[rows]], axis=0).astype(jnp.bfloat16)
    q_send.wait()
    for copy in passes:
        copy.wait()


def exchange(prefix, ql, hidden, gain, owner_t, slot_t, frequency, store, wd, qup, wuk, req):
    n_cols = prefix.shape[0] // req
    n_slots, page, key_dim = store.shape
    heads, nope, lat = wuk.shape
    tokens = ql.shape[0]
    new_len = 4 * tokens // req
    bf16 = jnp.bfloat16
    any_spec = pl.BlockSpec(memory_space=pl.ANY)
    vmem = pl.BlockSpec(memory_space=pltpu.VMEM)
    own_rows = heads * new_len
    pair = (2 * page * key_dim // lat, lat)
    query = jax.ShapeDtypeStruct((req, key_dim, own_rows), bf16)
    new = jax.ShapeDtypeStruct((tokens, key_dim), bf16)
    near = jax.ShapeDtypeStruct((FORWARDED,) + pair, bf16)
    far = jax.ShapeDtypeStruct((n_cols - FORWARDED,) + pair, bf16)
    dma = pltpu.SemaphoreType.DMA
    return pl.pallas_call(
        exchange_kernel,
        in_specs=[pl.BlockSpec(memory_space=pltpu.SMEM)] + [vmem] * 7 + [any_spec] * 4,
        out_specs=[any_spec] * 6 + [vmem] * 2,
        out_shape=[
            near,
            far,
            near,
            query,
            query,
            new,
            jax.ShapeDtypeStruct((req, 2 * tokens // req, key_dim), bf16),
            jax.ShapeDtypeStruct((8, 4 * n_cols), jnp.int32),
        ],
        scratch_shapes=[
            pltpu.VMEM(store.shape, bf16),
            pltpu.VMEM((n_cols,) + pair, bf16),
            pltpu.VMEM((4,) + ql.shape, bf16),
            pltpu.VMEM(wd.shape, bf16),
            pltpu.VMEM(qup.shape, bf16),
            pltpu.VMEM(wuk.shape, bf16),
            pltpu.VMEM(query.shape, bf16),
            pltpu.VMEM(new.shape, bf16),
            pltpu.VMEM(new.shape, bf16),
            pltpu.VMEM((req * new_len, ql.shape[1]), jnp.float32),
            pltpu.VMEM((2, prefix.shape[0]), jnp.int32),
            pltpu.SMEM((2, prefix.shape[0]), jnp.int32),
            dma((8,)),
            dma((3,)),
            dma((3,)),
            dma((n_cols,)),
            dma((n_cols,)),
            dma((FORWARDED,)),
            dma((FORWARDED,)),
            dma((2,)),
            dma((2,)),
        ],
        compiler_params=pltpu.CompilerParams(
            collective_id=1, has_side_effects=True, vmem_limit_bytes=EXCHANGE_VMEM
        ),
        cost_estimate=pl.CostEstimate(flops=10**10, bytes_accessed=10**8, transcendentals=0),
        name="exchange",
    )(prefix, ql, hidden, gain, prefix, owner_t, slot_t, frequency, store, wd, qup, wuk)


def gather_rows(parts, first, last):
    return jnp.concatenate([part[first:last] for part in parts], axis=0)


def attention_step(table_ref, *refs, call, sizes, base, first, kind, scale, page, new_len):
    n_blocks = len(sizes)
    blocks, refs = refs[:n_blocks], refs[n_blocks:]
    q_ref, refs = refs[0], refs[1:]
    n_inputs = 1 if first else 2
    inputs, refs = refs[:n_inputs], refs[n_inputs:]
    if kind == "own":
        wuv_hbm, refs = refs[0], refs[1:]
    result, mass, refs = refs[0], refs[1], refs[2:]
    pairs, sem, even, odd, even_keys, odd_keys, query = refs[:7]
    acc = result.at[0] if kind == "state" else refs[7]
    lat, rows = acc.shape
    request = pl.program_id(0)

    copies, at = [], 0
    for i, block in enumerate(blocks):
        copies.append(pltpu.make_async_copy(block, pairs.at[pl.ds(at, sizes[i])], sem.at[i]))
        at += sizes[i]
    if kind == "own":
        wuv_ref = refs[10]
        load_wuv = pltpu.make_async_copy(wuv_hbm, wuv_ref, refs[11])

    @pl.when(request == 0)
    def _():
        for copy in copies:
            copy.start()
        if kind == "own":
            load_wuv.start()

    tile_slots = TILES[call]
    factor = scale * math.log2(math.e)
    rope = q_ref.shape[1] - lat
    pad = 128 - rope
    bias_rows = jnp.where(
        lax.broadcasted_iota(jnp.int32, (pad, rows), 0) == 0, 1.0, 0.0
    ).astype(jnp.bfloat16)
    key_lane = lax.broadcasted_iota(jnp.int32, (page, pad), 1)

    query[: lat + rope, :] = q_ref[0]
    query[lat + rope :, :] = bias_rows

    def weigh(keys, weights):
        return lax.dot_general(
            keys, weights, (((0,), (0,)), ((), ())), preferred_element_type=jnp.float32
        )

    if first:
        new_keys = inputs[0][0]
        quarter = new_keys.shape[0] // 2
        row = lax.broadcasted_iota(jnp.int32, (2 * quarter, 1), 0)
        new_pos = jnp.where(row < quarter, table_ref[6, 0] + row, table_ref[6, quarter] + row - quarter)
        score = jnp.dot(new_keys, q_ref[0], preferred_element_type=jnp.float32)
        token = lax.broadcasted_iota(jnp.int32, score.shape, 1) % new_len
        live = new_pos <= token
        score = jnp.where(live, score, LOW)
        top = jnp.max(score, axis=0, keepdims=True)
        weights = jnp.where(live, jnp.exp2((score - top) * factor), 0.0)
        total = jnp.sum(weights, axis=0, keepdims=True)
        acc[...] = weigh(new_keys[:, :lat], weights.astype(jnp.bfloat16))
    else:
        acc_in, mass_in = inputs
        top, total = mass_in[0, 0:1, :], mass_in[0, 1:2, :]
        acc[...] = acc_in[0]

    @pl.when(request == 0)
    def _():
        for copy in copies:
            copy.wait()

    begin = table_ref[2 * call + 1, request]
    end = table_ref[2 * call + 1, request + 1]
    tiles = (end - begin + tile_slots - 1) // tile_slots

    def fetch(tile, keys, sheet):
        for g in range(tile_slots):
            spot = begin + tile * tile_slots + g
            index = table_ref[2 * call, jnp.maximum(jnp.minimum(spot, end - 1), 0)]
            half = table_ref.shape[1] // 2
            pair, turn = index % half - base, index // half
            rows = slice(g * page, (g + 1) * page)
            keys[rows, :lat] = pairs[pair, pl.ds(pl.multiple_of(turn * page, page), page), :]
            both = pairs[pair, pl.ds(2 * page, 2 * page * rope // lat), :]
            both = jnp.concatenate([both[:, i * 128 : (i + 1) * 128] for i in range(lat // 128)], axis=0)
            rotary = jnp.where(turn == 0, both[:, :rope], both[:, rope:])
            bias = jnp.where((key_lane == 0) & (spot >= end), LOW, 0.0).astype(jnp.bfloat16)
            keys[rows, lat:] = jnp.concatenate([rotary, bias], axis=1)
        sheet[...] = jnp.dot(keys[...], query[...], preferred_element_type=jnp.float32)

    def take(sheet, keys, top, total):
        score = sheet[...]
        new_top = jnp.maximum(top, jnp.max(score, axis=0, keepdims=True))
        shrink = jnp.exp2((top - new_top) * factor)
        weights = jnp.exp2((score - new_top) * factor)
        total = total * shrink + jnp.sum(weights, axis=0, keepdims=True)
        acc[...] = acc[...] * shrink + weigh(keys[:, :lat], weights.astype(jnp.bfloat16))
        return new_top, total

    @pl.when(tiles > 0)
    def _():
        fetch(0, even_keys, even)

    def body(step, carry):
        tile = 2 * step
        fetch(tile + 1, odd_keys, odd)
        carry = take(even, even_keys, *carry)
        fetch(jnp.minimum(tile + 2, tiles - 1), even_keys, even)
        return take(odd, odd_keys, *carry)

    carry = lax.fori_loop(0, tiles // 2, body, (top, total))
    top, total = lax.cond(
        tiles % 2 == 1,
        lambda c: take(even, even_keys, *c),
        lambda c: c,
        carry,
    )

    if kind == "state":
        mass[0, 0:1, :] = top
        mass[0, 1:2, :] = total
        return
    live = total > 0
    inverse = jnp.where(live, 1.0 / total, 0.0)
    log_mass = jnp.where(live, top * factor + jnp.log(total) * math.log2(math.e), LOW)
    mass[request] = log_mass
    mixed = (acc[...] * inverse).T
    high = mixed.astype(jnp.bfloat16)
    if kind == "partner":
        result[0, :rows, :] = high
        terms, rest = [], log_mass
        for _ in range(3):
            terms.append(rest.astype(jnp.bfloat16).astype(jnp.float32))
            rest = rest - terms[-1]
        row = lax.broadcasted_iota(jnp.int32, (16, rows), 0)
        tail = jnp.where(row == 2, terms[2], 0.0)
        tail = jnp.where(row == 0, terms[0], jnp.where(row == 1, terms[1], tail))
        result[0, rows:, :] = tail.astype(jnp.bfloat16)
    else:
        high_v, low_v = refs[8], refs[9]
        high_v[request] = high
        low_v[request] = (mixed - high.astype(jnp.float32)).astype(jnp.bfloat16)

    if kind == "own":

        @pl.when(request == pl.num_programs(0) - 1)
        def _():
            load_wuv.wait()
            req = high_v.shape[0]
            head_v = wuv_ref.shape[2]
            for head in range(wuv_ref.shape[0]):
                first_row, last_row = head * new_len, (head + 1) * new_len
                total = None
                for part in (high_v, low_v):
                    rows_of = gather_rows([part.at[r] for r in range(req)], first_row, last_row)
                    term = jnp.dot(rows_of, wuv_ref[head], preferred_element_type=jnp.float32)
                    total = term if total is None else total + term
                for r in range(req):
                    result[r, :, head * head_v : (head + 1) * head_v] = total[
                        r * new_len : (r + 1) * new_len
                    ]


def attend(call, table, base, blocks, query, inputs, kind, scale, lat, new_len, w_uv=None):
    first = inputs[0].dtype == jnp.bfloat16
    req, key_dim, rows = query.shape
    sizes = [b.shape[0] for b in blocks]
    count = sum(sizes)
    page = blocks[0].shape[1] * lat // key_dim // 2
    kernel = functools.partial(
        attention_step, call=call, sizes=sizes, base=base, first=first, kind=kind, scale=scale, page=page, new_len=new_len
    )
    acc_spec = pl.BlockSpec((1, lat, rows), lambda r, *_: (r, 0, 0))
    mass_spec = pl.BlockSpec((1, 2, rows), lambda r, *_: (r, 0, 0))
    in_specs = [pl.BlockSpec(memory_space=pl.ANY if call == 1 else pltpu.HBM)] * len(blocks)
    in_specs += [pl.BlockSpec((1, key_dim, rows), lambda r, *_: (r, 0, 0))]
    if first:
        in_specs += [pl.BlockSpec((1,) + inputs[0].shape[1:], lambda r, *_: (r, 0, 0))]
    else:
        in_specs += [acc_spec, mass_spec]
    scratch = [
        pltpu.VMEM((count,) + blocks[0].shape[1:], jnp.bfloat16),
        pltpu.SemaphoreType.DMA((len(blocks),)),
        pltpu.VMEM((TILES[call] * page, rows), jnp.float32),
        pltpu.VMEM((TILES[call] * page, rows), jnp.float32),
        pltpu.VMEM((TILES[call] * page, lat + 128), jnp.bfloat16),
        pltpu.VMEM((TILES[call] * page, lat + 128), jnp.bfloat16),
        pltpu.VMEM((lat + 128, rows), jnp.bfloat16),
    ]
    if kind == "state":
        out_specs = [acc_spec, mass_spec]
        out_shape = [
            jax.ShapeDtypeStruct((req, lat, rows), jnp.float32),
            jax.ShapeDtypeStruct((req, 2, rows), jnp.float32),
        ]
    else:
        scratch.append(pltpu.VMEM((lat, rows), jnp.float32))
        out_specs = [None, pl.BlockSpec((req, 1, rows), lambda r, *_: (0, 0, 0))]
        out_shape = [None, jax.ShapeDtypeStruct((req, 1, rows), jnp.float32)]
        if kind == "partner":
            out_specs[0] = pl.BlockSpec((1, rows + 16, lat), lambda r, *_: (r, 0, 0))
            out_shape[0] = jax.ShapeDtypeStruct((req, rows + 16, lat), jnp.bfloat16)
        else:
            heads, _, head_v = w_uv.shape
            in_specs.append(pl.BlockSpec(memory_space=pltpu.HBM))
            scratch += [pltpu.VMEM((req, lat, rows), jnp.bfloat16)] * 2
            scratch += [pltpu.VMEM(w_uv.shape, jnp.bfloat16), pltpu.SemaphoreType.DMA]
            out_specs[0] = pl.BlockSpec((req, new_len, heads * head_v), lambda r, *_: (0, 0, 0))
            out_shape[0] = jax.ShapeDtypeStruct((req, new_len, heads * head_v), jnp.float32)
    more = [w_uv] if kind == "own" else []
    return pl.pallas_call(
        kernel,
        grid_spec=pltpu.PrefetchScalarGridSpec(
            num_scalar_prefetch=1,
            grid=(req,),
            in_specs=in_specs,
            out_specs=out_specs,
            scratch_shapes=scratch,
        ),
        out_shape=out_shape,
        compiler_params=pltpu.CompilerParams(
            dimension_semantics=("arbitrary",), vmem_limit_bytes=ATTEND_VMEM[call]
        ),
        cost_estimate=pl.CostEstimate(
            flops=8 * rows * count * page * (key_dim + lat),
            bytes_accessed=4 * req * lat * rows * 2 + count * page * key_dim * 2,
            transcendentals=2 * rows * count * page,
        ),
        name=f"attend_{call}_{kind}",
    )(table, *blocks, query, *inputs, *more)


def merge_step(turn_ref, got_ref, got_mass_ref, own_ref, mass_ref, wuv_ref, new_ref, out_ref, handed_ref):
    req, width, lat = got_ref.shape
    group, _, head_v = wuv_ref.shape
    new_len = width // group

    @pl.when(pl.program_id(0) == 0)
    def _():
        for i in range(req):
            handed_ref[i] = new_ref[turn_ref[i]]

    shares = []
    for r in range(req):
        tail = got_mass_ref[r].astype(jnp.float32)
        got_mass = tail[0:1] + tail[1:2] + tail[2:3]
        share = 1.0 / (1.0 + jnp.exp2(mass_ref[r] - got_mass))
        shares.append(jnp.broadcast_to(share, (width, width)).T)
    for j in range(group):
        first, last = j * new_len, (j + 1) * new_len
        rows = gather_rows([got_ref.at[r] for r in range(req)], first, last)
        got = jnp.dot(rows, wuv_ref[j], preferred_element_type=jnp.float32)
        lanes = slice(j * head_v, (j + 1) * head_v)
        for r in range(req):
            share = shares[r][first:last]
            own = own_ref[r, :, lanes]
            out_ref[r, :, lanes] = (
                own * (1.0 - share) + got[r * new_len : (r + 1) * new_len] * share
            ).astype(jnp.bfloat16)


def merge(turns, got, own, mass, w_uv, new_rows):
    req, deep, lat = got.shape
    heads, _, head_v = w_uv.shape
    groups = (deep - 16) // 128
    group = heads // groups
    new_len = 128 // group
    wide = pl.BlockSpec((req, new_len, group * head_v), lambda g, *_: (0, 0, g))
    whole = pl.BlockSpec(new_rows.shape, lambda g, *_: (0, 0, 0))
    return pl.pallas_call(
        merge_step,
        grid_spec=pltpu.PrefetchScalarGridSpec(
            num_scalar_prefetch=1,
            grid=(groups,),
            in_specs=[
                pl.BlockSpec((req, 128, lat), lambda g, *_: (0, g, 0)),
                pl.BlockSpec((req, 16, 128), lambda g, *_: (0, (deep - 16) // 16, g)),
                wide,
                pl.BlockSpec((req, 1, 128), lambda g, *_: (0, 0, g)),
                pl.BlockSpec((group, lat, head_v), lambda g, *_: (g, 0, 0)),
                whole,
            ],
            out_specs=[wide, whole],
        ),
        out_shape=[
            jax.ShapeDtypeStruct((req, new_len, heads * head_v), jnp.bfloat16),
            jax.ShapeDtypeStruct(new_rows.shape, jnp.bfloat16),
        ],
        compiler_params=pltpu.CompilerParams(
            dimension_semantics=("arbitrary",), vmem_limit_bytes=MERGE_VMEM
        ),
        name="merge",
    )(turns, got, got, own, mass, w_uv, new_rows)


def partner_pairs(pool_count, dev_count, which):
    return [
        (pool * dev_count + dev, partners(pool, dev)[which] * dev_count + dev)
        for pool in range(pool_count)
        for dev in range(dev_count)
    ]


def on_device(
    hidden,
    query_latent_rows,
    store,
    w_down,
    kv_gain,
    query_up_weight,
    w_uk,
    w_uv,
    prefix_pages,
    page_owner,
    page_slot,
    decode_order,
):
    pool_count = lax.axis_size("pool")
    dev_count = lax.axis_size("dev")
    column = lax.axis_index("dev")
    req_col, quarter, model_width = hidden.shape
    new_len = quarter * pool_count
    lat_dim = kv_gain.shape[0]
    key_dim = w_down.shape[1]
    nope_dim = w_uk.shape[1]
    rope_dim = key_dim - lat_dim
    first_row = column * req_col
    score_scale = (nope_dim + rope_dim) ** (-0.5)
    powers = np.exp(np.arange(rope_dim // 2) * (-2.0 * np.log(50000.0) / rope_dim))
    frequency = np.repeat(powers.astype(np.float32)[:, None], req_col * new_len, axis=1)

    near, far, passed, query, query_other, new_local, new_keys, table = exchange(
        prefix_pages,
        query_latent_rows.reshape(req_col * quarter, -1),
        hidden.reshape(req_col * quarter, model_width),
        kv_gain,
        page_owner.T,
        page_slot.T,
        jnp.asarray(frequency),
        store[0],
        w_down.T,
        query_up_weight,
        w_uk,
        req_col,
    )
    axes = ("pool", "dev")
    passed_far = lax.ppermute(far, axes, partner_pairs(pool_count, dev_count, 1))

    new = (new_keys,)
    common = dict(scale=score_scale, lat=lat_dim, new_len=new_len)
    early_blocks = [near, far, passed]
    state = attend(0, table, 0, early_blocks, query_other, new, "state", **common)
    part, part_mass = attend(
        1,
        table,
        dev_count + FORWARDED,
        [passed_far],
        query_other,
        state,
        "partner",
        **common,
    )
    got = lax.ppermute(part, axes, partner_pairs(pool_count, dev_count, 0))
    table, part_mass = lax.optimization_barrier((table, part_mass))
    own, own_mass = attend(
        2, table, 0, early_blocks + [passed_far], query, new, "own", w_uv=w_uv, **common
    )
    turns = lax.dynamic_slice_in_dim(decode_order, first_row, req_col) - first_row
    attended, handed = merge(
        turns, got, own, own_mass, w_uv, new_local.reshape(req_col, quarter, key_dim)
    )
    return (attended, handed)


def solution(mesh):
    in_specs = (
        P("dev", "pool", None),
        P("dev", "pool", None),
        P(("pool", "dev"), None, None, None),
        P(),
        P(),
        P(None, "pool"),
        P("pool", None, None),
        P("pool", None, None),
        P(),
        P(),
        P(),
        P(),
    )
    out_specs = (P("dev", None, "pool"), P("dev", "pool", None))
    return jax.shard_map(
        on_device, mesh=mesh, in_specs=in_specs, out_specs=out_specs, check_vma=False
    )
```

```python
import functools
import math

import jax
import jax.numpy as jnp
import numpy as np
from jax import lax
from jax.experimental import pallas as pl
from jax.experimental.pallas import tpu as pltpu
from jax.sharding import PartitionSpec as P

TILES = (8, 4, 8)
LOW = -1e30
FORWARDED = 20
EXCHANGE_VMEM = 60 * 2**20
ATTEND_VMEM = (60 * 2**20, 52 * 2**20, 52 * 2**20)
MERGE_VMEM = 24 * 2**20
MESH = pl.DeviceIdType.MESH
STEPS = [
    (0, 1), (1, 0), (0, 3), (3, 0), (1, 1), (3, 3), (1, 3), (3, 1),
    (0, 2), (2, 0), (1, 2), (2, 1), (3, 2), (2, 3), (2, 2),
]
OFFSETS = [(0, 0, 0), (0, 0, 1)] + [(z, x, c) for z, x in STEPS for c in (0, 1)]


def shifted(dev, offset, sign):
    core, x, z = dev % 2, (dev // 2) % 4, dev // 8
    dz, dx, dc = offset
    return ((z + sign * dz + 4) % 4 * 4 + (x + sign * dx + 4) % 4) * 2 + (core + dc) % 2


def partners(pool, dev):
    near = pool + 1 - 2 * (pool % 2)
    far = 3 - pool
    odd = dev % 2
    return near + odd * (far - near), far + odd * (near - far)


def list_pages(pool, dev, key_partner, owners, table_ref, n_a, quarter):
    n_pairs = len(OFFSETS)
    width = 4 * n_pairs
    entries = owners.shape[1]
    entry = lax.broadcasted_iota(jnp.int32, (1, entries), 1)
    pair = lax.broadcasted_iota(jnp.int32, (2 * n_pairs, 1), 0)
    source = jnp.zeros((2 * n_pairs, 1), jnp.int32)
    for j, offset in enumerate(OFFSETS):
        source = jnp.where(pair % n_pairs == j, shifted(dev, offset, -1), source)
    source = source + n_pairs * jnp.where(pair < n_pairs, pool, key_partner)
    hit = owners == source
    head = jnp.min(jnp.where(hit, entry, entries), axis=1, keepdims=True)
    tail = jnp.max(jnp.where(hit, entry, -1), axis=1, keepdims=True)
    nobody = entries // 64
    low = head // 64
    high = jnp.where(tail > head, tail // 64, nobody)
    request = jnp.concatenate([low, high], axis=0)
    place = lax.broadcasted_iota(jnp.int32, (width, 1), 0)
    late = place % (2 * n_pairs) >= n_pairs + n_a
    lane = lax.broadcasted_iota(jnp.int32, (1, width), 1)
    rows = []
    for wanted in (jnp.logical_not(late), late, None):
        mine = request if wanted is None else jnp.where(wanted, request, nobody)
        key = (mine * width + place).astype(jnp.float32)
        key = jnp.broadcast_to(key, (width, width))
        rank = jnp.sum((key.T < key).astype(jnp.float32), axis=1, keepdims=True).astype(jnp.int32)
        rows.append(jnp.sum(jnp.where(rank == lane, place, 0), axis=0, keepdims=True))
        rows.append(jnp.sum((mine < lane).astype(jnp.int32), axis=0, keepdims=True))
    rows.append(
        jnp.where(lane < quarter, pool * quarter + lane, key_partner * quarter + lane - quarter)
    )
    for i, row in enumerate(rows):
        table_ref[i : i + 1, :] = row


def exchange_kernel(
    prefix_ref, ql_ref, hidden_ref, gain_ref, prefix_row, owner_ref, slot_ref, frequency_ref,
    store_ref, wd_ref, qup_ref, wuk_ref,
    arr_a, arr_b, pass_a, q_own, q_other, new_own, new_keys, table_ref,
    store_v, packed, ql_in, wd_v, qup_v, wuk_v, q_s, new_s, new_in, q_full, picks_v, picks,
    load_sem, ql_send, ql_recv, page_send, page_recv, pass_send, pass_recv, pair_send, pair_recv,
):
    pool, dev = lax.axis_index("pool"), lax.axis_index("dev")
    head_partner, key_partner = partners(pool, dev)
    _, req, key_dim, _ = q_s.shape
    heads, nope, lat = wuk_v.shape
    rope = key_dim - lat
    half_rope = rope // 2
    quarter = ql_in.shape[1] // req
    new_len = 4 * quarter
    page = store_v.shape[1]
    n_send = len(OFFSETS)
    n_a = arr_a.shape[0]

    load_store = pltpu.make_async_copy(store_ref, store_v, load_sem.at[6])
    load_store.start()
    loads = [
        pltpu.make_async_copy(qup_ref, qup_v, load_sem.at[1]),
        pltpu.make_async_copy(wuk_ref, wuk_v, load_sem.at[2]),
        pltpu.make_async_copy(wd_ref, wd_v, load_sem.at[0]),
    ]
    for copy in loads:
        copy.start()

    barrier = pltpu.get_barrier_semaphore()
    for offset in OFFSETS[1:]:
        pl.semaphore_signal(
            barrier, inc=1, device_id=(pool, shifted(dev, offset, 1)), device_id_type=MESH
        )
    for step in range(1, 4):
        pl.semaphore_signal(
            barrier, inc=1, device_id=((pool + step) % 4, dev), device_id_type=MESH
        )

    prefix = prefix_row[...][None, :]
    owners = owner_ref[...]
    page_of = lax.broadcasted_iota(jnp.int32, owners.shape, 0)
    lane_of = lax.broadcasted_iota(jnp.int32, owners.shape, 1)
    n_slots, max_pages = store_v.shape[0], owners.shape[0]
    used = page_of < prefix
    mine = used & (owners == pool * n_send + dev)
    code = (lane_of % req * max_pages + page_of) * n_slots + slot_ref[...]
    low = jnp.min(jnp.where(mine, code, req * max_pages * n_slots), axis=0, keepdims=True)
    high = jnp.max(jnp.where(mine, code, 0), axis=0, keepdims=True)
    n_lanes = owners.shape[1]
    for step in (1, 2):
        low = jnp.minimum(low, pltpu.roll(low, n_lanes - step, 1))
        high = jnp.maximum(high, pltpu.roll(high, n_lanes - step, 1))
    picks_v[0:1, :] = low % n_slots
    picks_v[1:2, :] = high % n_slots
    load_picks = pltpu.make_async_copy(picks_v, picks, load_sem.at[7])
    load_picks.start()

    def pack(j):
        target = shifted(dev, OFFSETS[j], 1)
        pages = [store_v[picks[k, req * target]] for k in range(2)]
        for k in range(2):
            packed[j, k * page : (k + 1) * page, :] = pages[k][:, :lat]
        keys = jnp.concatenate([p[:, lat:] for p in pages], axis=1)
        step = page * 2 * rope // lat
        packed[j, 2 * page :, :] = jnp.concatenate(
            [keys[i * step : (i + 1) * step] for i in range(page // step)], axis=1
        )

    load_picks.wait()
    load_store.wait()
    for j in (0, 1):
        pack(j)
    pl.semaphore_wait(barrier, n_send - 1 + 3)

    def remote(src, dst, send, recv, target):
        return pltpu.make_async_remote_copy(
            src_ref=src, dst_ref=dst, send_sem=send, recv_sem=recv, device_id=target, device_id_type=MESH
        )

    ql_sends = [
        remote(ql_ref, ql_in.at[pool], ql_send.at[s - 1], ql_recv.at[s - 1], ((pool + s) % 4, dev))
        for s in range(1, 4)
    ]
    ql_gets = [
        remote(
            ql_ref, ql_in.at[(pool + 4 - s) % 4], ql_send.at[s - 1], ql_recv.at[s - 1], (head_partner, dev)
        )
        for s in range(1, 4)
    ]
    for copy in ql_sends:
        copy.start()

    def landing(j):
        return arr_a.at[j] if j < n_a else arr_b.at[j - n_a]

    passes = [
        remote(
            packed.at[0] if j == 0 else arr_a.at[j],
            pass_a.at[j],
            pass_send.at[j],
            pass_recv.at[j],
            (key_partner, dev),
        )
        for j in range(n_a)
    ]
    sends = [None] * n_send
    for j in range(1, n_send):
        if j > 1:
            pack(j)
        copy = remote(
            packed.at[j],
            landing(j),
            page_send.at[j],
            page_recv.at[j],
            (pool, shifted(dev, OFFSETS[j], 1)),
        )
        copy.start()
        sends[j] = copy
        if j == 1:
            passes[0].start()
    own_pages = pltpu.make_async_copy(packed.at[0], arr_a.at[0], load_sem.at[3])
    own_pages.start()

    def pass_on(first, last):
        for j in range(first, last):
            sends[j].wait_recv()
            if j < n_a:
                passes[j].start()

    frequency = frequency_ref[...]
    lane = lax.broadcasted_iota(jnp.int32, (1, frequency.shape[1]), 1)
    position = pool * quarter + lane % quarter
    local_position = position
    position = lane % new_len
    for r in range(req):
        begin = prefix_ref[req * dev + r] * page
        local_position = local_position + jnp.where(lane // quarter == r, begin, 0)
        position = position + jnp.where(lane // new_len == r, begin, 0)
    local_angles = (frequency * local_position.astype(jnp.float32))[:, : req * quarter]
    angles = frequency * position.astype(jnp.float32)

    ql_in[pool] = ql_ref[...]
    for copy in ql_gets:
        copy.wait_recv()
    for y in range(4):
        rows = ql_in[y].astype(jnp.float32)
        for r in range(req):
            q_full[pl.ds(r * new_len + y * quarter, quarter), :] = rows[
                r * quarter : (r + 1) * quarter
            ]
    for copy in loads[:2]:
        copy.wait()
    group = 128 // new_len
    width = nope + rope

    cos, sin = jnp.cos(angles), jnp.sin(angles)

    def project(g):
        raw = jnp.dot(
            q_full[...].astype(jnp.bfloat16),
            qup_v[:, g * group * width : (g + 1) * group * width],
            preferred_element_type=jnp.float32,
        ).T
        built = []
        for j in range(group):
            at = j * width
            q_nope = raw[at : at + nope].astype(jnp.bfloat16)
            q_abs = lax.dot_general(
                wuk_v[g * group + j],
                q_nope,
                (((0,), (0,)), ((), ())),
                preferred_element_type=jnp.float32,
            )
            x = raw[at + nope : at + nope + half_rope]
            y = raw[at + nope + half_rope : at + width]
            built.append(
                jnp.concatenate([q_abs, x * cos - y * sin, x * sin + y * cos], axis=0).astype(
                    jnp.bfloat16
                )
            )
        for r in range(req):
            q_s[g, r] = jnp.concatenate(
                [b[:, r * new_len : (r + 1) * new_len] for b in built], axis=1
            )

    done = 1
    q_sends = []
    for g in range(heads // group):
        project(g)
        copy = remote(
            q_s.at[g], q_other.at[g], pair_send.at[1 + g], pair_recv.at[1 + g], (head_partner, dev)
        )
        copy.start()
        q_sends.append(copy)
        pass_on(done, done + 2)
        done += 2
    q_keep = pltpu.make_async_copy(q_s, q_own, load_sem.at[5])
    q_keep.start()

    loads[2].wait()
    projected = lax.dot_general(
        wd_v[...], hidden_ref[...], (((1,), (1,)), ((), ())), preferred_element_type=jnp.float32
    )
    latent = projected[:lat]
    latent = latent * lax.rsqrt(jnp.mean(latent * latent, axis=0, keepdims=True) + 1e-06)
    first, second = projected[lat : lat + half_rope], projected[lat + half_rope :]
    lcos, lsin = jnp.cos(local_angles), jnp.sin(local_angles)
    rotated = jnp.concatenate([first * lcos - second * lsin, first * lsin + second * lcos], axis=0)
    new_s[...] = jnp.concatenate(
        [latent.T * gain_ref[...].astype(jnp.float32)[None, :], rotated.T], axis=1
    ).astype(jnp.bfloat16)
    new_send = remote(new_s, new_in, pair_send.at[0], pair_recv.at[0], (key_partner, dev))
    new_send.start()
    new_keep = pltpu.make_async_copy(new_s, new_own, load_sem.at[4])
    new_keep.start()
    pass_on(done, done + 2)
    done += 2
    own = jnp.where(used, owners, -1).astype(jnp.float32)
    own = pltpu.roll(own, (n_lanes - req * dev) % n_lanes, 1)
    own = jnp.concatenate([own, jnp.zeros((n_lanes - max_pages, n_lanes), jnp.float32)], axis=0).T
    own = jnp.concatenate([own[r : r + 1, :max_pages] for r in range(req)], axis=1)
    list_pages(pool, dev, key_partner, own.astype(jnp.int32), table_ref, n_a, quarter)

    pass_on(done, n_send)
    for copy in ql_sends:
        copy.wait_send()
    for copy in sends[1:]:
        copy.wait_send()
    own_pages.wait()
    new_keep.wait()
    q_keep.wait()
    new_send.wait()
    own_new, got_new = new_s[...].astype(jnp.float32), new_in[...].astype(jnp.float32)
    for r in range(req):
        rows = slice(r * quarter, (r + 1) * quarter)
        new_keys[r] = jnp.concatenate([own_new[rows], got_new[rows]], axis=0).astype(jnp.bfloat16)
    for copy in q_sends:
        copy.wait()
    for copy in passes:
        copy.wait()


def exchange(prefix, ql, hidden, gain, owner_t, slot_t, frequency, store, wd, qup, wuk, req):
    n_cols = prefix.shape[0] // req
    n_slots, page, key_dim = store.shape
    heads, nope, lat = wuk.shape
    tokens = ql.shape[0]
    new_len = 4 * tokens // req
    bf16 = jnp.bfloat16
    any_spec = pl.BlockSpec(memory_space=pl.ANY)
    vmem = pl.BlockSpec(memory_space=pltpu.VMEM)
    own_rows = heads * new_len
    pair = (2 * page * key_dim // lat, lat)
    query = jax.ShapeDtypeStruct((own_rows // 128, req, key_dim, 128), bf16)
    new = jax.ShapeDtypeStruct((tokens, key_dim), bf16)
    near = jax.ShapeDtypeStruct((FORWARDED,) + pair, bf16)
    far = jax.ShapeDtypeStruct((n_cols - FORWARDED,) + pair, bf16)
    dma = pltpu.SemaphoreType.DMA
    return pl.pallas_call(
        exchange_kernel,
        in_specs=[pl.BlockSpec(memory_space=pltpu.SMEM)] + [vmem] * 7 + [any_spec] * 4,
        out_specs=[any_spec] * 6 + [vmem] * 2,
        out_shape=[
            near,
            far,
            near,
            query,
            query,
            new,
            jax.ShapeDtypeStruct((req, 2 * tokens // req, key_dim), bf16),
            jax.ShapeDtypeStruct((8, 4 * n_cols), jnp.int32),
        ],
        scratch_shapes=[
            pltpu.VMEM(store.shape, bf16),
            pltpu.VMEM((n_cols,) + pair, bf16),
            pltpu.VMEM((4,) + ql.shape, bf16),
            pltpu.VMEM(wd.shape, bf16),
            pltpu.VMEM(qup.shape, bf16),
            pltpu.VMEM(wuk.shape, bf16),
            pltpu.VMEM(query.shape, bf16),
            pltpu.VMEM(new.shape, bf16),
            pltpu.VMEM(new.shape, bf16),
            pltpu.VMEM((req * new_len, ql.shape[1]), jnp.float32),
            pltpu.VMEM((2, prefix.shape[0]), jnp.int32),
            pltpu.SMEM((2, prefix.shape[0]), jnp.int32),
            dma((8,)),
            dma((3,)),
            dma((3,)),
            dma((n_cols,)),
            dma((n_cols,)),
            dma((FORWARDED,)),
            dma((FORWARDED,)),
            dma((1 + own_rows // 128,)),
            dma((1 + own_rows // 128,)),
        ],
        compiler_params=pltpu.CompilerParams(
            collective_id=1, has_side_effects=True, vmem_limit_bytes=EXCHANGE_VMEM
        ),
        cost_estimate=pl.CostEstimate(flops=10**10, bytes_accessed=10**8, transcendentals=0),
        name="exchange",
    )(prefix, ql, hidden, gain, prefix, owner_t, slot_t, frequency, store, wd, qup, wuk)


def gather_rows(parts, first, last):
    return jnp.concatenate([part[first:last] for part in parts], axis=0)


def attention_step(table_ref, *refs, call, sizes, base, first, kind, scale, page, new_len):
    n_blocks = len(sizes)
    blocks, refs = refs[:n_blocks], refs[n_blocks:]
    q_ref, refs = refs[0], refs[1:]
    n_inputs = 1 if first else 2
    inputs, refs = refs[:n_inputs], refs[n_inputs:]
    if kind == "own":
        wuv_hbm, refs = refs[0], refs[1:]
    result, mass, refs = refs[0], refs[1], refs[2:]
    pairs, sem, even, odd, even_keys, odd_keys, query = refs[:7]
    acc = result.at[0] if kind == "state" else refs[7]
    lat, rows = acc.shape
    request = pl.program_id(0)

    copies, at = [], 0
    for i, block in enumerate(blocks):
        copies.append(pltpu.make_async_copy(block, pairs.at[pl.ds(at, sizes[i])], sem.at[i]))
        at += sizes[i]
    if kind == "own":
        wuv_ref = refs[10]
        load_wuv = pltpu.make_async_copy(wuv_hbm, wuv_ref, refs[11])

    @pl.when(request == 0)
    def _():
        for copy in copies:
            copy.start()
        if kind == "own":
            load_wuv.start()

    tile_slots = TILES[call]
    factor = scale * math.log2(math.e)
    rope = q_ref.shape[2] - lat
    pad = 128 - rope
    bias_rows = jnp.where(
        lax.broadcasted_iota(jnp.int32, (pad, rows), 0) == 0, 1.0, 0.0
    ).astype(jnp.bfloat16)
    key_lane = lax.broadcasted_iota(jnp.int32, (page, pad), 1)

    for g in range(q_ref.shape[0]):
        query[: lat + rope, g * 128 : (g + 1) * 128] = q_ref[g, 0]
    query[lat + rope :, :] = bias_rows

    def weigh(keys, weights):
        return lax.dot_general(
            keys, weights, (((0,), (0,)), ((), ())), preferred_element_type=jnp.float32
        )

    if first:
        new_keys = inputs[0][0]
        quarter = new_keys.shape[0] // 2
        row = lax.broadcasted_iota(jnp.int32, (2 * quarter, 1), 0)
        new_pos = jnp.where(row < quarter, table_ref[6, 0] + row, table_ref[6, quarter] + row - quarter)
        score = jnp.dot(new_keys, query[: lat + rope, :], preferred_element_type=jnp.float32)
        token = lax.broadcasted_iota(jnp.int32, score.shape, 1) % new_len
        live = new_pos <= token
        score = jnp.where(live, score, LOW)
        top = jnp.max(score, axis=0, keepdims=True)
        weights = jnp.where(live, jnp.exp2((score - top) * factor), 0.0)
        total = jnp.sum(weights, axis=0, keepdims=True)
        acc[...] = weigh(new_keys[:, :lat], weights.astype(jnp.bfloat16))
    else:
        acc_in, mass_in = inputs
        top, total = mass_in[0, 0:1, :], mass_in[0, 1:2, :]
        acc[...] = acc_in[0]

    @pl.when(request == 0)
    def _():
        for copy in copies:
            copy.wait()

    begin = table_ref[2 * call + 1, request]
    end = table_ref[2 * call + 1, request + 1]
    tiles = (end - begin + tile_slots - 1) // tile_slots

    def fetch(tile, keys, sheet):
        for g in range(tile_slots):
            spot = begin + tile * tile_slots + g
            index = table_ref[2 * call, jnp.maximum(jnp.minimum(spot, end - 1), 0)]
            half = table_ref.shape[1] // 2
            pair, turn = index % half - base, index // half
            rows = slice(g * page, (g + 1) * page)
            keys[rows, :lat] = pairs[pair, pl.ds(pl.multiple_of(turn * page, page), page), :]
            both = pairs[pair, pl.ds(2 * page, 2 * page * rope // lat), :]
            both = jnp.concatenate([both[:, i * 128 : (i + 1) * 128] for i in range(lat // 128)], axis=0)
            rotary = jnp.where(turn == 0, both[:, :rope], both[:, rope:])
            bias = jnp.where((key_lane == 0) & (spot >= end), LOW, 0.0).astype(jnp.bfloat16)
            keys[rows, lat:] = jnp.concatenate([rotary, bias], axis=1)
        sheet[...] = jnp.dot(keys[...], query[...], preferred_element_type=jnp.float32)

    def take(sheet, keys, top, total):
        score = sheet[...]
        new_top = jnp.maximum(top, jnp.max(score, axis=0, keepdims=True))
        shrink = jnp.exp2((top - new_top) * factor)
        weights = jnp.exp2((score - new_top) * factor)
        total = total * shrink + jnp.sum(weights, axis=0, keepdims=True)
        acc[...] = acc[...] * shrink + weigh(keys[:, :lat], weights.astype(jnp.bfloat16))
        return new_top, total

    @pl.when(tiles > 0)
    def _():
        fetch(0, even_keys, even)

    def body(step, carry):
        tile = 2 * step
        fetch(tile + 1, odd_keys, odd)
        carry = take(even, even_keys, *carry)
        fetch(jnp.minimum(tile + 2, tiles - 1), even_keys, even)
        return take(odd, odd_keys, *carry)

    carry = lax.fori_loop(0, tiles // 2, body, (top, total))
    top, total = lax.cond(
        tiles % 2 == 1,
        lambda c: take(even, even_keys, *c),
        lambda c: c,
        carry,
    )

    if kind == "state":
        mass[0, 0:1, :] = top
        mass[0, 1:2, :] = total
        return
    live = total > 0
    inverse = jnp.where(live, 1.0 / total, 0.0)
    log_mass = jnp.where(live, top * factor + jnp.log(total) * math.log2(math.e), LOW)
    mass[request] = log_mass
    mixed = (acc[...] * inverse).T
    high = mixed.astype(jnp.bfloat16)
    if kind == "partner":
        result[0, :rows, :] = high
        terms, rest = [], log_mass
        for _ in range(3):
            terms.append(rest.astype(jnp.bfloat16).astype(jnp.float32))
            rest = rest - terms[-1]
        row = lax.broadcasted_iota(jnp.int32, (16, rows), 0)
        tail = jnp.where(row == 2, terms[2], 0.0)
        tail = jnp.where(row == 0, terms[0], jnp.where(row == 1, terms[1], tail))
        result[0, rows:, :] = tail.astype(jnp.bfloat16)
    else:
        high_v, low_v = refs[8], refs[9]
        high_v[request] = high
        low_v[request] = (mixed - high.astype(jnp.float32)).astype(jnp.bfloat16)

    if kind == "own":

        @pl.when(request == pl.num_programs(0) - 1)
        def _():
            load_wuv.wait()
            req = high_v.shape[0]
            head_v = wuv_ref.shape[2]
            for head in range(wuv_ref.shape[0]):
                first_row, last_row = head * new_len, (head + 1) * new_len
                total = None
                for part in (high_v, low_v):
                    rows_of = gather_rows([part.at[r] for r in range(req)], first_row, last_row)
                    term = jnp.dot(rows_of, wuv_ref[head], preferred_element_type=jnp.float32)
                    total = term if total is None else total + term
                for r in range(req):
                    result[r, :, head * head_v : (head + 1) * head_v] = total[
                        r * new_len : (r + 1) * new_len
                    ]


def attend(call, table, base, blocks, query, inputs, kind, scale, lat, new_len, w_uv=None):
    first = inputs[0].dtype == jnp.bfloat16
    groups, req, key_dim, _ = query.shape
    rows = groups * 128
    sizes = [b.shape[0] for b in blocks]
    count = sum(sizes)
    page = blocks[0].shape[1] * lat // key_dim // 2
    kernel = functools.partial(
        attention_step, call=call, sizes=sizes, base=base, first=first, kind=kind, scale=scale, page=page, new_len=new_len
    )
    acc_spec = pl.BlockSpec((1, lat, rows), lambda r, *_: (r, 0, 0))
    mass_spec = pl.BlockSpec((1, 2, rows), lambda r, *_: (r, 0, 0))
    in_specs = [pl.BlockSpec(memory_space=pl.ANY if call == 1 else pltpu.HBM)] * len(blocks)
    in_specs += [pl.BlockSpec((groups, 1, key_dim, 128), lambda r, *_: (0, r, 0, 0))]
    if first:
        in_specs += [pl.BlockSpec((1,) + inputs[0].shape[1:], lambda r, *_: (r, 0, 0))]
    else:
        in_specs += [acc_spec, mass_spec]
    scratch = [
        pltpu.VMEM((count,) + blocks[0].shape[1:], jnp.bfloat16),
        pltpu.SemaphoreType.DMA((len(blocks),)),
        pltpu.VMEM((TILES[call] * page, rows), jnp.float32),
        pltpu.VMEM((TILES[call] * page, rows), jnp.float32),
        pltpu.VMEM((TILES[call] * page, lat + 128), jnp.bfloat16),
        pltpu.VMEM((TILES[call] * page, lat + 128), jnp.bfloat16),
        pltpu.VMEM((lat + 128, rows), jnp.bfloat16),
    ]
    if kind == "state":
        out_specs = [acc_spec, mass_spec]
        out_shape = [
            jax.ShapeDtypeStruct((req, lat, rows), jnp.float32),
            jax.ShapeDtypeStruct((req, 2, rows), jnp.float32),
        ]
    else:
        scratch.append(pltpu.VMEM((lat, rows), jnp.float32))
        out_specs = [None, pl.BlockSpec((req, 1, rows), lambda r, *_: (0, 0, 0))]
        out_shape = [None, jax.ShapeDtypeStruct((req, 1, rows), jnp.float32)]
        if kind == "partner":
            out_specs[0] = pl.BlockSpec((1, rows + 16, lat), lambda r, *_: (r, 0, 0))
            out_shape[0] = jax.ShapeDtypeStruct((req, rows + 16, lat), jnp.bfloat16)
        else:
            heads, _, head_v = w_uv.shape
            in_specs.append(pl.BlockSpec(memory_space=pltpu.HBM))
            scratch += [pltpu.VMEM((req, lat, rows), jnp.bfloat16)] * 2
            scratch += [pltpu.VMEM(w_uv.shape, jnp.bfloat16), pltpu.SemaphoreType.DMA]
            out_specs[0] = pl.BlockSpec((req, new_len, heads * head_v), lambda r, *_: (0, 0, 0))
            out_shape[0] = jax.ShapeDtypeStruct((req, new_len, heads * head_v), jnp.float32)
    more = [w_uv] if kind == "own" else []
    return pl.pallas_call(
        kernel,
        grid_spec=pltpu.PrefetchScalarGridSpec(
            num_scalar_prefetch=1,
            grid=(req,),
            in_specs=in_specs,
            out_specs=out_specs,
            scratch_shapes=scratch,
        ),
        out_shape=out_shape,
        compiler_params=pltpu.CompilerParams(
            dimension_semantics=("arbitrary",), vmem_limit_bytes=ATTEND_VMEM[call]
        ),
        cost_estimate=pl.CostEstimate(
            flops=8 * rows * count * page * (key_dim + lat),
            bytes_accessed=4 * req * lat * rows * 2 + count * page * key_dim * 2,
            transcendentals=2 * rows * count * page,
        ),
        name=f"attend_{call}_{kind}",
    )(table, *blocks, query, *inputs, *more)


def merge_step(turn_ref, got_ref, got_mass_ref, own_ref, mass_ref, wuv_ref, new_ref, out_ref, handed_ref):
    req, width, lat = got_ref.shape
    group, _, head_v = wuv_ref.shape
    new_len = width // group

    @pl.when(pl.program_id(0) == 0)
    def _():
        for i in range(req):
            handed_ref[i] = new_ref[turn_ref[i]]

    shares = []
    for r in range(req):
        tail = got_mass_ref[r].astype(jnp.float32)
        got_mass = tail[0:1] + tail[1:2] + tail[2:3]
        share = 1.0 / (1.0 + jnp.exp2(mass_ref[r] - got_mass))
        shares.append(jnp.broadcast_to(share, (width, width)).T)
    for j in range(group):
        first, last = j * new_len, (j + 1) * new_len
        rows = gather_rows([got_ref.at[r] for r in range(req)], first, last)
        got = jnp.dot(rows, wuv_ref[j], preferred_element_type=jnp.float32)
        lanes = slice(j * head_v, (j + 1) * head_v)
        for r in range(req):
            share = shares[r][first:last]
            own = own_ref[r, :, lanes]
            out_ref[r, :, lanes] = (
                own * (1.0 - share) + got[r * new_len : (r + 1) * new_len] * share
            ).astype(jnp.bfloat16)


def merge(turns, got, own, mass, w_uv, new_rows):
    req, deep, lat = got.shape
    heads, _, head_v = w_uv.shape
    groups = (deep - 16) // 128
    group = heads // groups
    new_len = 128 // group
    wide = pl.BlockSpec((req, new_len, group * head_v), lambda g, *_: (0, 0, g))
    whole = pl.BlockSpec(new_rows.shape, lambda g, *_: (0, 0, 0))
    return pl.pallas_call(
        merge_step,
        grid_spec=pltpu.PrefetchScalarGridSpec(
            num_scalar_prefetch=1,
            grid=(groups,),
            in_specs=[
                pl.BlockSpec((req, 128, lat), lambda g, *_: (0, g, 0)),
                pl.BlockSpec((req, 16, 128), lambda g, *_: (0, (deep - 16) // 16, g)),
                wide,
                pl.BlockSpec((req, 1, 128), lambda g, *_: (0, 0, g)),
                pl.BlockSpec((group, lat, head_v), lambda g, *_: (g, 0, 0)),
                whole,
            ],
            out_specs=[wide, whole],
        ),
        out_shape=[
            jax.ShapeDtypeStruct((req, new_len, heads * head_v), jnp.bfloat16),
            jax.ShapeDtypeStruct(new_rows.shape, jnp.bfloat16),
        ],
        compiler_params=pltpu.CompilerParams(
            dimension_semantics=("arbitrary",), vmem_limit_bytes=MERGE_VMEM
        ),
        name="merge",
    )(turns, got, got, own, mass, w_uv, new_rows)


def partner_pairs(pool_count, dev_count, which):
    return [
        (pool * dev_count + dev, partners(pool, dev)[which] * dev_count + dev)
        for pool in range(pool_count)
        for dev in range(dev_count)
    ]


def on_device(
    hidden,
    query_latent_rows,
    store,
    w_down,
    kv_gain,
    query_up_weight,
    w_uk,
    w_uv,
    prefix_pages,
    page_owner,
    page_slot,
    decode_order,
):
    pool_count = lax.axis_size("pool")
    dev_count = lax.axis_size("dev")
    column = lax.axis_index("dev")
    req_col, quarter, model_width = hidden.shape
    new_len = quarter * pool_count
    lat_dim = kv_gain.shape[0]
    key_dim = w_down.shape[1]
    nope_dim = w_uk.shape[1]
    rope_dim = key_dim - lat_dim
    first_row = column * req_col
    score_scale = (nope_dim + rope_dim) ** (-0.5)
    powers = np.exp(np.arange(rope_dim // 2) * (-2.0 * np.log(50000.0) / rope_dim))
    frequency = np.repeat(powers.astype(np.float32)[:, None], req_col * new_len, axis=1)

    near, far, passed, query, query_other, new_local, new_keys, table = exchange(
        prefix_pages,
        query_latent_rows.reshape(req_col * quarter, -1),
        hidden.reshape(req_col * quarter, model_width),
        kv_gain,
        page_owner.T,
        page_slot.T,
        jnp.asarray(frequency),
        store[0],
        w_down.T,
        query_up_weight,
        w_uk,
        req_col,
    )
    axes = ("pool", "dev")
    passed_far = lax.ppermute(far, axes, partner_pairs(pool_count, dev_count, 1))

    new = (new_keys,)
    common = dict(scale=score_scale, lat=lat_dim, new_len=new_len)
    early_blocks = [near, far, passed]
    state = attend(0, table, 0, early_blocks, query_other, new, "state", **common)
    part, part_mass = attend(
        1,
        table,
        dev_count + FORWARDED,
        [passed_far],
        query_other,
        state,
        "partner",
        **common,
    )
    got = lax.ppermute(part, axes, partner_pairs(pool_count, dev_count, 0))
    table, part_mass = lax.optimization_barrier((table, part_mass))
    own, own_mass = attend(
        2, table, 0, early_blocks + [passed_far], query, new, "own", w_uv=w_uv, **common
    )
    turns = lax.dynamic_slice_in_dim(decode_order, first_row, req_col) - first_row
    attended, handed = merge(
        turns, got, own, own_mass, w_uv, new_local.reshape(req_col, quarter, key_dim)
    )
    return (attended, handed)


def solution(mesh):
    in_specs = (
        P("dev", "pool", None),
        P("dev", "pool", None),
        P(("pool", "dev"), None, None, None),
        P(),
        P(),
        P(None, "pool"),
        P("pool", None, None),
        P("pool", None, None),
        P(),
        P(),
        P(),
        P(),
    )
    out_specs = (P("dev", None, "pool"), P("dev", "pool", None))
    return jax.shard_map(
        on_device, mesh=mesh, in_specs=in_specs, out_specs=out_specs, check_vma=False
    )
```

```python
import functools
import math

import jax
import jax.numpy as jnp
import numpy as np
from jax import lax
from jax.experimental import pallas as pl
from jax.experimental.pallas import tpu as pltpu
from jax.sharding import PartitionSpec as P

TILES = (8, 4, 8)
LOW = -1e30
FORWARDED = 20
EXCHANGE_VMEM = 60 * 2**20
ATTEND_VMEM = (60 * 2**20, 52 * 2**20, 52 * 2**20)
MERGE_VMEM = 24 * 2**20
MESH = pl.DeviceIdType.MESH
STEPS = [
    (0, 1), (1, 0), (0, 3), (3, 0), (1, 1), (3, 3), (1, 3), (3, 1),
    (0, 2), (2, 0), (1, 2), (2, 1), (3, 2), (2, 3), (2, 2),
]
OFFSETS = [(0, 0, 0), (0, 0, 1)] + [(z, x, c) for z, x in STEPS for c in (0, 1)]


def shifted(dev, offset, sign):
    core, x, z = dev % 2, (dev // 2) % 4, dev // 8
    dz, dx, dc = offset
    return ((z + sign * dz + 4) % 4 * 4 + (x + sign * dx + 4) % 4) * 2 + (core + dc) % 2


def partners(pool, dev):
    near = pool + 1 - 2 * (pool % 2)
    far = 3 - pool
    odd = dev % 2
    return near + odd * (far - near), far + odd * (near - far)


def list_pages(pool, dev, key_partner, owners, table_ref, n_a, quarter):
    n_pairs = len(OFFSETS)
    width = 4 * n_pairs
    entries = owners.shape[1]
    entry = lax.broadcasted_iota(jnp.int32, (1, entries), 1)
    pair = lax.broadcasted_iota(jnp.int32, (2 * n_pairs, 1), 0)
    source = jnp.zeros((2 * n_pairs, 1), jnp.int32)
    for j, offset in enumerate(OFFSETS):
        source = jnp.where(pair % n_pairs == j, shifted(dev, offset, -1), source)
    source = source + n_pairs * jnp.where(pair < n_pairs, pool, key_partner)
    hit = owners == source
    head = jnp.min(jnp.where(hit, entry, entries), axis=1, keepdims=True)
    tail = jnp.max(jnp.where(hit, entry, -1), axis=1, keepdims=True)
    nobody = entries // 64
    low = head // 64
    high = jnp.where(tail > head, tail // 64, nobody)
    request = jnp.concatenate([low, high], axis=0)
    place = lax.broadcasted_iota(jnp.int32, (width, 1), 0)
    late = place % (2 * n_pairs) >= n_pairs + n_a
    lane = lax.broadcasted_iota(jnp.int32, (1, width), 1)
    rows = []
    for wanted in (jnp.logical_not(late), late, None):
        mine = request if wanted is None else jnp.where(wanted, request, nobody)
        key = (mine * width + place).astype(jnp.float32)
        key = jnp.broadcast_to(key, (width, width))
        rank = jnp.sum((key.T < key).astype(jnp.float32), axis=1, keepdims=True).astype(jnp.int32)
        rows.append(jnp.sum(jnp.where(rank == lane, place, 0), axis=0, keepdims=True))
        rows.append(jnp.sum((mine < lane).astype(jnp.int32), axis=0, keepdims=True))
    rows.append(
        jnp.where(lane < quarter, pool * quarter + lane, key_partner * quarter + lane - quarter)
    )
    for i, row in enumerate(rows):
        table_ref[i : i + 1, :] = row


def exchange_kernel(
    prefix_ref, ql_ref, hidden_ref, gain_ref, prefix_row, owner_ref, slot_ref, frequency_ref,
    store_ref, wd_ref, qup_ref, wuk_ref,
    arr_a, arr_b, pass_a, q_own, q_other, new_own, new_keys, table_ref,
    store_v, packed, ql_in, wd_v, qup_v, wuk_v, q_s, new_s, new_in, q_full, picks_v, picks,
    load_sem, ql_send, ql_recv, page_send, page_recv, pass_send, pass_recv, pair_send, pair_recv,
):
    pool, dev = lax.axis_index("pool"), lax.axis_index("dev")
    head_partner, key_partner = partners(pool, dev)
    req, key_dim, own_rows = q_s.shape
    heads, nope, lat = wuk_v.shape
    rope = key_dim - lat
    half_rope = rope // 2
    quarter = ql_in.shape[1] // req
    new_len = 4 * quarter
    page = store_v.shape[1]
    n_send = len(OFFSETS)
    n_a = arr_a.shape[0]

    load_store = pltpu.make_async_copy(store_ref, store_v, load_sem.at[6])
    load_store.start()
    loads = [
        pltpu.make_async_copy(wd_ref, wd_v, load_sem.at[0]),
        pltpu.make_async_copy(qup_ref, qup_v, load_sem.at[1]),
        pltpu.make_async_copy(wuk_ref, wuk_v, load_sem.at[2]),
    ]
    for copy in loads:
        copy.start()

    barrier = pltpu.get_barrier_semaphore()
    for offset in OFFSETS[1:]:
        pl.semaphore_signal(
            barrier, inc=1, device_id=(pool, shifted(dev, offset, 1)), device_id_type=MESH
        )
    for step in range(1, 4):
        pl.semaphore_signal(
            barrier, inc=1, device_id=((pool + step) % 4, dev), device_id_type=MESH
        )

    prefix = prefix_row[...][None, :]
    owners = owner_ref[...]
    page_of = lax.broadcasted_iota(jnp.int32, owners.shape, 0)
    lane_of = lax.broadcasted_iota(jnp.int32, owners.shape, 1)
    n_slots, max_pages = store_v.shape[0], owners.shape[0]
    used = page_of < prefix
    mine = used & (owners == pool * n_send + dev)
    code = (lane_of % req * max_pages + page_of) * n_slots + slot_ref[...]
    low = jnp.min(jnp.where(mine, code, req * max_pages * n_slots), axis=0, keepdims=True)
    high = jnp.max(jnp.where(mine, code, 0), axis=0, keepdims=True)
    n_lanes = owners.shape[1]
    for step in (1, 2):
        low = jnp.minimum(low, pltpu.roll(low, n_lanes - step, 1))
        high = jnp.maximum(high, pltpu.roll(high, n_lanes - step, 1))
    picks_v[0:1, :] = low % n_slots
    picks_v[1:2, :] = high % n_slots
    load_picks = pltpu.make_async_copy(picks_v, picks, load_sem.at[7])
    load_picks.start()

    def pack(j):
        target = shifted(dev, OFFSETS[j], 1)
        pages = [store_v[picks[k, req * target]] for k in range(2)]
        for k in range(2):
            packed[j, k * page : (k + 1) * page, :] = pages[k][:, :lat]
        keys = jnp.concatenate([p[:, lat:] for p in pages], axis=1)
        step = page * 2 * rope // lat
        packed[j, 2 * page :, :] = jnp.concatenate(
            [keys[i * step : (i + 1) * step] for i in range(page // step)], axis=1
        )

    load_picks.wait()
    load_store.wait()
    for j in (0, 1):
        pack(j)
    pl.semaphore_wait(barrier, n_send - 1 + 3)

    def remote(src, dst, send, recv, target):
        return pltpu.make_async_remote_copy(
            src_ref=src, dst_ref=dst, send_sem=send, recv_sem=recv, device_id=target, device_id_type=MESH
        )

    ql_sends = [
        remote(ql_ref, ql_in.at[pool], ql_send.at[s - 1], ql_recv.at[s - 1], ((pool + s) % 4, dev))
        for s in range(1, 4)
    ]
    ql_gets = [
        remote(
            ql_ref, ql_in.at[(pool + 4 - s) % 4], ql_send.at[s - 1], ql_recv.at[s - 1], (head_partner, dev)
        )
        for s in range(1, 4)
    ]
    for copy in ql_sends:
        copy.start()

    def landing(j):
        return arr_a.at[j] if j < n_a else arr_b.at[j - n_a]

    passes = [
        remote(
            packed.at[0] if j == 0 else arr_a.at[j],
            pass_a.at[j],
            pass_send.at[j],
            pass_recv.at[j],
            (key_partner, dev),
        )
        for j in range(n_a)
    ]
    sends = [None] * n_send
    for j in range(1, n_send):
        if j > 1:
            pack(j)
        copy = remote(
            packed.at[j],
            landing(j),
            page_send.at[j],
            page_recv.at[j],
            (pool, shifted(dev, OFFSETS[j], 1)),
        )
        copy.start()
        sends[j] = copy
        if j == 1:
            passes[0].start()
    own_pages = pltpu.make_async_copy(packed.at[0], arr_a.at[0], load_sem.at[3])
    own_pages.start()

    def pass_on(first, last):
        for j in range(first, last):
            sends[j].wait_recv()
            if j < n_a:
                passes[j].start()

    pass_on(1, 2)
    frequency = frequency_ref[...]
    lane = lax.broadcasted_iota(jnp.int32, (1, frequency.shape[1]), 1)
    position = pool * quarter + lane % quarter
    local_position = position
    position = lane % new_len
    for r in range(req):
        begin = prefix_ref[req * dev + r] * page
        local_position = local_position + jnp.where(lane // quarter == r, begin, 0)
        position = position + jnp.where(lane // new_len == r, begin, 0)
    local_angles = (frequency * local_position.astype(jnp.float32))[:, : req * quarter]
    angles = frequency * position.astype(jnp.float32)

    loads[0].wait()
    projected = lax.dot_general(
        wd_v[...], hidden_ref[...], (((1,), (1,)), ((), ())), preferred_element_type=jnp.float32
    )
    latent = projected[:lat]
    latent = latent * lax.rsqrt(jnp.mean(latent * latent, axis=0, keepdims=True) + 1e-06)
    first, second = projected[lat : lat + half_rope], projected[lat + half_rope :]
    lcos, lsin = jnp.cos(local_angles), jnp.sin(local_angles)
    rotated = jnp.concatenate([first * lcos - second * lsin, first * lsin + second * lcos], axis=0)
    new_s[...] = jnp.concatenate(
        [latent.T * gain_ref[...].astype(jnp.float32)[None, :], rotated.T], axis=1
    ).astype(jnp.bfloat16)
    new_send = remote(new_s, new_in, pair_send.at[0], pair_recv.at[0], (key_partner, dev))
    new_send.start()
    new_keep = pltpu.make_async_copy(new_s, new_own, load_sem.at[4])
    new_keep.start()
    pass_on(2, 4)
    own = jnp.where(used, owners, -1).astype(jnp.float32)
    own = pltpu.roll(own, (n_lanes - req * dev) % n_lanes, 1)
    own = jnp.concatenate([own, jnp.zeros((n_lanes - max_pages, n_lanes), jnp.float32)], axis=0).T
    own = jnp.concatenate([own[r : r + 1, :max_pages] for r in range(req)], axis=1)
    list_pages(pool, dev, key_partner, own.astype(jnp.int32), table_ref, n_a, quarter)

    ql_in[pool] = ql_ref[...]
    for copy in ql_gets:
        copy.wait_recv()
    for y in range(4):
        rows = ql_in[y].astype(jnp.float32)
        for r in range(req):
            q_full[pl.ds(r * new_len + y * quarter, quarter), :] = rows[
                r * quarter : (r + 1) * quarter
            ]
    for copy in loads[1:]:
        copy.wait()
    group = 128 // new_len
    width = nope + rope

    cos, sin = jnp.cos(angles), jnp.sin(angles)

    def project(g):
        raw = jnp.dot(
            q_full[...].astype(jnp.bfloat16),
            qup_v[:, g * group * width : (g + 1) * group * width],
            preferred_element_type=jnp.float32,
        ).T
        built = []
        for j in range(group):
            at = j * width
            q_nope = raw[at : at + nope].astype(jnp.bfloat16)
            q_abs = lax.dot_general(
                wuk_v[g * group + j],
                q_nope,
                (((0,), (0,)), ((), ())),
                preferred_element_type=jnp.float32,
            )
            x = raw[at + nope : at + nope + half_rope]
            y = raw[at + nope + half_rope : at + width]
            built.append(
                jnp.concatenate([q_abs, x * cos - y * sin, x * sin + y * cos], axis=0).astype(
                    jnp.bfloat16
                )
            )
        for r in range(req):
            q_s[r, :, g * 128 : (g + 1) * 128] = jnp.concatenate(
                [b[:, r * new_len : (r + 1) * new_len] for b in built], axis=1
            )

    done = 4
    for g in range(heads // group):
        project(g)
        if g < heads // group - 1:
            pass_on(done, done + 2)
            done += 2

    q_send = remote(q_s, q_other, pair_send.at[1], pair_recv.at[1], (head_partner, dev))
    q_send.start()
    q_keep = pltpu.make_async_copy(q_s, q_own, load_sem.at[5])
    q_keep.start()

    pass_on(done, n_send)
    for copy in ql_sends:
        copy.wait_send()
    for copy in sends[1:]:
        copy.wait_send()
    own_pages.wait()
    new_keep.wait()
    q_keep.wait()
    new_send.wait()
    own_new, got_new = new_s[...].astype(jnp.float32), new_in[...].astype(jnp.float32)
    for r in range(req):
        rows = slice(r * quarter, (r + 1) * quarter)
        new_keys[r] = jnp.concatenate([own_new[rows], got_new[rows]], axis=0).astype(jnp.bfloat16)
    q_send.wait()
    for copy in passes:
        copy.wait()


def exchange(prefix, ql, hidden, gain, owner_t, slot_t, frequency, store, wd, qup, wuk, req):
    n_cols = prefix.shape[0] // req
    n_slots, page, key_dim = store.shape
    heads, nope, lat = wuk.shape
    tokens = ql.shape[0]
    new_len = 4 * tokens // req
    bf16 = jnp.bfloat16
    any_spec = pl.BlockSpec(memory_space=pl.ANY)
    vmem = pl.BlockSpec(memory_space=pltpu.VMEM)
    own_rows = heads * new_len
    pair = (2 * page * key_dim // lat, lat)
    query = jax.ShapeDtypeStruct((req, key_dim, own_rows), bf16)
    new = jax.ShapeDtypeStruct((tokens, key_dim), bf16)
    near = jax.ShapeDtypeStruct((FORWARDED,) + pair, bf16)
    far = jax.ShapeDtypeStruct((n_cols - FORWARDED,) + pair, bf16)
    dma = pltpu.SemaphoreType.DMA
    return pl.pallas_call(
        exchange_kernel,
        in_specs=[pl.BlockSpec(memory_space=pltpu.SMEM)] + [vmem] * 7 + [any_spec] * 4,
        out_specs=[any_spec] * 6 + [vmem] * 2,
        out_shape=[
            near,
            far,
            near,
            query,
            query,
            new,
            jax.ShapeDtypeStruct((req, 2 * tokens // req, key_dim), bf16),
            jax.ShapeDtypeStruct((8, 4 * n_cols), jnp.int32),
        ],
        scratch_shapes=[
            pltpu.VMEM(store.shape, bf16),
            pltpu.VMEM((n_cols,) + pair, bf16),
            pltpu.VMEM((4,) + ql.shape, bf16),
            pltpu.VMEM(wd.shape, bf16),
            pltpu.VMEM(qup.shape, bf16),
            pltpu.VMEM(wuk.shape, bf16),
            pltpu.VMEM(query.shape, bf16),
            pltpu.VMEM(new.shape, bf16),
            pltpu.VMEM(new.shape, bf16),
            pltpu.VMEM((req * new_len, ql.shape[1]), jnp.float32),
            pltpu.VMEM((2, prefix.shape[0]), jnp.int32),
            pltpu.SMEM((2, prefix.shape[0]), jnp.int32),
            dma((8,)),
            dma((3,)),
            dma((3,)),
            dma((n_cols,)),
            dma((n_cols,)),
            dma((FORWARDED,)),
            dma((FORWARDED,)),
            dma((2,)),
            dma((2,)),
        ],
        compiler_params=pltpu.CompilerParams(
            collective_id=1, has_side_effects=True, vmem_limit_bytes=EXCHANGE_VMEM
        ),
        cost_estimate=pl.CostEstimate(flops=10**10, bytes_accessed=10**8, transcendentals=0),
        name="exchange",
    )(prefix, ql, hidden, gain, prefix, owner_t, slot_t, frequency, store, wd, qup, wuk)


def gather_rows(parts, first, last):
    return jnp.concatenate([part[first:last] for part in parts], axis=0)


def attention_step(table_ref, *refs, call, sizes, base, first, kind, scale, page, new_len):
    n_blocks = len(sizes)
    blocks, refs = refs[:n_blocks], refs[n_blocks:]
    q_ref, refs = refs[0], refs[1:]
    given, refs = refs[0], refs[1:]
    if kind == "own":
        wuv_hbm, refs = refs[0], refs[1:]
    result, refs = refs[0], refs[1:]
    if kind != "state":
        mass, refs = refs[0], refs[1:]
    pairs, sem, even, odd, even_keys, odd_keys, query = refs[:7]
    acc = result.at[0, pl.ds(0, result.shape[1] - 8)] if kind == "state" else refs[7]
    lat, rows = acc.shape
    request = pl.program_id(0)

    copies, at = [], 0
    for i, block in enumerate(blocks):
        copies.append(pltpu.make_async_copy(block, pairs.at[pl.ds(at, sizes[i])], sem.at[i]))
        at += sizes[i]
    if kind == "own":
        wuv_ref = refs[10]
        load_wuv = pltpu.make_async_copy(wuv_hbm, wuv_ref, refs[11])

    @pl.when(request == 0)
    def _():
        for copy in copies:
            copy.start()
        if kind == "own":
            load_wuv.start()

    tile_slots = TILES[call]
    factor = scale * math.log2(math.e)
    rope = q_ref.shape[1] - lat
    pad = 128 - rope
    bias_rows = jnp.where(
        lax.broadcasted_iota(jnp.int32, (pad, rows), 0) == 0, 1.0, 0.0
    ).astype(jnp.bfloat16)
    key_lane = lax.broadcasted_iota(jnp.int32, (page, pad), 1)

    query[: lat + rope, :] = q_ref[0]
    query[lat + rope :, :] = bias_rows

    def weigh(keys, weights):
        return lax.dot_general(
            keys, weights, (((0,), (0,)), ((), ())), preferred_element_type=jnp.float32
        )

    if first:
        new_keys = given[0]
        quarter = new_keys.shape[0] // 2
        row = lax.broadcasted_iota(jnp.int32, (2 * quarter, 1), 0)
        new_pos = jnp.where(row < quarter, table_ref[6, 0] + row, table_ref[6, quarter] + row - quarter)
        score = jnp.dot(new_keys, q_ref[0], preferred_element_type=jnp.float32)
        token = lax.broadcasted_iota(jnp.int32, score.shape, 1) % new_len
        live = new_pos <= token
        score = jnp.where(live, score, LOW)
        top = jnp.max(score, axis=0, keepdims=True)
        weights = jnp.where(live, jnp.exp2((score - top) * factor), 0.0)
        total = jnp.sum(weights, axis=0, keepdims=True)
        acc[...] = weigh(new_keys[:, :lat], weights.astype(jnp.bfloat16))
    else:
        top, total = given[0, lat : lat + 1, :], given[0, lat + 1 : lat + 2, :]
        acc[...] = given[0, :lat, :]

    @pl.when(request == 0)
    def _():
        for copy in copies:
            copy.wait()

    begin = table_ref[2 * call + 1, request]
    end = table_ref[2 * call + 1, request + 1]
    tiles = (end - begin + tile_slots - 1) // tile_slots

    def fetch(tile, keys, sheet):
        for g in range(tile_slots):
            spot = begin + tile * tile_slots + g
            index = table_ref[2 * call, jnp.maximum(jnp.minimum(spot, end - 1), 0)]
            half = table_ref.shape[1] // 2
            pair, turn = index % half - base, index // half
            rows = slice(g * page, (g + 1) * page)
            keys[rows, :lat] = pairs[pair, pl.ds(pl.multiple_of(turn * page, page), page), :]
            both = pairs[pair, pl.ds(2 * page, 2 * page * rope // lat), :]
            both = jnp.concatenate([both[:, i * 128 : (i + 1) * 128] for i in range(lat // 128)], axis=0)
            rotary = jnp.where(turn == 0, both[:, :rope], both[:, rope:])
            bias = jnp.where((key_lane == 0) & (spot >= end), LOW, 0.0).astype(jnp.bfloat16)
            keys[rows, lat:] = jnp.concatenate([rotary, bias], axis=1)
        sheet[...] = jnp.dot(keys[...], query[...], preferred_element_type=jnp.float32)

    def take(sheet, keys, top, total):
        score = sheet[...]
        new_top = jnp.maximum(top, jnp.max(score, axis=0, keepdims=True))
        shrink = jnp.exp2((top - new_top) * factor)
        weights = jnp.exp2((score - new_top) * factor)
        total = total * shrink + jnp.sum(weights, axis=0, keepdims=True)
        acc[...] = acc[...] * shrink + weigh(keys[:, :lat], weights.astype(jnp.bfloat16))
        return new_top, total

    @pl.when(tiles > 0)
    def _():
        fetch(0, even_keys, even)

    def body(step, carry):
        tile = 2 * step
        fetch(tile + 1, odd_keys, odd)
        carry = take(even, even_keys, *carry)
        fetch(jnp.minimum(tile + 2, tiles - 1), even_keys, even)
        return take(odd, odd_keys, *carry)

    carry = lax.fori_loop(0, tiles // 2, body, (top, total))
    top, total = lax.cond(
        tiles % 2 == 1,
        lambda c: take(even, even_keys, *c),
        lambda c: c,
        carry,
    )

    if kind == "state":
        result[0, lat : lat + 1, :] = top
        result[0, lat + 1 : lat + 2, :] = total
        return
    live = total > 0
    inverse = jnp.where(live, 1.0 / total, 0.0)
    log_mass = jnp.where(live, top * factor + jnp.log(total) * math.log2(math.e), LOW)
    mass[request] = log_mass
    mixed = (acc[...] * inverse).T
    high = mixed.astype(jnp.bfloat16)
    if kind == "partner":
        result[0, :rows, :] = high
        terms, rest = [], log_mass
        for _ in range(3):
            terms.append(rest.astype(jnp.bfloat16).astype(jnp.float32))
            rest = rest - terms[-1]
        row = lax.broadcasted_iota(jnp.int32, (16, rows), 0)
        tail = jnp.where(row == 2, terms[2], 0.0)
        tail = jnp.where(row == 0, terms[0], jnp.where(row == 1, terms[1], tail))
        result[0, rows:, :] = tail.astype(jnp.bfloat16)
    else:
        high_v, low_v = refs[8], refs[9]
        high_v[request] = high
        low_v[request] = (mixed - high.astype(jnp.float32)).astype(jnp.bfloat16)

    if kind == "own":

        @pl.when(request == pl.num_programs(0) - 1)
        def _():
            load_wuv.wait()
            req = high_v.shape[0]
            head_v = wuv_ref.shape[2]
            for head in range(wuv_ref.shape[0]):
                first_row, last_row = head * new_len, (head + 1) * new_len
                total = None
                for part in (high_v, low_v):
                    rows_of = gather_rows([part.at[r] for r in range(req)], first_row, last_row)
                    term = jnp.dot(rows_of, wuv_ref[head], preferred_element_type=jnp.float32)
                    total = term if total is None else total + term
                for r in range(req):
                    result[r, :, head * head_v : (head + 1) * head_v] = total[
                        r * new_len : (r + 1) * new_len
                    ]


def attend(call, table, base, blocks, query, inputs, kind, scale, lat, new_len, w_uv=None):
    first = inputs[0].dtype == jnp.bfloat16
    req, key_dim, rows = query.shape
    sizes = [b.shape[0] for b in blocks]
    count = sum(sizes)
    page = blocks[0].shape[1] * lat // key_dim // 2
    kernel = functools.partial(
        attention_step, call=call, sizes=sizes, base=base, first=first, kind=kind, scale=scale, page=page, new_len=new_len
    )
    acc_spec = pl.BlockSpec((1, lat + 8, rows), lambda r, *_: (r, 0, 0))
    in_specs = [pl.BlockSpec(memory_space=pl.ANY if call == 1 else pltpu.HBM)] * len(blocks)
    in_specs += [pl.BlockSpec((1, key_dim, rows), lambda r, *_: (r, 0, 0))]
    if first:
        in_specs += [pl.BlockSpec((1,) + inputs[0].shape[1:], lambda r, *_: (r, 0, 0))]
    else:
        in_specs += [acc_spec]
    scratch = [
        pltpu.VMEM((count,) + blocks[0].shape[1:], jnp.bfloat16),
        pltpu.SemaphoreType.DMA((len(blocks),)),
        pltpu.VMEM((TILES[call] * page, rows), jnp.float32),
        pltpu.VMEM((TILES[call] * page, rows), jnp.float32),
        pltpu.VMEM((TILES[call] * page, lat + 128), jnp.bfloat16),
        pltpu.VMEM((TILES[call] * page, lat + 128), jnp.bfloat16),
        pltpu.VMEM((lat + 128, rows), jnp.bfloat16),
    ]
    if kind == "state":
        out_specs = [acc_spec]
        out_shape = [jax.ShapeDtypeStruct((req, lat + 8, rows), jnp.float32)]
    else:
        scratch.append(pltpu.VMEM((lat, rows), jnp.float32))
        out_specs = [None, pl.BlockSpec((req, 1, rows), lambda r, *_: (0, 0, 0))]
        out_shape = [None, jax.ShapeDtypeStruct((req, 1, rows), jnp.float32)]
        if kind == "partner":
            out_specs[0] = pl.BlockSpec((1, rows + 16, lat), lambda r, *_: (r, 0, 0))
            out_shape[0] = jax.ShapeDtypeStruct((req, rows + 16, lat), jnp.bfloat16)
        else:
            heads, _, head_v = w_uv.shape
            in_specs.append(pl.BlockSpec(memory_space=pltpu.HBM))
            scratch += [pltpu.VMEM((req, lat, rows), jnp.bfloat16)] * 2
            scratch += [pltpu.VMEM(w_uv.shape, jnp.bfloat16), pltpu.SemaphoreType.DMA]
            out_specs[0] = pl.BlockSpec((req, new_len, heads * head_v), lambda r, *_: (0, 0, 0))
            out_shape[0] = jax.ShapeDtypeStruct((req, new_len, heads * head_v), jnp.float32)
    more = [w_uv] if kind == "own" else []
    return pl.pallas_call(
        kernel,
        grid_spec=pltpu.PrefetchScalarGridSpec(
            num_scalar_prefetch=1,
            grid=(req,),
            in_specs=in_specs,
            out_specs=out_specs,
            scratch_shapes=scratch,
        ),
        out_shape=out_shape,
        compiler_params=pltpu.CompilerParams(
            dimension_semantics=("arbitrary",), vmem_limit_bytes=ATTEND_VMEM[call]
        ),
        cost_estimate=pl.CostEstimate(
            flops=8 * rows * count * page * (key_dim + lat),
            bytes_accessed=4 * req * lat * rows * 2 + count * page * key_dim * 2,
            transcendentals=2 * rows * count * page,
        ),
        name=f"attend_{call}_{kind}",
    )(table, *blocks, query, *inputs, *more)


def merge_step(turn_ref, got_ref, got_mass_ref, own_ref, mass_ref, wuv_ref, new_ref, out_ref, handed_ref):
    req, width, lat = got_ref.shape
    group, _, head_v = wuv_ref.shape
    new_len = width // group

    @pl.when(pl.program_id(0) == 0)
    def _():
        for i in range(req):
            at = lax.axis_index("dev") * req
            handed_ref[i] = new_ref[turn_ref[at + i] - at]

    shares = []
    for r in range(req):
        tail = got_mass_ref[r].astype(jnp.float32)
        got_mass = tail[0:1] + tail[1:2] + tail[2:3]
        share = 1.0 / (1.0 + jnp.exp2(mass_ref[r] - got_mass))
        shares.append(jnp.broadcast_to(share, (width, width)).T)
    for j in range(group):
        first, last = j * new_len, (j + 1) * new_len
        rows = gather_rows([got_ref.at[r] for r in range(req)], first, last)
        got = jnp.dot(rows, wuv_ref[j], preferred_element_type=jnp.float32)
        lanes = slice(j * head_v, (j + 1) * head_v)
        for r in range(req):
            share = shares[r][first:last]
            own = own_ref[r, :, lanes]
            out_ref[r, :, lanes] = (
                own * (1.0 - share) + got[r * new_len : (r + 1) * new_len] * share
            ).astype(jnp.bfloat16)


def merge(turns, got, own, mass, w_uv, new_rows):
    req, deep, lat = got.shape
    heads, _, head_v = w_uv.shape
    groups = (deep - 16) // 128
    group = heads // groups
    new_len = 128 // group
    wide = pl.BlockSpec((req, new_len, group * head_v), lambda g, *_: (0, 0, g))
    whole = pl.BlockSpec(new_rows.shape, lambda g, *_: (0, 0, 0))
    return pl.pallas_call(
        merge_step,
        grid_spec=pltpu.PrefetchScalarGridSpec(
            num_scalar_prefetch=1,
            grid=(groups,),
            in_specs=[
                pl.BlockSpec((req, 128, lat), lambda g, *_: (0, g, 0)),
                pl.BlockSpec((req, 16, 128), lambda g, *_: (0, (deep - 16) // 16, g)),
                wide,
                pl.BlockSpec((req, 1, 128), lambda g, *_: (0, 0, g)),
                pl.BlockSpec((group, lat, head_v), lambda g, *_: (g, 0, 0)),
                whole,
            ],
            out_specs=[wide, whole],
        ),
        out_shape=[
            jax.ShapeDtypeStruct((req, new_len, heads * head_v), jnp.bfloat16),
            jax.ShapeDtypeStruct(new_rows.shape, jnp.bfloat16),
        ],
        compiler_params=pltpu.CompilerParams(
            dimension_semantics=("arbitrary",), vmem_limit_bytes=MERGE_VMEM
        ),
        name="merge",
    )(turns, got, got, own, mass, w_uv, new_rows)


def partner_pairs(pool_count, dev_count, which):
    return [
        (pool * dev_count + dev, partners(pool, dev)[which] * dev_count + dev)
        for pool in range(pool_count)
        for dev in range(dev_count)
    ]


def on_device(
    hidden,
    query_latent_rows,
    store,
    w_down,
    kv_gain,
    query_up_weight,
    w_uk,
    w_uv,
    prefix_pages,
    page_owner,
    page_slot,
    decode_order,
):
    pool_count = lax.axis_size("pool")
    dev_count = lax.axis_size("dev")
    req_col, quarter, model_width = hidden.shape
    new_len = quarter * pool_count
    lat_dim = kv_gain.shape[0]
    key_dim = w_down.shape[1]
    nope_dim = w_uk.shape[1]
    rope_dim = key_dim - lat_dim
    score_scale = (nope_dim + rope_dim) ** (-0.5)
    powers = np.exp(np.arange(rope_dim // 2) * (-2.0 * np.log(50000.0) / rope_dim))
    frequency = np.repeat(powers.astype(np.float32)[:, None], req_col * new_len, axis=1)

    near, far, passed, query, query_other, new_local, new_keys, table = exchange(
        prefix_pages,
        query_latent_rows.reshape(req_col * quarter, -1),
        hidden.reshape(req_col * quarter, model_width),
        kv_gain,
        page_owner.T,
        page_slot.T,
        jnp.asarray(frequency),
        store[0],
        w_down.T,
        query_up_weight,
        w_uk,
        req_col,
    )
    axes = ("pool", "dev")
    passed_far = lax.ppermute(far, axes, partner_pairs(pool_count, dev_count, 1))

    new = (new_keys,)
    common = dict(scale=score_scale, lat=lat_dim, new_len=new_len)
    early_blocks = [near, far, passed]
    state = attend(0, table, 0, early_blocks, query_other, new, "state", **common)
    part, part_mass = attend(
        1,
        table,
        dev_count + FORWARDED,
        [passed_far],
        query_other,
        state,
        "partner",
        **common,
    )
    got = lax.ppermute(part, axes, partner_pairs(pool_count, dev_count, 0))
    table, part_mass = lax.optimization_barrier((table, part_mass))
    own, own_mass = attend(
        2, table, 0, early_blocks + [passed_far], query, new, "own", w_uv=w_uv, **common
    )
    attended, handed = merge(
        decode_order, got, own, own_mass, w_uv, new_local.reshape(req_col, quarter, key_dim)
    )
    return (attended, handed)


def solution(mesh):
    in_specs = (
        P("dev", "pool", None),
        P("dev", "pool", None),
        P(("pool", "dev"), None, None, None),
        P(),
        P(),
        P(None, "pool"),
        P("pool", None, None),
        P("pool", None, None),
        P(),
        P(),
        P(),
        P(),
    )
    out_specs = (P("dev", None, "pool"), P("dev", "pool", None))
    return jax.shard_map(
        on_device, mesh=mesh, in_specs=in_specs, out_specs=out_specs, check_vma=False
    )
```
